32 devices in a mesh: grp: 2 (over y), col: 16 (over z, x, core).
Axes of the slice: x: 2, y: 2, z: 4, core: 2. Of those that a mesh axis runs over, the one named last changes fastest.
Arguments:
- tokens: bfloat16 [256, 14336], P(('grp', 'col')), parts along dimension 0, may hold values from -6 to 6
- slab_lengths: int32 [32], P('grp'), parts along dimension 0, may hold values from 1 to 8, 96 in all
- tile_owner: int32 [136], replicated, may hold values from 0 to 15, as said below
Outputs:
- factor_tiles: float32 [352, 896, 896], P(('grp', 'col')), parts along dimension 0
The draws below stay inside these ranges and needn't reach their ends.
There are 2 independent parts, one for each index of `grp`. The reference program is written for one: setup_inputs(seed, part) draws one part's arguments, and reference() takes and returns one part's arrays. A program takes and returns all parts, laid end to end along the dimension named above; an argument that names none is the same for every part. Nothing has to cross between parts.
Inputs may be any that keep to these rules, and one draw needn't show every extreme that they name: tile_owner[t] is one of the two blocks i, j of tile t, and the other block lies at most 10 indices before the owner, counted cyclically over 16; no device owns more than 11 tiles and some device owns exactly 11.
All inputs are finite; a program needn't handle non-finite values.
Results may differ from the reference program's by a relative error of at most 0.0003.
Values may be sent and summed in bfloat16 or wider, within the bound.
No kernel may reach another device: no remote copies, remote signals or barrier semaphores. Data moves between devices by JAX's collectives and lax.ppermute only.
A program may use at most 128 MiB of HBM per device.

```python
import math
import jax
import jax.numpy as jnp
import numpy as np
from jax import lax

UNITS = 14336
TOK_DEV = 8
TOKENS = 128
BLOCK = 896
REACH = 10
SLOTS = 11
TILES = 136
VALID = 96
N_COL = 16


def draw_tile_owner(key, part):
    key = jax.random.fold_in(key, 7)
    first_np, second_np = np.triu_indices(N_COL)
    first_block = jnp.asarray(first_np, jnp.int32)
    second_block = jnp.asarray(second_np, jnp.int32)
    ahead = (second_block - first_block) % N_COL
    first_allowed = (N_COL - ahead) % N_COL <= REACH
    second_allowed = ahead <= REACH
    key_pref, key_coin, key_favored = jax.random.split(key, 3)
    preference = jax.random.randint(key_pref, (N_COL,), 0, 4)
    coin_flip = jax.random.randint(key_coin, first_block.shape, 0, 2)
    favored = jax.random.randint(key_favored, (), 0, N_COL)
    pref_first = preference[first_block]
    pref_second = preference[second_block]
    pick_first = (pref_first > pref_second) | (pref_first == pref_second) & (coin_flip == 0)
    pick_first = jnp.where(first_block == favored, True, jnp.where(second_block == favored, False, pick_first))
    pick_first = jnp.where(first_allowed & ~second_allowed, True, jnp.where(second_allowed & ~first_allowed, False, pick_first))
    return jnp.where(pick_first, first_block, second_block).astype(jnp.int32)


def level_of(own_key, extent, cuts, least, largest):
    def one(dim, parts):
        draws = jax.random.uniform(jax.random.fold_in(jax.random.fold_in(own_key, 6), dim), (parts,), jnp.float32, least / len(cuts), largest / len(cuts))
        return jnp.repeat(jnp.exp(draws), extent[dim] // parts).reshape((-1,) + (1,) * (len(extent) - dim - 1))

    loudness = one(*cuts[0])
    for cut in cuts[1:]:
        loudness = loudness * one(*cut)
    return loudness


def length_profile(number_of, total, most, lean):
    portions = [(1 << 20) // math.isqrt(rank ** lean) + 1 for rank in range(2, number_of + 1)]
    surplus, given = total - most - (number_of - 1), [1] * (number_of - 1)
    while surplus > 0:
        candidates = [i for i in range(number_of - 1) if given[i] < most]
        pool, budget = sum([portions[i] for i in candidates]), surplus
        for i in candidates:
            more = min(most - given[i], max(1, budget * portions[i] // pool), surplus)
            given[i] = given[i] + more
            surplus = surplus - more
    return np.array([most] + given)


def ragged_sizes(stream_key, number_of, total, bound, skew):
    if number_of == 2:
        one = jax.random.randint(stream_key, (), max(1, total - bound), min(bound, total - 1) + 1)
        return jnp.stack([one, total - one])
    lengths = jnp.asarray(length_profile(number_of, total, bound, skew), jnp.int32)
    pairs = (number_of - 1) // 2
    source_of, receiver = lengths[1:1 + 2 * pairs:2], lengths[2:2 + 2 * pairs:2]
    slack = jnp.minimum(source_of - 1, bound - receiver)
    passed = jax.random.randint(jax.random.fold_in(stream_key, 1), (pairs,), 0, 1 << 20) % (slack + 1)
    lengths = lengths.at[1:1 + 2 * pairs:2].set(source_of - passed).at[2:2 + 2 * pairs:2].set(receiver + passed)
    return lengths[jax.random.permutation(jax.random.fold_in(stream_key, 2), number_of)]


def bell_draw(own_key, shape, spread, most, cuts=(), kind=jnp.bfloat16):
    level = level_of(own_key, shape, cuts, -0.22, 0.18) if cuts else 1.0
    result = jax.random.normal(own_key, shape, jnp.float32) * spread * level
    return jnp.minimum(jnp.maximum(result, -most), most).astype(kind)


def setup_inputs(seed: int = 0, part: int = 0) -> dict:
    splits = jax.random.split(jax.random.key(seed), 4)
    own_keys = jax.random.split(jax.random.fold_in(splits[3], part), 4)
    return {
        "tokens": bell_draw(own_keys[0], (TOKENS, UNITS), 1.0, 6.0, ((0, 16),)),
        "slab_lengths": ragged_sizes(own_keys[1], N_COL, VALID, TOK_DEV, 2).astype(jnp.int32),
        "tile_owner": draw_tile_owner(jax.random.fold_in(splits[3], 71), part),
    }


def reference(tokens, slab_lengths, tile_owner):
    row_index = jnp.arange(TOKENS, dtype=jnp.int32)
    valid_rows = (row_index % TOK_DEV) < slab_lengths[row_index // TOK_DEV]
    masked = jnp.where(valid_rows[:, None], tokens, jnp.zeros_like(tokens))
    valid_count = jnp.sum(slab_lengths).astype(jnp.float32)
    first_np, second_np = np.triu_indices(N_COL)
    first_block = jnp.asarray(first_np, jnp.int32)
    second_block = jnp.asarray(second_np, jnp.int32)
    owner_onehot = (tile_owner[:, None] == jnp.arange(N_COL, dtype=jnp.int32)[None, :]).astype(jnp.int32)
    ranks = jnp.cumsum(owner_onehot, axis=0) - 1
    slot_of_tile = jnp.sum(ranks * owner_onehot, axis=1).astype(jnp.int32)
    position = (tile_owner * SLOTS + slot_of_tile).astype(jnp.int32)
    tile_at = jnp.full((N_COL * SLOTS,), -1, jnp.int32).at[position].set(jnp.arange(TILES, dtype=jnp.int32))

    def one_slot(tile_number):
        safe_number = jnp.maximum(tile_number, 0)
        left_cols = lax.dynamic_slice_in_dim(masked, (first_block[safe_number] * BLOCK).astype(jnp.int32), BLOCK, 1)
        right_cols = lax.dynamic_slice_in_dim(masked, (second_block[safe_number] * BLOCK).astype(jnp.int32), BLOCK, 1)
        product = jnp.dot(left_cols.T, right_cols, preferred_element_type=jnp.float32) / valid_count
        return jnp.where(tile_number >= 0, product, jnp.zeros_like(product))

    return lax.map(one_slot, tile_at)
```

```python
import functools

import jax
import jax.numpy as jnp
from jax import lax
from jax.experimental import pallas as pl
from jax.experimental.pallas import tpu as pltpu
from jax.sharding import PartitionSpec as P

BUFFERS = 4


def tile_kernel(
    devices, reach, slots, aligned, owner_ref, device_ref, scale_ref, x_ref, mask_ref,
    out_ref, blocks, mask, tiles, zeros, in_sems, mask_sem, out_sems, zero_sems,
):
    device = device_ref[0]
    width = blocks.shape[2]

    def owned(partner):
        low = jnp.minimum(device, partner)
        high = jnp.maximum(device, partner)
        index = low * devices - low * (low - 1) // 2 + (high - low)
        return owner_ref[index] == device

    def fetch(partner):
        if aligned:
            source = x_ref.at[:, pl.ds(pl.multiple_of(partner * width, 128), width)]
        else:
            source = x_ref.at[partner]
        return pltpu.make_async_copy(source, blocks.at[partner], in_sems.at[partner])

    def put(buffer, slot):
        return pltpu.make_async_copy(tiles.at[buffer], out_ref.at[slot], out_sems.at[buffer])

    def clear(slot):
        return pltpu.make_async_copy(zeros, out_ref.at[slot], zero_sems.at[slot])

    mask_copy = pltpu.make_async_copy(mask_ref, mask, mask_sem)
    mask_copy.start()
    fetch(device).start()

    def start_fetch(partner, count):
        mine = owned(partner)

        @pl.when(mine & (partner != device))
        def _():
            fetch(partner).start()

        return count + mine.astype(jnp.int32)

    count = lax.fori_loop(0, devices, start_fetch, jnp.int32(0))

    zeros[...] = jnp.zeros_like(zeros)

    def start_clear(slot, carry):
        clear(slot).start()
        return carry

    lax.fori_loop(count, slots, start_clear, 0)

    mask_copy.wait()
    fetch(device).wait()
    blocks[devices] = blocks[device] * mask[...]
    scale = scale_ref[0]

    def visit(partner, slot):
        mine = owned(partner)

        @pl.when(mine)
        def _():
            @pl.when(partner != device)
            def _():
                fetch(partner).wait()

            buffer = lax.rem(slot, BUFFERS)

            @pl.when(slot >= BUFFERS)
            def _():
                put(buffer, slot - BUFFERS).wait()

            left = jnp.where(partner <= device, partner, devices)
            right = jnp.where(partner <= device, devices, partner)
            step = 128 if aligned else width
            for row in range(0, width, step):
                product = lax.dot_general(
                    blocks[left, :, row:row + step],
                    blocks[right],
                    (((0,), (0,)), ((), ())),
                    preferred_element_type=jnp.float32,
                )
                tiles[buffer, row:row + step, :] = product * scale
            put(buffer, slot).start()

        return slot + mine.astype(jnp.int32)

    lax.fori_loop(0, devices, visit, jnp.int32(0))

    def drain(slot, carry):
        put(lax.rem(slot, BUFFERS), slot).wait()
        return carry

    lax.fori_loop(jnp.maximum(count - BUFFERS, 0), count, drain, 0)

    def end_clear(slot, carry):
        clear(slot).wait()
        return carry

    lax.fori_loop(count, slots, end_clear, 0)


def per_device(tokens, slab_lengths, tile_owner):
    devices = lax.axis_size("col")
    device = lax.axis_index("col")
    reach = devices // 2 + devices // 8
    slots = reach + 1
    slab, units = tokens.shape
    rows = slab * devices
    width = units // devices
    aligned = width % 128 == 0

    x = lax.all_gather(tokens, "col", axis=0, tiled=True)
    if not aligned:
        x = x.reshape(rows, devices, width).transpose(1, 0, 2)

    valid = jnp.arange(slab, dtype=jnp.int32)[None, :] < slab_lengths[:, None]
    mask = jnp.broadcast_to(valid.reshape(rows, 1), (rows, width)).astype(jnp.bfloat16)
    scale = 1.0 / jnp.sum(slab_lengths).astype(jnp.float32)

    return pl.pallas_call(
        functools.partial(tile_kernel, devices, reach, slots, aligned),
        out_shape=jax.ShapeDtypeStruct((slots, width, width), jnp.float32),
        in_specs=[
            pl.BlockSpec(memory_space=pltpu.SMEM),
            pl.BlockSpec(memory_space=pltpu.SMEM),
            pl.BlockSpec(memory_space=pltpu.SMEM),
            pl.BlockSpec(memory_space=pl.ANY),
            pl.BlockSpec(memory_space=pl.ANY),
        ],
        out_specs=pl.BlockSpec(memory_space=pl.ANY),
        scratch_shapes=[
            pltpu.VMEM((devices + 1, rows, width), jnp.bfloat16),
            pltpu.VMEM((rows, width), jnp.bfloat16),
            pltpu.VMEM((BUFFERS, width, width), jnp.float32),
            pltpu.VMEM((width, width), jnp.float32),
            pltpu.SemaphoreType.DMA((devices,)),
            pltpu.SemaphoreType.DMA,
            pltpu.SemaphoreType.DMA((BUFFERS,)),
            pltpu.SemaphoreType.DMA((slots,)),
        ],
        compiler_params=pltpu.CompilerParams(vmem_limit_bytes=50 * 1024 * 1024),
        cost_estimate=pl.CostEstimate(
            flops=2 * slots * rows * width * width,
            bytes_accessed=4 * slots * width * width + 2 * slots * rows * width,
            transcendentals=0,
        ),
    )(tile_owner, device.reshape(1).astype(jnp.int32), scale.reshape(1), x, mask)


def solution(mesh):
    return jax.shard_map(
        per_device,
        mesh=mesh,
        in_specs=(P(("grp", "col"), None), P("grp"), P()),
        out_specs=P(("grp", "col"), None, None),
        check_vma=False,
    )
```

```python
import functools

import jax
import jax.numpy as jnp
import numpy as np
from jax import lax
from jax.experimental import pallas as pl
from jax.experimental.pallas import tpu as pltpu
from jax.sharding import PartitionSpec as P

BUFFERS = 4
RING_LIMIT = 16


def tile_number(devices, device, partner):
    low = jnp.minimum(device, partner)
    high = jnp.maximum(device, partner)
    return low * devices - low * (low - 1) // 2 + (high - low)


def gathered_kernel(
    devices, slots, owner_ref, device_ref, scale_ref, x_ref, mask_ref,
    out_ref, blocks, mask, tiles, zeros, in_sems, mask_sem, out_sems, zero_sems,
):
    device = device_ref[0]
    width = blocks.shape[2]

    def owned(partner):
        return owner_ref[tile_number(devices, device, partner)] == device

    def fetch(partner):
        return pltpu.make_async_copy(x_ref.at[partner], blocks.at[partner], in_sems.at[partner])

    def put(buffer, slot):
        return pltpu.make_async_copy(tiles.at[buffer], out_ref.at[slot], out_sems.at[buffer])

    def clear(slot):
        return pltpu.make_async_copy(zeros, out_ref.at[slot], zero_sems.at[slot])

    mask_copy = pltpu.make_async_copy(mask_ref, mask, mask_sem)
    mask_copy.start()
    fetch(device).start()

    def start_fetch(partner, count):
        mine = owned(partner)

        @pl.when(mine & (partner != device))
        def _():
            fetch(partner).start()

        return count + mine.astype(jnp.int32)

    count = lax.fori_loop(0, devices, start_fetch, jnp.int32(0))

    zeros[...] = jnp.zeros_like(zeros)

    def start_clear(slot, carry):
        clear(slot).start()
        return carry

    lax.fori_loop(count, slots, start_clear, 0)

    mask_copy.wait()
    fetch(device).wait()
    blocks[devices] = blocks[device] * mask[...]
    scale = scale_ref[0]

    def visit(partner, slot):
        mine = owned(partner)

        @pl.when(mine)
        def _():
            @pl.when(partner != device)
            def _():
                fetch(partner).wait()

            buffer = lax.rem(slot, BUFFERS)

            @pl.when(slot >= BUFFERS)
            def _():
                put(buffer, slot - BUFFERS).wait()

            left = jnp.where(partner <= device, partner, devices)
            right = jnp.where(partner <= device, devices, partner)
            product = lax.dot_general(
                blocks[left], blocks[right], (((0,), (0,)), ((), ())),
                preferred_element_type=jnp.float32,
            )
            tiles[buffer] = product * scale
            put(buffer, slot).start()

        return slot + mine.astype(jnp.int32)

    lax.fori_loop(0, devices, visit, jnp.int32(0))

    def drain(slot, carry):
        put(lax.rem(slot, BUFFERS), slot).wait()
        return carry

    lax.fori_loop(jnp.maximum(count - BUFFERS, 0), count, drain, 0)

    def end_clear(slot, carry):
        clear(slot).wait()
        return carry

    lax.fori_loop(count, slots, end_clear, 0)


def gathered_form(tokens, slab_lengths, tile_owner, devices, device, slots, scale):
    slab, units = tokens.shape
    rows = slab * devices
    width = units // devices
    x = lax.all_gather(tokens, "col", axis=0, tiled=True)
    x = x.reshape(rows, devices, width).transpose(1, 0, 2)
    valid = jnp.arange(slab, dtype=jnp.int32)[None, :] < slab_lengths[:, None]
    mask = jnp.broadcast_to(valid.reshape(rows, 1), (rows, width)).astype(jnp.bfloat16)
    return pl.pallas_call(
        functools.partial(gathered_kernel, devices, slots),
        out_shape=jax.ShapeDtypeStruct((slots, width, width), jnp.float32),
        in_specs=[pl.BlockSpec(memory_space=pltpu.SMEM)] * 3 + [pl.BlockSpec(memory_space=pl.ANY)] * 2,
        out_specs=pl.BlockSpec(memory_space=pl.ANY),
        scratch_shapes=[
            pltpu.VMEM((devices + 1, rows, width), jnp.bfloat16),
            pltpu.VMEM((rows, width), jnp.bfloat16),
            pltpu.VMEM((BUFFERS, width, width), jnp.float32),
            pltpu.VMEM((width, width), jnp.float32),
            pltpu.SemaphoreType.DMA((devices,)),
            pltpu.SemaphoreType.DMA,
            pltpu.SemaphoreType.DMA((BUFFERS,)),
            pltpu.SemaphoreType.DMA((slots,)),
        ],
        compiler_params=pltpu.CompilerParams(vmem_limit_bytes=50 * 1024 * 1024),
    )(tile_owner, device.reshape(1), scale.reshape(1), x, mask)


def ring_plan(devices):
    chips = devices // 2
    order = list(range(0, chips, 2)) + list(range(1, chips, 2))[::-1]
    place = {chip: at for at, chip in enumerate(order)}
    onward = []
    for device in range(devices):
        chip, core = divmod(device, 2)
        step = 1 if core == 0 else -1
        onward.append(order[(place[chip] + step) % chips] * 2 + core)
    backward = [onward.index(device) for device in range(devices)]
    return onward, backward


def ring_gather(tokens, devices):
    onward, backward = ring_plan(devices)
    sibling = [device ^ 1 for device in range(devices)]
    here = list(range(devices))

    def send(value, target):
        return lax.ppermute(value, "col", list(enumerate(target)))

    def received(source, target):
        return [source[target.index(device)] for device in range(devices)]

    chips = devices // 2
    ahead, back = tokens, tokens
    ahead_from, back_from = here, here
    slabs, sources = [tokens], [here]
    for step in range(1, chips // 2 + 1):
        ahead = send(ahead, onward)
        ahead_from = received(ahead_from, onward)
        slabs.append(ahead)
        sources.append(ahead_from)
        if 2 * step < chips:
            back = send(back, backward)
            back_from = received(back_from, backward)
            slabs.append(back)
            sources.append(back_from)
    for value, source in list(zip(slabs, sources)):
        slabs.append(send(value, sibling))
        sources.append(received(source, sibling))
    return slabs, np.array(sources, np.int32).T


def ring_kernel(devices, slots, count_in, owner_ref, device_ref, kept_ref, scale_ref, *refs):
    slabs = refs[:count_in]
    out_ref, pair, tiles, zeros, out_sems, zero_sems = refs[count_in:]
    device = device_ref[0]
    slab, width = slabs[0].shape[0], pair.shape[2]

    def owned(partner):
        return owner_ref[tile_number(devices, device, partner)] == device

    def put(buffer, slot):
        return pltpu.make_async_copy(tiles.at[buffer], out_ref.at[slot], out_sems.at[buffer])

    def clear(slot):
        return pltpu.make_async_copy(zeros, out_ref.at[slot], zero_sems.at[slot])

    def column_block(partner, masked):
        columns = pl.ds(pl.multiple_of(partner * width, 128), width)
        parts = []
        for at, ref in enumerate(slabs):
            part = ref[:, columns].astype(jnp.float32)
            if masked:
                row = lax.broadcasted_iota(jnp.int32, (slab, width), 0)
                part = jnp.where(row < kept_ref[at], part, 0.0)
            parts.append(part)
        return jnp.concatenate(parts, axis=0).astype(jnp.bfloat16)

    count = lax.fori_loop(
        0, devices, lambda partner, total: total + owned(partner).astype(jnp.int32), jnp.int32(0)
    )

    @pl.when(count < slots)
    def _():
        zeros[...] = jnp.zeros_like(zeros)

    def start_clear(slot, carry):
        clear(slot).start()
        return carry

    lax.fori_loop(count, slots, start_clear, 0)

    pair[0] = column_block(device, True)
    scale = scale_ref[0]

    def visit(partner, slot):
        mine = owned(partner)

        @pl.when(mine)
        def _():
            buffer = lax.rem(slot, BUFFERS)
            pair[1] = column_block(partner, False)

            @pl.when(slot >= BUFFERS)
            def _():
                put(buffer, slot - BUFFERS).wait()

            left = (partner <= device).astype(jnp.int32)
            for row in range(0, width, 128):
                product = lax.dot_general(
                    pair[left, :, row:row + 128], pair[1 - left], (((0,), (0,)), ((), ())),
                    preferred_element_type=jnp.float32,
                )
                tiles[buffer, row:row + 128, :] = product * scale
            put(buffer, slot).start()

        return slot + mine.astype(jnp.int32)

    lax.fori_loop(0, devices, visit, jnp.int32(0))

    def drain(slot, carry):
        put(lax.rem(slot, BUFFERS), slot).wait()
        return carry

    lax.fori_loop(jnp.maximum(count - BUFFERS, 0), count, drain, 0)

    def end_clear(slot, carry):
        clear(slot).wait()
        return carry

    lax.fori_loop(count, slots, end_clear, 0)


def ring_form(tokens, slab_lengths, tile_owner, devices, device, slots, scale):
    slab, units = tokens.shape
    width = units // devices
    slabs, sources = ring_gather(tokens, devices)
    kept = slab_lengths[jnp.asarray(sources)[device]]
    return pl.pallas_call(
        functools.partial(ring_kernel, devices, slots, len(slabs)),
        out_shape=jax.ShapeDtypeStruct((slots, width, width), jnp.float32),
        in_specs=[pl.BlockSpec(memory_space=pltpu.SMEM)] * 4
        + [pl.BlockSpec(memory_space=pltpu.VMEM)] * len(slabs),
        out_specs=pl.BlockSpec(memory_space=pl.ANY),
        scratch_shapes=[
            pltpu.VMEM((2, slab * devices, width), jnp.bfloat16),
            pltpu.VMEM((BUFFERS, width, width), jnp.float32),
            pltpu.VMEM((width, width), jnp.float32),
            pltpu.SemaphoreType.DMA((BUFFERS,)),
            pltpu.SemaphoreType.DMA((slots,)),
        ],
        compiler_params=pltpu.CompilerParams(vmem_limit_bytes=32 * 1024 * 1024),
        cost_estimate=pl.CostEstimate(
            flops=2 * slots * slab * devices * width * width,
            bytes_accessed=4 * slots * width * width,
            transcendentals=0,
        ),
    )(tile_owner, device.reshape(1), kept, scale.reshape(1), *slabs)


def per_device(tokens, slab_lengths, tile_owner):
    devices = lax.axis_size("col")
    device = lax.axis_index("col").astype(jnp.int32)
    slots = devices // 2 + devices // 8 + 1
    width = tokens.shape[1] // devices
    scale = 1.0 / jnp.sum(slab_lengths).astype(jnp.float32)
    form = ring_form if devices <= RING_LIMIT and width % 128 == 0 else gathered_form
    return form(tokens, slab_lengths, tile_owner, devices, device, slots, scale)


def solution(mesh):
    return jax.shard_map(
        per_device,
        mesh=mesh,
        in_specs=(P(("grp", "col"), None), P("grp"), P()),
        out_specs=P(("grp", "col"), None, None),
        check_vma=False,
    )
```

```python
import functools

import jax
import jax.numpy as jnp
from jax import lax
from jax.experimental import pallas as pl
from jax.experimental.pallas import tpu as pltpu
from jax.sharding import PartitionSpec as P

BUFFERS = 4
RING_LIMIT = 16


def tile_number(devices, device, partner):
    low = jnp.minimum(device, partner)
    high = jnp.maximum(device, partner)
    return low * devices - low * (low - 1) // 2 + (high - low)


def gathered_kernel(
    devices, slots, owner_ref, device_ref, scale_ref, x_ref, mask_ref,
    out_ref, blocks, mask, tiles, zeros, in_sems, mask_sem, out_sems, zero_sems,
):
    device = device_ref[0]
    width = blocks.shape[2]

    def owned(partner):
        return owner_ref[tile_number(devices, device, partner)] == device

    def fetch(partner):
        return pltpu.make_async_copy(x_ref.at[partner], blocks.at[partner], in_sems.at[partner])

    def put(buffer, slot):
        return pltpu.make_async_copy(tiles.at[buffer], out_ref.at[slot], out_sems.at[buffer])

    def clear(slot):
        return pltpu.make_async_copy(zeros, out_ref.at[slot], zero_sems.at[slot])

    mask_copy = pltpu.make_async_copy(mask_ref, mask, mask_sem)
    mask_copy.start()
    fetch(device).start()

    def start_fetch(partner, count):
        mine = owned(partner)

        @pl.when(mine & (partner != device))
        def _():
            fetch(partner).start()

        return count + mine.astype(jnp.int32)

    count = lax.fori_loop(0, devices, start_fetch, jnp.int32(0))

    zeros[...] = jnp.zeros_like(zeros)

    def start_clear(slot, carry):
        clear(slot).start()
        return carry

    lax.fori_loop(count, slots, start_clear, 0)

    mask_copy.wait()
    fetch(device).wait()
    blocks[devices] = blocks[device] * mask[...]
    scale = scale_ref[0]

    def visit(partner, slot):
        mine = owned(partner)

        @pl.when(mine)
        def _():
            @pl.when(partner != device)
            def _():
                fetch(partner).wait()

            buffer = lax.rem(slot, BUFFERS)

            @pl.when(slot >= BUFFERS)
            def _():
                put(buffer, slot - BUFFERS).wait()

            left = jnp.where(partner <= device, partner, devices)
            right = jnp.where(partner <= device, devices, partner)
            product = lax.dot_general(
                blocks[left], blocks[right], (((0,), (0,)), ((), ())),
                preferred_element_type=jnp.float32,
            )
            tiles[buffer] = product * scale
            put(buffer, slot).start()

        return slot + mine.astype(jnp.int32)

    lax.fori_loop(0, devices, visit, jnp.int32(0))

    def drain(slot, carry):
        put(lax.rem(slot, BUFFERS), slot).wait()
        return carry

    lax.fori_loop(jnp.maximum(count - BUFFERS, 0), count, drain, 0)

    def end_clear(slot, carry):
        clear(slot).wait()
        return carry

    lax.fori_loop(count, slots, end_clear, 0)


def gathered_form(tokens, slab_lengths, tile_owner, devices, device, slots):
    slab, units = tokens.shape
    rows = slab * devices
    width = units // devices
    x = lax.all_gather(tokens, "col", axis=0, tiled=True)
    x = x.reshape(rows, devices, width).transpose(1, 0, 2)
    scale = 1.0 / jnp.sum(slab_lengths).astype(jnp.float32)
    valid = jnp.arange(slab, dtype=jnp.int32)[None, :] < slab_lengths[:, None]
    mask = jnp.broadcast_to(valid.reshape(rows, 1), (rows, width)).astype(jnp.bfloat16)
    return pl.pallas_call(
        functools.partial(gathered_kernel, devices, slots),
        out_shape=jax.ShapeDtypeStruct((slots, width, width), jnp.float32),
        in_specs=[pl.BlockSpec(memory_space=pltpu.SMEM)] * 3 + [pl.BlockSpec(memory_space=pl.ANY)] * 2,
        out_specs=pl.BlockSpec(memory_space=pl.ANY),
        scratch_shapes=[
            pltpu.VMEM((devices + 1, rows, width), jnp.bfloat16),
            pltpu.VMEM((rows, width), jnp.bfloat16),
            pltpu.VMEM((BUFFERS, width, width), jnp.float32),
            pltpu.VMEM((width, width), jnp.float32),
            pltpu.SemaphoreType.DMA((devices,)),
            pltpu.SemaphoreType.DMA,
            pltpu.SemaphoreType.DMA((BUFFERS,)),
            pltpu.SemaphoreType.DMA((slots,)),
        ],
        compiler_params=pltpu.CompilerParams(vmem_limit_bytes=50 * 1024 * 1024),
    )(tile_owner, device.reshape(1), scale.reshape(1), x, mask)


def ring_plan(devices):
    chips = devices // 2
    order = list(range(0, chips, 2)) + list(range(1, chips, 2))[::-1]
    place = {chip: at for at, chip in enumerate(order)}
    onward = []
    for device in range(devices):
        chip, core = divmod(device, 2)
        step = 1 if core == 0 else -1
        onward.append(order[(place[chip] + step) % chips] * 2 + core)
    backward = [onward.index(device) for device in range(devices)]
    return onward, backward


def ring_gather(parts, devices):
    onward, backward = ring_plan(devices)
    sibling = [device ^ 1 for device in range(devices)]

    def send(values, target):
        return [lax.ppermute(value, "col", list(enumerate(target))) for value in values]

    chips = devices // 2
    ahead, back = parts, parts
    slabs = [parts]
    for step in range(1, chips // 2 + 1):
        ahead = send(ahead, onward)
        slabs.append(ahead)
        if 2 * step < chips:
            back = send(back, backward)
            slabs.append(back)
    slabs += [send(values, sibling) for values in slabs]
    return [list(part) for part in zip(*slabs)]


def slab_origin(devices, device, number):
    chips = devices // 2
    number, flip = number % chips, number // chips
    hops = (number + 1) // 2 if number % 2 else -(number // 2)
    chip, core = device // 2, device % 2
    core = 1 - core if flip else core
    place = jnp.where(chip % 2 == 0, chip // 2, chips - 1 - chip // 2)
    place = (place - (1 - 2 * core) * hops + chips) % chips
    chip = jnp.where(2 * place < chips, 2 * place, 2 * (chips - 1 - place) + 1)
    return 2 * chip + core


def ring_kernel(devices, slots, cuts, device_ref, table_ref, *refs):
    slabs = [refs[at * devices:(at + 1) * devices] for at in range(len(cuts))]
    out_ref, pair, tiles, zeros, out_sems, zero_sems = refs[len(cuts) * devices:]
    device = device_ref[0]
    slab, width = slabs[0][0].shape[0], pair.shape[2]

    def owned(partner):
        return table_ref[devices + tile_number(devices, device, partner)] == device

    def put(buffer, slot):
        return pltpu.make_async_copy(tiles.at[buffer], out_ref.at[slot], out_sems.at[buffer])

    def clear(slot):
        return pltpu.make_async_copy(zeros, out_ref.at[slot], zero_sems.at[slot])

    def load_block(partner, masked):
        for (start, size), refs_of_part in zip(cuts, slabs):
            columns = pl.ds(pl.multiple_of(partner * size, 128), size)
            parts = []
            for at, ref in enumerate(refs_of_part):
                part = ref[:, columns].astype(jnp.float32)
                if masked:
                    row = lax.broadcasted_iota(jnp.int32, (slab, size), 0)
                    kept = table_ref[slab_origin(devices, device, at)]
                    part = jnp.where(row < kept, part, 0.0)
                parts.append(part)
            block = jnp.concatenate(parts, axis=0).astype(jnp.bfloat16)
            pair[0 if masked else 1, :, start:start + size] = block

    count = lax.fori_loop(
        0, devices, lambda partner, total: total + owned(partner).astype(jnp.int32), jnp.int32(0)
    )

    @pl.when(count < slots)
    def _():
        zeros[...] = jnp.zeros_like(zeros)

    def start_clear(slot, carry):
        clear(slot).start()
        return carry

    lax.fori_loop(count, slots, start_clear, 0)

    load_block(device, True)
    valid_count = lax.fori_loop(0, devices, lambda at, total: total + table_ref[at], jnp.int32(0))
    scale = 1.0 / jnp.full((128, width), valid_count.astype(jnp.float32))

    def visit(partner, slot):
        mine = owned(partner)

        @pl.when(mine)
        def _():
            buffer = lax.rem(slot, BUFFERS)
            load_block(partner, False)

            @pl.when(slot >= BUFFERS)
            def _():
                put(buffer, slot - BUFFERS).wait()

            left = (partner <= device).astype(jnp.int32)
            for row in range(0, width, 128):
                strip = pl.ds(row, 128)
                product = lax.dot_general(
                    pair[left, :, row:row + 128], pair[1 - left], (((0,), (0,)), ((), ())),
                    preferred_element_type=jnp.float32,
                )
                tiles[buffer, strip, :] = product * scale
                pltpu.make_async_copy(
                    tiles.at[buffer, strip], out_ref.at[slot, strip], out_sems.at[buffer]
                ).start()

        return slot + mine.astype(jnp.int32)

    lax.fori_loop(0, devices, visit, jnp.int32(0))

    def drain(slot, carry):
        put(lax.rem(slot, BUFFERS), slot).wait()
        return carry

    lax.fori_loop(jnp.maximum(count - BUFFERS, 0), count, drain, 0)

    def end_clear(slot, carry):
        clear(slot).wait()
        return carry

    lax.fori_loop(count, slots, end_clear, 0)


def ring_form(tokens, slab_lengths, tile_owner, devices, device, slots):
    slab, units = tokens.shape
    width = units // devices
    first = -(-width // 256) * 128
    cuts = [(0, first), (first, width - first)] if first < width else [(0, width)]
    by_block = tokens.reshape(slab, devices, width)
    parts = [by_block[:, :, start:start + size].reshape(slab, devices * size) for start, size in cuts]
    slabs = ring_gather(parts, devices)
    table = jnp.concatenate([slab_lengths, tile_owner])
    return pl.pallas_call(
        functools.partial(ring_kernel, devices, slots, cuts),
        out_shape=jax.ShapeDtypeStruct((slots, width, width), jnp.float32),
        in_specs=[pl.BlockSpec(memory_space=pltpu.SMEM)] * 2
        + [pl.BlockSpec(memory_space=pltpu.VMEM)] * (len(cuts) * devices),
        out_specs=pl.BlockSpec(memory_space=pl.ANY),
        scratch_shapes=[
            pltpu.VMEM((2, slab * devices, width), jnp.bfloat16),
            pltpu.VMEM((BUFFERS, width, width), jnp.float32),
            pltpu.VMEM((width, width), jnp.float32),
            pltpu.SemaphoreType.DMA((BUFFERS,)),
            pltpu.SemaphoreType.DMA((slots,)),
        ],
        compiler_params=pltpu.CompilerParams(vmem_limit_bytes=32 * 1024 * 1024),
        cost_estimate=pl.CostEstimate(
            flops=2 * slots * slab * devices * width * width,
            bytes_accessed=4 * slots * width * width,
            transcendentals=0,
        ),
    )(device.reshape(1), table, *sum(slabs, []))


def per_device(tokens, slab_lengths, tile_owner):
    devices = lax.axis_size("col")
    device = lax.axis_index("col").astype(jnp.int32)
    slots = devices // 2 + devices // 8 + 1
    width = tokens.shape[1] // devices
    form = ring_form if devices <= RING_LIMIT and width % 128 == 0 else gathered_form
    return form(tokens, slab_lengths, tile_owner, devices, device, slots)


def solution(mesh):
    return jax.shard_map(
        per_device,
        mesh=mesh,
        in_specs=(P(("grp", "col"), None), P("grp"), P()),
        out_specs=P(("grp", "col"), None, None),
        check_vma=False,
    )
```

```python
import functools

import jax
import jax.numpy as jnp
from jax import lax
from jax.experimental import pallas as pl
from jax.experimental.pallas import tpu as pltpu
from jax.sharding import PartitionSpec as P

BUFFERS = 4
RING_LIMIT = 16


def tile_number(devices, device, partner):
    low = jnp.minimum(device, partner)
    high = jnp.maximum(device, partner)
    return low * devices - low * (low - 1) // 2 + (high - low)


def gathered_kernel(
    devices, slots, owner_ref, device_ref, scale_ref, x_ref, mask_ref,
    out_ref, blocks, mask, tiles, zeros, in_sems, mask_sem, out_sems, zero_sems,
):
    device = device_ref[0]
    width = blocks.shape[2]

    def owned(partner):
        return owner_ref[tile_number(devices, device, partner)] == device

    def fetch(partner):
        return pltpu.make_async_copy(x_ref.at[partner], blocks.at[partner], in_sems.at[partner])

    def put(buffer, slot):
        return pltpu.make_async_copy(tiles.at[buffer], out_ref.at[slot], out_sems.at[buffer])

    def clear(slot):
        return pltpu.make_async_copy(zeros, out_ref.at[slot], zero_sems.at[slot])

    mask_copy = pltpu.make_async_copy(mask_ref, mask, mask_sem)
    mask_copy.start()
    fetch(device).start()

    def start_fetch(partner, count):
        mine = owned(partner)

        @pl.when(mine & (partner != device))
        def _():
            fetch(partner).start()

        return count + mine.astype(jnp.int32)

    count = lax.fori_loop(0, devices, start_fetch, jnp.int32(0))

    zeros[...] = jnp.zeros_like(zeros)

    def start_clear(slot, carry):
        clear(slot).start()
        return carry

    lax.fori_loop(count, slots, start_clear, 0)

    mask_copy.wait()
    fetch(device).wait()
    blocks[devices] = blocks[device] * mask[...]
    scale = scale_ref[0]

    def visit(partner, slot):
        mine = owned(partner)

        @pl.when(mine)
        def _():
            @pl.when(partner != device)
            def _():
                fetch(partner).wait()

            buffer = lax.rem(slot, BUFFERS)

            @pl.when(slot >= BUFFERS)
            def _():
                put(buffer, slot - BUFFERS).wait()

            left = jnp.where(partner <= device, partner, devices)
            right = jnp.where(partner <= device, devices, partner)
            product = lax.dot_general(
                blocks[left], blocks[right], (((0,), (0,)), ((), ())),
                preferred_element_type=jnp.float32,
            )
            tiles[buffer] = product * scale
            put(buffer, slot).start()

        return slot + mine.astype(jnp.int32)

    lax.fori_loop(0, devices, visit, jnp.int32(0))

    def drain(slot, carry):
        put(lax.rem(slot, BUFFERS), slot).wait()
        return carry

    lax.fori_loop(jnp.maximum(count - BUFFERS, 0), count, drain, 0)

    def end_clear(slot, carry):
        clear(slot).wait()
        return carry

    lax.fori_loop(count, slots, end_clear, 0)


def gathered_form(tokens, slab_lengths, tile_owner, devices, device, slots):
    slab, units = tokens.shape
    rows = slab * devices
    width = units // devices
    x = lax.all_gather(tokens, "col", axis=0, tiled=True)
    x = x.reshape(rows, devices, width).transpose(1, 0, 2)
    scale = 1.0 / jnp.sum(slab_lengths).astype(jnp.float32)
    valid = jnp.arange(slab, dtype=jnp.int32)[None, :] < slab_lengths[:, None]
    mask = jnp.broadcast_to(valid.reshape(rows, 1), (rows, width)).astype(jnp.bfloat16)
    return pl.pallas_call(
        functools.partial(gathered_kernel, devices, slots),
        out_shape=jax.ShapeDtypeStruct((slots, width, width), jnp.float32),
        in_specs=[pl.BlockSpec(memory_space=pltpu.SMEM)] * 3 + [pl.BlockSpec(memory_space=pl.ANY)] * 2,
        out_specs=pl.BlockSpec(memory_space=pl.ANY),
        scratch_shapes=[
            pltpu.VMEM((devices + 1, rows, width), jnp.bfloat16),
            pltpu.VMEM((rows, width), jnp.bfloat16),
            pltpu.VMEM((BUFFERS, width, width), jnp.float32),
            pltpu.VMEM((width, width), jnp.float32),
            pltpu.SemaphoreType.DMA((devices,)),
            pltpu.SemaphoreType.DMA,
            pltpu.SemaphoreType.DMA((BUFFERS,)),
            pltpu.SemaphoreType.DMA((slots,)),
        ],
        compiler_params=pltpu.CompilerParams(vmem_limit_bytes=50 * 1024 * 1024),
    )(tile_owner, device.reshape(1), scale.reshape(1), x, mask)


def ring_plan(devices):
    chips = devices // 2
    order = list(range(0, chips, 2)) + list(range(1, chips, 2))[::-1]
    place = {chip: at for at, chip in enumerate(order)}
    onward = []
    for device in range(devices):
        chip, core = divmod(device, 2)
        step = 1 if core == 0 else -1
        onward.append(order[(place[chip] + step) % chips] * 2 + core)
    backward = [onward.index(device) for device in range(devices)]
    return onward, backward


def ring_gather(tokens, devices):
    onward, backward = ring_plan(devices)
    sibling = [device ^ 1 for device in range(devices)]

    def send(value, target):
        return lax.ppermute(value, "col", list(enumerate(target)))

    chips = devices // 2
    beside = send(tokens, sibling)
    later, beside = lax.optimization_barrier((tokens, beside))
    ahead, back = tokens, later
    slabs, passed = [tokens], [beside]
    for step in range(1, chips // 2 + 1):
        ahead = send(ahead, onward)
        slabs.append(ahead)
        passed.append(send(ahead, sibling))
        if 2 * step < chips:
            back = send(back, backward)
            slabs.append(back)
            passed.append(send(back, sibling))
    return slabs + passed


def slab_origin(devices, device, number):
    chips = devices // 2
    number, flip = number % chips, number // chips
    hops = (number + 1) // 2 if number % 2 else -(number // 2)
    chip, core = device // 2, device % 2
    core = 1 - core if flip else core
    place = jnp.where(chip % 2 == 0, chip // 2, chips - 1 - chip // 2)
    place = (place - (1 - 2 * core) * hops + chips) % chips
    chip = jnp.where(2 * place < chips, 2 * place, 2 * (chips - 1 - place) + 1)
    return 2 * chip + core


def ring_kernel(devices, slots, device_ref, table_ref, *refs):
    slabs = refs[:devices]
    out_ref, pair, tiles, zeros, out_sems, zero_sems = refs[devices:]
    device = device_ref[0]
    slab, width = slabs[0].shape[0], pair.shape[2]

    def owned(partner):
        return table_ref[devices + tile_number(devices, device, partner)] == device

    def put(buffer, slot):
        return pltpu.make_async_copy(tiles.at[buffer], out_ref.at[slot], out_sems.at[buffer])

    def clear(slot):
        return pltpu.make_async_copy(zeros, out_ref.at[slot], zero_sems.at[slot])

    def load_block(partner, masked):
        columns = pl.ds(pl.multiple_of(partner * width, 128), width)
        parts = []
        for at, ref in enumerate(slabs):
            part = ref[:, columns].astype(jnp.float32)
            if masked:
                row = lax.broadcasted_iota(jnp.int32, (slab, width), 0)
                part = jnp.where(row < table_ref[slab_origin(devices, device, at)], part, 0.0)
            parts.append(part)
        pair[0 if masked else 1] = jnp.concatenate(parts, axis=0).astype(jnp.bfloat16)

    count = lax.fori_loop(
        0, devices, lambda partner, total: total + owned(partner).astype(jnp.int32), jnp.int32(0)
    )

    @pl.when(count < slots)
    def _():
        zeros[...] = jnp.zeros_like(zeros)

    def start_clear(slot, carry):
        clear(slot).start()
        return carry

    lax.fori_loop(count, slots, start_clear, 0)

    load_block(device, True)
    valid_count = lax.fori_loop(0, devices, lambda at, total: total + table_ref[at], jnp.int32(0))
    scale = 1.0 / jnp.full((128, width), valid_count.astype(jnp.float32))

    def visit(partner, slot):
        mine = owned(partner)

        @pl.when(mine)
        def _():
            buffer = lax.rem(slot, BUFFERS)
            load_block(partner, False)

            @pl.when(slot >= BUFFERS)
            def _():
                put(buffer, slot - BUFFERS).wait()

            left = (partner <= device).astype(jnp.int32)
            for row in range(0, width, 128):
                strip = pl.ds(row, 128)
                product = lax.dot_general(
                    pair[left, :, row:row + 128], pair[1 - left], (((0,), (0,)), ((), ())),
                    preferred_element_type=jnp.float32,
                )
                tiles[buffer, strip, :] = product * scale
                pltpu.make_async_copy(
                    tiles.at[buffer, strip], out_ref.at[slot, strip], out_sems.at[buffer]
                ).start()

        return slot + mine.astype(jnp.int32)

    lax.fori_loop(0, devices, visit, jnp.int32(0))

    def drain(slot, carry):
        put(lax.rem(slot, BUFFERS), slot).wait()
        return carry

    lax.fori_loop(jnp.maximum(count - BUFFERS, 0), count, drain, 0)

    def end_clear(slot, carry):
        clear(slot).wait()
        return carry

    lax.fori_loop(count, slots, end_clear, 0)


def ring_form(tokens, slab_lengths, tile_owner, devices, device, slots):
    slab, units = tokens.shape
    width = units // devices
    slabs = ring_gather(tokens, devices)
    kept = jnp.arange(slab, dtype=jnp.int32)[:, None] < slab_lengths[device]
    slabs[0] = jnp.where(kept, tokens, jnp.zeros_like(tokens))
    table = jnp.concatenate([slab_lengths, tile_owner])
    return pl.pallas_call(
        functools.partial(ring_kernel, devices, slots),
        out_shape=jax.ShapeDtypeStruct((slots, width, width), jnp.float32),
        in_specs=[pl.BlockSpec(memory_space=pltpu.SMEM)] * 2
        + [pl.BlockSpec(memory_space=pltpu.VMEM)] * devices,
        out_specs=pl.BlockSpec(memory_space=pl.ANY),
        scratch_shapes=[
            pltpu.VMEM((2, slab * devices, width), jnp.bfloat16),
            pltpu.VMEM((BUFFERS, width, width), jnp.float32),
            pltpu.VMEM((width, width), jnp.float32),
            pltpu.SemaphoreType.DMA((BUFFERS,)),
            pltpu.SemaphoreType.DMA((slots,)),
        ],
        compiler_params=pltpu.CompilerParams(vmem_limit_bytes=32 * 1024 * 1024),
        cost_estimate=pl.CostEstimate(
            flops=2 * slots * slab * devices * width * width,
            bytes_accessed=4 * slots * width * width,
            transcendentals=0,
        ),
    )(device.reshape(1), table, *slabs)


def per_device(tokens, slab_lengths, tile_owner):
    devices = lax.axis_size("col")
    device = lax.axis_index("col").astype(jnp.int32)
    slots = devices // 2 + devices // 8 + 1
    width = tokens.shape[1] // devices
    form = ring_form if devices <= RING_LIMIT and width % 128 == 0 else gathered_form
    return form(tokens, slab_lengths, tile_owner, devices, device, slots)


def solution(mesh):
    return jax.shard_map(
        per_device,
        mesh=mesh,
        in_specs=(P(("grp", "col"), None), P("grp"), P()),
        out_specs=P(("grp", "col"), None, None),
        check_vma=False,
    )
```

```python
import functools

import jax
import jax.numpy as jnp
from jax import lax
from jax.experimental import pallas as pl
from jax.experimental.pallas import tpu as pltpu
from jax.sharding import PartitionSpec as P

BUFFERS = 4
RING_LIMIT = 16


def tile_number(devices, device, partner):
    low = jnp.minimum(device, partner)
    high = jnp.maximum(device, partner)
    return low * devices - low * (low - 1) // 2 + (high - low)


def gathered_kernel(
    devices, slots, owner_ref, device_ref, scale_ref, x_ref, mask_ref,
    out_ref, blocks, mask, tiles, zeros, in_sems, mask_sem, out_sems, zero_sems,
):
    device = device_ref[0]
    width = blocks.shape[2]

    def owned(partner):
        return owner_ref[tile_number(devices, device, partner)] == device

    def fetch(partner):
        return pltpu.make_async_copy(x_ref.at[partner], blocks.at[partner], in_sems.at[partner])

    def put(buffer, slot):
        return pltpu.make_async_copy(tiles.at[buffer], out_ref.at[slot], out_sems.at[buffer])

    def clear(slot):
        return pltpu.make_async_copy(zeros, out_ref.at[slot], zero_sems.at[slot])

    mask_copy = pltpu.make_async_copy(mask_ref, mask, mask_sem)
    mask_copy.start()
    fetch(device).start()

    def start_fetch(partner, count):
        mine = owned(partner)

        @pl.when(mine & (partner != device))
        def _():
            fetch(partner).start()

        return count + mine.astype(jnp.int32)

    count = lax.fori_loop(0, devices, start_fetch, jnp.int32(0))

    zeros[...] = jnp.zeros_like(zeros)

    def start_clear(slot, carry):
        clear(slot).start()
        return carry

    lax.fori_loop(count, slots, start_clear, 0)

    mask_copy.wait()
    fetch(device).wait()
    blocks[devices] = blocks[device] * mask[...]
    scale = scale_ref[0]

    def visit(partner, slot):
        mine = owned(partner)

        @pl.when(mine)
        def _():
            @pl.when(partner != device)
            def _():
                fetch(partner).wait()

            buffer = lax.rem(slot, BUFFERS)

            @pl.when(slot >= BUFFERS)
            def _():
                put(buffer, slot - BUFFERS).wait()

            left = jnp.where(partner <= device, partner, devices)
            right = jnp.where(partner <= device, devices, partner)
            product = lax.dot_general(
                blocks[left], blocks[right], (((0,), (0,)), ((), ())),
                preferred_element_type=jnp.float32,
            )
            tiles[buffer] = product * scale
            put(buffer, slot).start()

        return slot + mine.astype(jnp.int32)

    lax.fori_loop(0, devices, visit, jnp.int32(0))

    def drain(slot, carry):
        put(lax.rem(slot, BUFFERS), slot).wait()
        return carry

    lax.fori_loop(jnp.maximum(count - BUFFERS, 0), count, drain, 0)

    def end_clear(slot, carry):
        clear(slot).wait()
        return carry

    lax.fori_loop(count, slots, end_clear, 0)


def gathered_form(tokens, slab_lengths, tile_owner, devices, device, slots):
    slab, units = tokens.shape
    rows = slab * devices
    width = units // devices
    x = lax.all_gather(tokens, "col", axis=0, tiled=True)
    x = x.reshape(rows, devices, width).transpose(1, 0, 2)
    scale = 1.0 / jnp.sum(slab_lengths).astype(jnp.float32)
    valid = jnp.arange(slab, dtype=jnp.int32)[None, :] < slab_lengths[:, None]
    mask = jnp.broadcast_to(valid.reshape(rows, 1), (rows, width)).astype(jnp.bfloat16)
    return pl.pallas_call(
        functools.partial(gathered_kernel, devices, slots),
        out_shape=jax.ShapeDtypeStruct((slots, width, width), jnp.float32),
        in_specs=[pl.BlockSpec(memory_space=pltpu.SMEM)] * 3 + [pl.BlockSpec(memory_space=pl.ANY)] * 2,
        out_specs=pl.BlockSpec(memory_space=pl.ANY),
        scratch_shapes=[
            pltpu.VMEM((devices + 1, rows, width), jnp.bfloat16),
            pltpu.VMEM((rows, width), jnp.bfloat16),
            pltpu.VMEM((BUFFERS, width, width), jnp.float32),
            pltpu.VMEM((width, width), jnp.float32),
            pltpu.SemaphoreType.DMA((devices,)),
            pltpu.SemaphoreType.DMA,
            pltpu.SemaphoreType.DMA((BUFFERS,)),
            pltpu.SemaphoreType.DMA((slots,)),
        ],
        compiler_params=pltpu.CompilerParams(vmem_limit_bytes=50 * 1024 * 1024),
    )(tile_owner, device.reshape(1), scale.reshape(1), x, mask)


def ring_plan(devices):
    chips = devices // 2
    order = list(range(0, chips, 2)) + list(range(1, chips, 2))[::-1]
    place = {chip: at for at, chip in enumerate(order)}
    onward = []
    for device in range(devices):
        chip, core = divmod(device, 2)
        step = 1 if core == 0 else -1
        onward.append(order[(place[chip] + step) % chips] * 2 + core)
    backward = [onward.index(device) for device in range(devices)]
    return onward, backward


def ring_gather(tokens, parts, devices):
    onward, backward = ring_plan(devices)
    sibling = [device ^ 1 for device in range(devices)]

    def send(values, target):
        return [lax.ppermute(value, "col", list(enumerate(target))) for value in values]

    chips = devices // 2
    ahead, back = parts, [tokens]
    slabs, passed = [], [send([tokens], sibling)]
    for step in range(1, chips // 2 + 1):
        ahead = send(ahead, onward)
        slabs.append(ahead)
        passed.append(send(ahead, sibling))
        if 2 * step < chips:
            back = send(back, backward)
            slabs.append(back)
            passed.append(send(back, sibling))
    return slabs + passed


def slab_origin(devices, device, number):
    chips = devices // 2
    number, flip = number % chips, number // chips
    hops = (number + 1) // 2 if number % 2 else -(number // 2)
    chip, core = device // 2, device % 2
    core = 1 - core if flip else core
    place = jnp.where(chip % 2 == 0, chip // 2, chips - 1 - chip // 2)
    place = (place - (1 - 2 * core) * hops + chips) % chips
    chip = jnp.where(2 * place < chips, 2 * place, 2 * (chips - 1 - place) + 1)
    return 2 * chip + core


def ring_kernel(devices, slots, sizes, device_ref, table_ref, *refs):
    refs = list(refs)
    slabs = [[refs.pop(0) for _ in group] for group in sizes]
    out_ref, pair, tiles, zeros, out_sems, zero_sems = refs
    device = device_ref[0]
    slab, width = slabs[0][0].shape[0], pair.shape[2]

    def owned(partner):
        return table_ref[devices + tile_number(devices, device, partner)] == device

    def put(buffer, slot):
        return pltpu.make_async_copy(tiles.at[buffer], out_ref.at[slot], out_sems.at[buffer])

    def clear(slot):
        return pltpu.make_async_copy(zeros, out_ref.at[slot], zero_sems.at[slot])

    def load_block(partner, masked):
        parts = []
        for at, (group, group_sizes) in enumerate(zip(slabs, sizes)):
            pieces = [
                ref[:, pl.ds(pl.multiple_of(partner * size, 128), size)].astype(jnp.float32)
                for ref, size in zip(group, group_sizes)
            ]
            part = pieces[0] if len(pieces) == 1 else jnp.concatenate(pieces, axis=1)
            if masked:
                row = lax.broadcasted_iota(jnp.int32, (slab, width), 0)
                part = jnp.where(row < table_ref[slab_origin(devices, device, at)], part, 0.0)
            parts.append(part)
        pair[0 if masked else 1] = jnp.concatenate(parts, axis=0).astype(jnp.bfloat16)

    count = lax.fori_loop(
        0, devices, lambda partner, total: total + owned(partner).astype(jnp.int32), jnp.int32(0)
    )

    @pl.when(count < slots)
    def _():
        zeros[...] = jnp.zeros_like(zeros)

    def start_clear(slot, carry):
        clear(slot).start()
        return carry

    lax.fori_loop(count, slots, start_clear, 0)

    load_block(device, True)
    valid_count = lax.fori_loop(0, devices, lambda at, total: total + table_ref[at], jnp.int32(0))
    scale = 1.0 / jnp.full((128, width), valid_count.astype(jnp.float32))

    def visit(partner, slot):
        mine = owned(partner)

        @pl.when(mine)
        def _():
            buffer = lax.rem(slot, BUFFERS)
            load_block(partner, False)

            @pl.when(slot >= BUFFERS)
            def _():
                put(buffer, slot - BUFFERS).wait()

            left = (partner <= device).astype(jnp.int32)
            for row in range(0, width, 128):
                strip = pl.ds(row, 128)
                product = lax.dot_general(
                    pair[left, :, row:row + 128], pair[1 - left], (((0,), (0,)), ((), ())),
                    preferred_element_type=jnp.float32,
                )
                tiles[buffer, strip, :] = product * scale
                pltpu.make_async_copy(
                    tiles.at[buffer, strip], out_ref.at[slot, strip], out_sems.at[buffer]
                ).start()

        return slot + mine.astype(jnp.int32)

    lax.fori_loop(0, devices, visit, jnp.int32(0))

    def drain(slot, carry):
        put(lax.rem(slot, BUFFERS), slot).wait()
        return carry

    lax.fori_loop(jnp.maximum(count - BUFFERS, 0), count, drain, 0)

    def end_clear(slot, carry):
        clear(slot).wait()
        return carry

    lax.fori_loop(count, slots, end_clear, 0)


def ring_form(tokens, slab_lengths, tile_owner, devices, device, slots):
    slab, units = tokens.shape
    width = units // devices
    first = -(-width // 256) * 128
    by_block = tokens.reshape(slab, devices, width)
    parts = [
        by_block[:, :, start:stop].reshape(slab, devices * (stop - start))
        for start, stop in ((0, first), (first, width)) if start < stop
    ]
    kept = jnp.arange(slab, dtype=jnp.int32)[:, None] < slab_lengths[device]
    slabs = [[jnp.where(kept, tokens, jnp.zeros_like(tokens))]] + ring_gather(tokens, parts, devices)
    sizes = [[value.shape[1] // devices for value in group] for group in slabs]
    table = jnp.concatenate([slab_lengths, tile_owner])
    return pl.pallas_call(
        functools.partial(ring_kernel, devices, slots, sizes),
        out_shape=jax.ShapeDtypeStruct((slots, width, width), jnp.float32),
        in_specs=[pl.BlockSpec(memory_space=pltpu.SMEM)] * 2
        + [pl.BlockSpec(memory_space=pltpu.VMEM)] * sum(len(group) for group in slabs),
        out_specs=pl.BlockSpec(memory_space=pl.ANY),
        scratch_shapes=[
            pltpu.VMEM((2, slab * devices, width), jnp.bfloat16),
            pltpu.VMEM((BUFFERS, width, width), jnp.float32),
            pltpu.VMEM((width, width), jnp.float32),
            pltpu.SemaphoreType.DMA((BUFFERS,)),
            pltpu.SemaphoreType.DMA((slots,)),
        ],
        compiler_params=pltpu.CompilerParams(vmem_limit_bytes=32 * 1024 * 1024),
        cost_estimate=pl.CostEstimate(
            flops=2 * slots * slab * devices * width * width,
            bytes_accessed=4 * slots * width * width,
            transcendentals=0,
        ),
    )(device.reshape(1), table, *sum(slabs, []))


def per_device(tokens, slab_lengths, tile_owner):
    devices = lax.axis_size("col")
    device = lax.axis_index("col").astype(jnp.int32)
    slots = devices // 2 + devices // 8 + 1
    width = tokens.shape[1] // devices
    form = ring_form if devices <= RING_LIMIT and width % 128 == 0 else gathered_form
    return form(tokens, slab_lengths, tile_owner, devices, device, slots)


def solution(mesh):
    return jax.shard_map(
        per_device,
        mesh=mesh,
        in_specs=(P(("grp", "col"), None), P("grp"), P()),
        out_specs=P(("grp", "col"), None, None),
        check_vma=False,
    )
```

```python
import functools

import jax
import jax.numpy as jnp
from jax import lax
from jax.experimental import pallas as pl
from jax.experimental.pallas import tpu as pltpu
from jax.sharding import PartitionSpec as P

BUFFERS = 4
RING_LIMIT = 16


def tile_number(devices, device, partner):
    low = jnp.minimum(device, partner)
    high = jnp.maximum(device, partner)
    return low * devices - low * (low - 1) // 2 + (high - low)


def gathered_kernel(
    devices, slots, owner_ref, device_ref, scale_ref, x_ref, mask_ref,
    out_ref, blocks, mask, tiles, zeros, in_sems, mask_sem, out_sems, zero_sems,
):
    device = device_ref[0]
    width = blocks.shape[2]

    def owned(partner):
        return owner_ref[tile_number(devices, device, partner)] == device

    def fetch(partner):
        return pltpu.make_async_copy(x_ref.at[partner], blocks.at[partner], in_sems.at[partner])

    def put(buffer, slot):
        return pltpu.make_async_copy(tiles.at[buffer], out_ref.at[slot], out_sems.at[buffer])

    def clear(slot):
        return pltpu.make_async_copy(zeros, out_ref.at[slot], zero_sems.at[slot])

    mask_copy = pltpu.make_async_copy(mask_ref, mask, mask_sem)
    mask_copy.start()
    fetch(device).start()

    def start_fetch(partner, count):
        mine = owned(partner)

        @pl.when(mine & (partner != device))
        def _():
            fetch(partner).start()

        return count + mine.astype(jnp.int32)

    count = lax.fori_loop(0, devices, start_fetch, jnp.int32(0))

    zeros[...] = jnp.zeros_like(zeros)

    def start_clear(slot, carry):
        clear(slot).start()
        return carry

    lax.fori_loop(count, slots, start_clear, 0)

    mask_copy.wait()
    fetch(device).wait()
    blocks[devices] = blocks[device] * mask[...]
    scale = scale_ref[0]

    def visit(partner, slot):
        mine = owned(partner)

        @pl.when(mine)
        def _():
            @pl.when(partner != device)
            def _():
                fetch(partner).wait()

            buffer = lax.rem(slot, BUFFERS)

            @pl.when(slot >= BUFFERS)
            def _():
                put(buffer, slot - BUFFERS).wait()

            left = jnp.where(partner <= device, partner, devices)
            right = jnp.where(partner <= device, devices, partner)
            product = lax.dot_general(
                blocks[left], blocks[right], (((0,), (0,)), ((), ())),
                preferred_element_type=jnp.float32,
            )
            tiles[buffer] = product * scale
            put(buffer, slot).start()

        return slot + mine.astype(jnp.int32)

    lax.fori_loop(0, devices, visit, jnp.int32(0))

    def drain(slot, carry):
        put(lax.rem(slot, BUFFERS), slot).wait()
        return carry

    lax.fori_loop(jnp.maximum(count - BUFFERS, 0), count, drain, 0)

    def end_clear(slot, carry):
        clear(slot).wait()
        return carry

    lax.fori_loop(count, slots, end_clear, 0)


def gathered_form(tokens, slab_lengths, tile_owner, devices, device, slots):
    slab, units = tokens.shape
    rows = slab * devices
    width = units // devices
    x = lax.all_gather(tokens, "col", axis=0, tiled=True)
    x = x.reshape(rows, devices, width).transpose(1, 0, 2)
    scale = 1.0 / jnp.sum(slab_lengths).astype(jnp.float32)
    valid = jnp.arange(slab, dtype=jnp.int32)[None, :] < slab_lengths[:, None]
    mask = jnp.broadcast_to(valid.reshape(rows, 1), (rows, width)).astype(jnp.bfloat16)
    return pl.pallas_call(
        functools.partial(gathered_kernel, devices, slots),
        out_shape=jax.ShapeDtypeStruct((slots, width, width), jnp.float32),
        in_specs=[pl.BlockSpec(memory_space=pltpu.SMEM)] * 3 + [pl.BlockSpec(memory_space=pl.ANY)] * 2,
        out_specs=pl.BlockSpec(memory_space=pl.ANY),
        scratch_shapes=[
            pltpu.VMEM((devices + 1, rows, width), jnp.bfloat16),
            pltpu.VMEM((rows, width), jnp.bfloat16),
            pltpu.VMEM((BUFFERS, width, width), jnp.float32),
            pltpu.VMEM((width, width), jnp.float32),
            pltpu.SemaphoreType.DMA((devices,)),
            pltpu.SemaphoreType.DMA,
            pltpu.SemaphoreType.DMA((BUFFERS,)),
            pltpu.SemaphoreType.DMA((slots,)),
        ],
        compiler_params=pltpu.CompilerParams(vmem_limit_bytes=50 * 1024 * 1024),
    )(tile_owner, device.reshape(1), scale.reshape(1), x, mask)


def ring_plan(devices):
    chips = devices // 2
    order = list(range(0, chips, 2)) + list(range(1, chips, 2))[::-1]
    place = {chip: at for at, chip in enumerate(order)}
    onward = []
    for device in range(devices):
        chip, core = divmod(device, 2)
        step = 1 if core == 0 else -1
        onward.append(order[(place[chip] + step) % chips] * 2 + core)
    backward = [onward.index(device) for device in range(devices)]
    return onward, backward


def ring_gather(tokens, parts, devices):
    onward, backward = ring_plan(devices)
    sibling = [device ^ 1 for device in range(devices)]

    def send(values, target):
        return [lax.ppermute(value, "col", list(enumerate(target))) for value in values]

    def after(values, others):
        return list(lax.optimization_barrier((*values, *others))[:len(values)])

    chips = devices // 2
    ahead, back = parts, [tokens]
    slabs, passed = [], [send([tokens], sibling)]
    for step in range(1, chips // 2 + 1):
        if step > 1:
            ahead = ahead[:1] + after(ahead[1:], ahead[:1])
        ahead = send(ahead, onward)
        slabs.append(ahead)
        if 2 * step < chips:
            back = send(back if step == 1 else after(back, ahead_before[-1:]), backward)
            slabs.append(back)
            passed += [(ahead, back), (back, None)]
        else:
            passed.append((ahead, None))
        ahead_before = ahead
    beside = passed[:1]
    for values, others in passed[1:]:
        beside.append(send(after(values, others) if others else values, sibling))
    return slabs + beside


def slab_origin(devices, device, number):
    chips = devices // 2
    number, flip = number % chips, number // chips
    hops = (number + 1) // 2 if number % 2 else -(number // 2)
    chip, core = device // 2, device % 2
    core = 1 - core if flip else core
    place = jnp.where(chip % 2 == 0, chip // 2, chips - 1 - chip // 2)
    place = (place - (1 - 2 * core) * hops + chips) % chips
    chip = jnp.where(2 * place < chips, 2 * place, 2 * (chips - 1 - place) + 1)
    return 2 * chip + core


def ring_kernel(devices, slots, sizes, device_ref, table_ref, *refs):
    refs = list(refs)
    slabs = [[refs.pop(0) for _ in group] for group in sizes]
    out_ref, pair, tiles, zeros, out_sems, zero_sems = refs
    device = device_ref[0]
    slab, width = slabs[0][0].shape[0], pair.shape[2]

    def owned(partner):
        return table_ref[devices + tile_number(devices, device, partner)] == device

    def put(buffer, slot):
        return pltpu.make_async_copy(tiles.at[buffer], out_ref.at[slot], out_sems.at[buffer])

    def clear(slot):
        return pltpu.make_async_copy(zeros, out_ref.at[slot], zero_sems.at[slot])

    def load_block(partner, masked):
        parts = []
        for at, (group, group_sizes) in enumerate(zip(slabs, sizes)):
            pieces = [
                ref[:, pl.ds(pl.multiple_of(partner * size, 128), size)].astype(jnp.float32)
                for ref, size in zip(group, group_sizes)
            ]
            part = pieces[0] if len(pieces) == 1 else jnp.concatenate(pieces, axis=1)
            if masked:
                row = lax.broadcasted_iota(jnp.int32, (slab, width), 0)
                part = jnp.where(row < table_ref[slab_origin(devices, device, at)], part, 0.0)
            parts.append(part)
        pair[0 if masked else 1] = jnp.concatenate(parts, axis=0).astype(jnp.bfloat16)

    count = lax.fori_loop(
        0, devices, lambda partner, total: total + owned(partner).astype(jnp.int32), jnp.int32(0)
    )

    @pl.when(count < slots)
    def _():
        zeros[...] = jnp.zeros_like(zeros)

    def start_clear(slot, carry):
        clear(slot).start()
        return carry

    lax.fori_loop(count, slots, start_clear, 0)

    load_block(device, True)
    valid_count = lax.fori_loop(0, devices, lambda at, total: total + table_ref[at], jnp.int32(0))
    scale = 1.0 / jnp.full((128, width), valid_count.astype(jnp.float32))

    def visit(partner, slot):
        mine = owned(partner)

        @pl.when(mine)
        def _():
            buffer = lax.rem(slot, BUFFERS)
            load_block(partner, False)

            @pl.when(slot >= BUFFERS)
            def _():
                put(buffer, slot - BUFFERS).wait()

            left = (partner <= device).astype(jnp.int32)
            for row in range(0, width, 128):
                strip = pl.ds(row, 128)
                product = lax.dot_general(
                    pair[left, :, row:row + 128], pair[1 - left], (((0,), (0,)), ((), ())),
                    preferred_element_type=jnp.float32,
                )
                tiles[buffer, strip, :] = product * scale
                pltpu.make_async_copy(
                    tiles.at[buffer, strip], out_ref.at[slot, strip], out_sems.at[buffer]
                ).start()

        return slot + mine.astype(jnp.int32)

    lax.fori_loop(0, devices, visit, jnp.int32(0))

    def drain(slot, carry):
        put(lax.rem(slot, BUFFERS), slot).wait()
        return carry

    lax.fori_loop(jnp.maximum(count - BUFFERS, 0), count, drain, 0)

    def end_clear(slot, carry):
        clear(slot).wait()
        return carry

    lax.fori_loop(count, slots, end_clear, 0)


def ring_form(tokens, slab_lengths, tile_owner, devices, device, slots):
    slab, units = tokens.shape
    width = units // devices
    first = -(-width // 256) * 128
    by_block = tokens.reshape(slab, devices, width)
    parts = [
        by_block[:, :, start:stop].reshape(slab, devices * (stop - start))
        for start, stop in ((0, first), (first, width)) if start < stop
    ]
    parts = list(lax.optimization_barrier(tuple(parts)))
    slabs = [parts] + ring_gather(tokens, parts, devices)
    sizes = [[value.shape[1] // devices for value in group] for group in slabs]
    table = jnp.concatenate([slab_lengths, tile_owner])
    return pl.pallas_call(
        functools.partial(ring_kernel, devices, slots, sizes),
        out_shape=jax.ShapeDtypeStruct((slots, width, width), jnp.float32),
        in_specs=[pl.BlockSpec(memory_space=pltpu.SMEM)] * 2
        + [pl.BlockSpec(memory_space=pltpu.VMEM)] * sum(len(group) for group in slabs),
        out_specs=pl.BlockSpec(memory_space=pl.ANY),
        scratch_shapes=[
            pltpu.VMEM((2, slab * devices, width), jnp.bfloat16),
            pltpu.VMEM((BUFFERS, width, width), jnp.float32),
            pltpu.VMEM((width, width), jnp.float32),
            pltpu.SemaphoreType.DMA((BUFFERS,)),
            pltpu.SemaphoreType.DMA((slots,)),
        ],
        compiler_params=pltpu.CompilerParams(vmem_limit_bytes=32 * 1024 * 1024),
        cost_estimate=pl.CostEstimate(
            flops=2 * slots * slab * devices * width * width,
            bytes_accessed=4 * slots * width * width,
            transcendentals=0,
        ),
    )(device.reshape(1), table, *sum(slabs, []))


def per_device(tokens, slab_lengths, tile_owner):
    devices = lax.axis_size("col")
    device = lax.axis_index("col").astype(jnp.int32)
    slots = devices // 2 + devices // 8 + 1
    width = tokens.shape[1] // devices
    form = ring_form if devices <= RING_LIMIT and width % 128 == 0 else gathered_form
    return form(tokens, slab_lengths, tile_owner, devices, device, slots)


def solution(mesh):
    return jax.shard_map(
        per_device,
        mesh=mesh,
        in_specs=(P(("grp", "col"), None), P("grp"), P()),
        out_specs=P(("grp", "col"), None, None),
        check_vma=False,
    )
```

```python
import functools

import jax
import jax.numpy as jnp
from jax import lax
from jax.experimental import pallas as pl
from jax.experimental.pallas import tpu as pltpu
from jax.sharding import PartitionSpec as P

BUFFERS = 4
RING_DEVICES = 16


def tile_number(devices, device, partner):
    low = jnp.minimum(device, partner)
    high = jnp.maximum(device, partner)
    return low * devices - low * (low - 1) // 2 + (high - low)


def gathered_kernel(
    devices, slots, owner_ref, device_ref, scale_ref, x_ref, mask_ref,
    out_ref, blocks, mask, tiles, zeros, in_sems, mask_sem, out_sems, zero_sems,
):
    device = device_ref[0]
    width = blocks.shape[2]

    def owned(partner):
        return owner_ref[tile_number(devices, device, partner)] == device

    def fetch(partner):
        return pltpu.make_async_copy(x_ref.at[partner], blocks.at[partner], in_sems.at[partner])

    def put(buffer, slot):
        return pltpu.make_async_copy(tiles.at[buffer], out_ref.at[slot], out_sems.at[buffer])

    def clear(slot):
        return pltpu.make_async_copy(zeros, out_ref.at[slot], zero_sems.at[slot])

    mask_copy = pltpu.make_async_copy(mask_ref, mask, mask_sem)
    mask_copy.start()
    fetch(device).start()

    def start_fetch(partner, count):
        mine = owned(partner)

        @pl.when(mine & (partner != device))
        def _():
            fetch(partner).start()

        return count + mine.astype(jnp.int32)

    count = lax.fori_loop(0, devices, start_fetch, jnp.int32(0))

    zeros[...] = jnp.zeros_like(zeros)

    def start_clear(slot, carry):
        clear(slot).start()
        return carry

    lax.fori_loop(count, slots, start_clear, 0)

    mask_copy.wait()
    fetch(device).wait()
    blocks[devices] = blocks[device] * mask[...]
    scale = scale_ref[0]

    def visit(partner, slot):
        mine = owned(partner)

        @pl.when(mine)
        def _():
            @pl.when(partner != device)
            def _():
                fetch(partner).wait()

            buffer = lax.rem(slot, BUFFERS)

            @pl.when(slot >= BUFFERS)
            def _():
                put(buffer, slot - BUFFERS).wait()

            left = jnp.where(partner <= device, partner, devices)
            right = jnp.where(partner <= device, devices, partner)
            product = lax.dot_general(
                blocks[left], blocks[right], (((0,), (0,)), ((), ())),
                preferred_element_type=jnp.float32,
            )
            tiles[buffer] = product * scale
            put(buffer, slot).start()

        return slot + mine.astype(jnp.int32)

    lax.fori_loop(0, devices, visit, jnp.int32(0))

    def drain(slot, carry):
        put(lax.rem(slot, BUFFERS), slot).wait()
        return carry

    lax.fori_loop(jnp.maximum(count - BUFFERS, 0), count, drain, 0)

    def end_clear(slot, carry):
        clear(slot).wait()
        return carry

    lax.fori_loop(count, slots, end_clear, 0)


def gathered_form(tokens, slab_lengths, tile_owner, devices, device, slots):
    slab, units = tokens.shape
    rows = slab * devices
    width = units // devices
    x = lax.all_gather(tokens, "col", axis=0, tiled=True)
    x = x.reshape(rows, devices, width).transpose(1, 0, 2)
    scale = 1.0 / jnp.sum(slab_lengths).astype(jnp.float32)
    valid = jnp.arange(slab, dtype=jnp.int32)[None, :] < slab_lengths[:, None]
    mask = jnp.broadcast_to(valid.reshape(rows, 1), (rows, width)).astype(jnp.bfloat16)
    return pl.pallas_call(
        functools.partial(gathered_kernel, devices, slots),
        out_shape=jax.ShapeDtypeStruct((slots, width, width), jnp.float32),
        in_specs=[pl.BlockSpec(memory_space=pltpu.SMEM)] * 3 + [pl.BlockSpec(memory_space=pl.ANY)] * 2,
        out_specs=pl.BlockSpec(memory_space=pl.ANY),
        scratch_shapes=[
            pltpu.VMEM((devices + 1, rows, width), jnp.bfloat16),
            pltpu.VMEM((rows, width), jnp.bfloat16),
            pltpu.VMEM((BUFFERS, width, width), jnp.float32),
            pltpu.VMEM((width, width), jnp.float32),
            pltpu.SemaphoreType.DMA((devices,)),
            pltpu.SemaphoreType.DMA,
            pltpu.SemaphoreType.DMA((BUFFERS,)),
            pltpu.SemaphoreType.DMA((slots,)),
        ],
        compiler_params=pltpu.CompilerParams(vmem_limit_bytes=50 * 1024 * 1024),
    )(tile_owner, device.reshape(1), scale.reshape(1), x, mask)


def ring_plan(devices):
    chips = devices // 2
    order = list(range(0, chips, 2)) + list(range(1, chips, 2))[::-1]
    place = {chip: at for at, chip in enumerate(order)}

    def moved(device, hops):
        chip, core = divmod(device, 2)
        return order[(place[chip] + (hops if core == 0 else -hops)) % chips] * 2 + core

    def target(hops):
        return [moved(device, hops) for device in range(devices)]

    return target, place


def ring_gather(tokens, device, devices):
    target, place = ring_plan(devices)
    sibling = [device ^ 1 for device in range(devices)]
    corner = [place[at // 2] in (0, 3, 4, 7) for at in range(devices)]
    across = [at ^ 2 for at in range(devices)]

    def send(value, target):
        return lax.ppermute(value, "col", list(enumerate(target)))

    def after(value, *others):
        return lax.optimization_barrier((value, *others))[0]

    straight = send(tokens, [there if corner[at] else at for at, there in enumerate(target(4))])
    own = send(tokens, list(range(devices)))
    ahead, back = [tokens], [tokens]
    for _ in range(3):
        ahead.append(send(ahead[-1], target(1)))
        back.append(send(back[-1], target(-1)))
    chip, core = device // 2, device % 2
    at_corner = (chip < 2) | (chip >= devices // 2 - 2)
    came_ahead = ((chip == 3) | (chip == 4)) == (core == 0)
    held = jnp.where(at_corner, after(straight, ahead[2], back[2]), jnp.where(came_ahead, ahead[1], back[1]))
    half = send(held, [at if corner[at] else across[at] for at in range(devices)])
    slabs = [own, ahead[1], back[1], ahead[2], back[2], ahead[3], back[3], half]
    beside = [
        tokens, after(ahead[1], back[1]), after(back[1], ahead[1]), after(ahead[2], back[2]),
        after(back[2], ahead[2]), ahead[3], back[3], half,
    ]
    return slabs + [send(value, sibling) for value in beside]


def slab_origin(devices, device, number):
    chips = devices // 2
    number, flip = number % chips, number // chips
    hops = (number + 1) // 2 if number % 2 else -(number // 2)
    chip, core = device // 2, device % 2
    core = 1 - core if flip else core
    place = jnp.where(chip % 2 == 0, chip // 2, chips - 1 - chip // 2)
    place = (place - (1 - 2 * core) * hops + chips) % chips
    chip = jnp.where(2 * place < chips, 2 * place, 2 * (chips - 1 - place) + 1)
    return 2 * chip + core


def ring_kernel(devices, slots, device_ref, table_ref, *refs):
    slabs = refs[:devices]
    out_ref, pair, tiles, zeros, out_sems, zero_sems = refs[devices:]
    device = device_ref[0]
    slab, width = slabs[0].shape[0], pair.shape[2]

    def owned(partner):
        return table_ref[devices + tile_number(devices, device, partner)] == device

    def put(buffer, slot):
        return pltpu.make_async_copy(tiles.at[buffer], out_ref.at[slot], out_sems.at[buffer])

    def clear(slot):
        return pltpu.make_async_copy(zeros, out_ref.at[slot], zero_sems.at[slot])

    def load_block(partner, masked):
        columns = pl.ds(pl.multiple_of(partner * width, 128), width)
        parts = []
        for at, ref in enumerate(slabs):
            part = ref[:, columns].astype(jnp.float32)
            if masked:
                row = lax.broadcasted_iota(jnp.int32, (slab, width), 0)
                part = jnp.where(row < table_ref[slab_origin(devices, device, at)], part, 0.0)
            parts.append(part)
        pair[0 if masked else 1] = jnp.concatenate(parts, axis=0).astype(jnp.bfloat16)

    count = lax.fori_loop(
        0, devices, lambda partner, total: total + owned(partner).astype(jnp.int32), jnp.int32(0)
    )

    @pl.when(count < slots)
    def _():
        zeros[...] = jnp.zeros_like(zeros)

    def start_clear(slot, carry):
        clear(slot).start()
        return carry

    lax.fori_loop(count, slots, start_clear, 0)

    load_block(device, True)
    valid_count = lax.fori_loop(0, devices, lambda at, total: total + table_ref[at], jnp.int32(0))
    scale = 1.0 / jnp.full((128, width), valid_count.astype(jnp.float32))

    def visit(partner, slot):
        mine = owned(partner)

        @pl.when(mine)
        def _():
            buffer = lax.rem(slot, BUFFERS)
            load_block(partner, False)

            @pl.when(slot >= BUFFERS)
            def _():
                put(buffer, slot - BUFFERS).wait()

            left = (partner <= device).astype(jnp.int32)
            for row in range(0, width, 128):
                strip = pl.ds(row, 128)
                product = lax.dot_general(
                    pair[left, :, row:row + 128], pair[1 - left], (((0,), (0,)), ((), ())),
                    preferred_element_type=jnp.float32,
                )
                tiles[buffer, strip, :] = product * scale
                pltpu.make_async_copy(
                    tiles.at[buffer, strip], out_ref.at[slot, strip], out_sems.at[buffer]
                ).start()

        return slot + mine.astype(jnp.int32)

    lax.fori_loop(0, devices, visit, jnp.int32(0))

    def drain(slot, carry):
        put(lax.rem(slot, BUFFERS), slot).wait()
        return carry

    lax.fori_loop(jnp.maximum(count - BUFFERS, 0), count, drain, 0)

    def end_clear(slot, carry):
        clear(slot).wait()
        return carry

    lax.fori_loop(count, slots, end_clear, 0)


def ring_form(tokens, slab_lengths, tile_owner, devices, device, slots):
    slab, units = tokens.shape
    width = units // devices
    slabs = ring_gather(tokens, device, devices)
    table = jnp.concatenate([slab_lengths, tile_owner])
    return pl.pallas_call(
        functools.partial(ring_kernel, devices, slots),
        out_shape=jax.ShapeDtypeStruct((slots, width, width), jnp.float32),
        in_specs=[pl.BlockSpec(memory_space=pltpu.SMEM)] * 2
        + [pl.BlockSpec(memory_space=pltpu.VMEM)] * devices,
        out_specs=pl.BlockSpec(memory_space=pl.ANY),
        scratch_shapes=[
            pltpu.VMEM((2, slab * devices, width), jnp.bfloat16),
            pltpu.VMEM((BUFFERS, width, width), jnp.float32),
            pltpu.VMEM((width, width), jnp.float32),
            pltpu.SemaphoreType.DMA((BUFFERS,)),
            pltpu.SemaphoreType.DMA((slots,)),
        ],
        compiler_params=pltpu.CompilerParams(vmem_limit_bytes=32 * 1024 * 1024),
        cost_estimate=pl.CostEstimate(
            flops=2 * slots * slab * devices * width * width,
            bytes_accessed=4 * slots * width * width,
            transcendentals=0,
        ),
    )(device.reshape(1), table, *slabs)


def per_device(tokens, slab_lengths, tile_owner):
    devices = lax.axis_size("col")
    device = lax.axis_index("col").astype(jnp.int32)
    slots = devices // 2 + devices // 8 + 1
    width = tokens.shape[1] // devices
    form = ring_form if devices == RING_DEVICES and width % 128 == 0 else gathered_form
    return form(tokens, slab_lengths, tile_owner, devices, device, slots)


def solution(mesh):
    return jax.shard_map(
        per_device,
        mesh=mesh,
        in_specs=(P(("grp", "col"), None), P("grp"), P()),
        out_specs=P(("grp", "col"), None, None),
        check_vma=False,
    )
```

```python
import functools

import jax
import jax.numpy as jnp
from jax import lax
from jax.experimental import pallas as pl
from jax.experimental.pallas import tpu as pltpu
from jax.sharding import PartitionSpec as P

BUFFERS = 4
RING_DEVICES = 16


def tile_number(devices, device, partner):
    low = jnp.minimum(device, partner)
    high = jnp.maximum(device, partner)
    return low * devices - low * (low - 1) // 2 + (high - low)


def gathered_kernel(
    devices, slots, owner_ref, device_ref, scale_ref, x_ref, mask_ref,
    out_ref, blocks, mask, tiles, zeros, in_sems, mask_sem, out_sems, zero_sems,
):
    device = device_ref[0]
    width = blocks.shape[2]

    def owned(partner):
        return owner_ref[tile_number(devices, device, partner)] == device

    def fetch(partner):
        return pltpu.make_async_copy(x_ref.at[partner], blocks.at[partner], in_sems.at[partner])

    def put(buffer, slot):
        return pltpu.make_async_copy(tiles.at[buffer], out_ref.at[slot], out_sems.at[buffer])

    def clear(slot):
        return pltpu.make_async_copy(zeros, out_ref.at[slot], zero_sems.at[slot])

    mask_copy = pltpu.make_async_copy(mask_ref, mask, mask_sem)
    mask_copy.start()
    fetch(device).start()

    def start_fetch(partner, count):
        mine = owned(partner)

        @pl.when(mine & (partner != device))
        def _():
            fetch(partner).start()

        return count + mine.astype(jnp.int32)

    count = lax.fori_loop(0, devices, start_fetch, jnp.int32(0))

    zeros[...] = jnp.zeros_like(zeros)

    def start_clear(slot, carry):
        clear(slot).start()
        return carry

    lax.fori_loop(count, slots, start_clear, 0)

    mask_copy.wait()
    fetch(device).wait()
    blocks[devices] = blocks[device] * mask[...]
    scale = scale_ref[0]

    def visit(partner, slot):
        mine = owned(partner)

        @pl.when(mine)
        def _():
            @pl.when(partner != device)
            def _():
                fetch(partner).wait()

            buffer = lax.rem(slot, BUFFERS)

            @pl.when(slot >= BUFFERS)
            def _():
                put(buffer, slot - BUFFERS).wait()

            left = jnp.where(partner <= device, partner, devices)
            right = jnp.where(partner <= device, devices, partner)
            product = lax.dot_general(
                blocks[left], blocks[right], (((0,), (0,)), ((), ())),
                preferred_element_type=jnp.float32,
            )
            tiles[buffer] = product * scale
            put(buffer, slot).start()

        return slot + mine.astype(jnp.int32)

    lax.fori_loop(0, devices, visit, jnp.int32(0))

    def drain(slot, carry):
        put(lax.rem(slot, BUFFERS), slot).wait()
        return carry

    lax.fori_loop(jnp.maximum(count - BUFFERS, 0), count, drain, 0)

    def end_clear(slot, carry):
        clear(slot).wait()
        return carry

    lax.fori_loop(count, slots, end_clear, 0)


def gathered_form(tokens, slab_lengths, tile_owner, devices, device, slots):
    slab, units = tokens.shape
    rows = slab * devices
    width = units // devices
    x = lax.all_gather(tokens, "col", axis=0, tiled=True)
    x = x.reshape(rows, devices, width).transpose(1, 0, 2)
    scale = 1.0 / jnp.sum(slab_lengths).astype(jnp.float32)
    valid = jnp.arange(slab, dtype=jnp.int32)[None, :] < slab_lengths[:, None]
    mask = jnp.broadcast_to(valid.reshape(rows, 1), (rows, width)).astype(jnp.bfloat16)
    return pl.pallas_call(
        functools.partial(gathered_kernel, devices, slots),
        out_shape=jax.ShapeDtypeStruct((slots, width, width), jnp.float32),
        in_specs=[pl.BlockSpec(memory_space=pltpu.SMEM)] * 3 + [pl.BlockSpec(memory_space=pl.ANY)] * 2,
        out_specs=pl.BlockSpec(memory_space=pl.ANY),
        scratch_shapes=[
            pltpu.VMEM((devices + 1, rows, width), jnp.bfloat16),
            pltpu.VMEM((rows, width), jnp.bfloat16),
            pltpu.VMEM((BUFFERS, width, width), jnp.float32),
            pltpu.VMEM((width, width), jnp.float32),
            pltpu.SemaphoreType.DMA((devices,)),
            pltpu.SemaphoreType.DMA,
            pltpu.SemaphoreType.DMA((BUFFERS,)),
            pltpu.SemaphoreType.DMA((slots,)),
        ],
        compiler_params=pltpu.CompilerParams(vmem_limit_bytes=50 * 1024 * 1024),
    )(tile_owner, device.reshape(1), scale.reshape(1), x, mask)


def ring_plan(devices):
    chips = devices // 2
    order = list(range(0, chips, 2)) + list(range(1, chips, 2))[::-1]
    place = {chip: at for at, chip in enumerate(order)}
    onward = []
    for device in range(devices):
        chip, core = divmod(device, 2)
        step = 1 if core == 0 else -1
        onward.append(order[(place[chip] + step) % chips] * 2 + core)
    backward = [onward.index(device) for device in range(devices)]
    return onward, backward


GROUPS = ((0, 1, 2), (8, 9, 10), (3, 4), (11, 12), (5, 6, 7), (13, 14, 15))
EACH = len(GROUPS) - 2


def ring_gather(tokens, cuts, devices):
    onward, backward = ring_plan(devices)
    sibling = [device ^ 1 for device in range(devices)]
    slab, units = tokens.shape
    width = units // devices

    def send(value, target):
        return lax.ppermute(value, "col", list(enumerate(target)))

    def after(value, *others):
        return lax.optimization_barrier((value, *others))[0]

    def part(value, cut):
        start, stop = cut
        return value.reshape(slab, devices, width)[:, :, start:stop].reshape(slab, -1)

    ahead, back = send(tokens, onward), send(tokens, backward)
    near = jnp.concatenate([tokens, ahead, back], axis=0)
    groups = [near, send(near, sibling)]
    hops = {}
    for cut in cuts:
        ahead_2, back_2 = send(part(ahead, cut), onward), send(part(back, cut), backward)
        ahead_3, back_3 = send(ahead_2, onward), send(back_2, backward)
        ahead_4 = send(after(ahead_3, groups[1]) if cut == cuts[0] else ahead_3, onward)
        hops[cut] = (ahead_2, back_2, ahead_3, back_3, ahead_4)
    two = [jnp.concatenate(hops[cut][:2], axis=0) for cut in cuts]
    two = jnp.concatenate(two, axis=1)
    groups += [two, send(after(two, groups[1]), sibling)]
    by_cut = []
    for cut in cuts:
        three = jnp.concatenate(hops[cut][2:], axis=0)
        by_cut.append([three, send(three, sibling)])
    return groups, by_cut


def slab_origin(devices, device, number):
    chips = devices // 2
    number, flip = number % chips, number // chips
    hops = (number + 1) // 2 if number % 2 else -(number // 2)
    chip, core = device // 2, device % 2
    core = 1 - core if flip else core
    place = jnp.where(chip % 2 == 0, chip // 2, chips - 1 - chip // 2)
    place = (place - (1 - 2 * core) * hops + chips) % chips
    chip = jnp.where(2 * place < chips, 2 * place, 2 * (chips - 1 - place) + 1)
    return 2 * chip + core


def ring_kernel(devices, slots, cuts, known, device_ref, table_ref, *refs):
    whole, both, refs = refs[:2], refs[2:4], refs[4:]
    by_cut = [refs[2 * at:2 * at + 2] for at in range(known + 1)]
    refs = refs[2 * (known + 1):]
    out_ref, pair, tiles, zeros, out_sems, zero_sems = refs[1:] if known else refs
    device = device_ref[0]
    slab, width = pair.shape[1] // devices, pair.shape[2]
    done, end = cuts[known] if known else (0, cuts[0][1])
    pieces = [(done, end, 0, end)] + ([(0, done, done, end)] if known else [])

    def owned(partner):
        return table_ref[devices + tile_number(devices, device, partner)] == device

    def put(buffer, slot, piece, top, bottom):
        _, _, left, right = pieces[piece]
        rows, columns = pl.ds(top, bottom - top), pl.ds(left, right - left)
        return pltpu.make_async_copy(
            tiles.at[buffer, rows, columns], out_ref.at[slot, rows, columns], out_sems.at[buffer, piece]
        )

    def wait_put(buffer, slot):
        for piece, (top, bottom, _, _) in enumerate(pieces):
            put(buffer, slot, piece, top, bottom).wait()

    def clear(slot):
        return pltpu.make_async_copy(zeros, out_ref.at[slot], zero_sems.at[slot])

    def load_block(partner, masked):
        for (start, stop), own_refs in zip(cuts, by_cut):
            size = stop - start
            parts = []
            for at, (numbers, ref) in enumerate(zip(GROUPS, (*whole, *both, *own_refs))):
                if at < len(whole):
                    columns = pl.ds(pl.multiple_of(partner * width + start, 128), size)
                elif at < len(whole) + len(both):
                    columns = pl.ds(pl.multiple_of(devices * start + partner * size, 128), size)
                else:
                    columns = pl.ds(pl.multiple_of(partner * size, 128), size)
                group = ref[:, columns].astype(jnp.float32)
                for row, number in enumerate(numbers):
                    part = group[row * slab:(row + 1) * slab]
                    if masked:
                        place = lax.broadcasted_iota(jnp.int32, (slab, size), 0)
                        part = jnp.where(place < table_ref[slab_origin(devices, device, number)], part, 0.0)
                    parts.append(part)
            pair[0 if masked else 1, :, start:stop] = jnp.concatenate(parts, axis=0).astype(jnp.bfloat16)

    count = lax.fori_loop(
        0, devices, lambda partner, total: total + owned(partner).astype(jnp.int32), jnp.int32(0)
    )

    if not known:

        @pl.when(count < slots)
        def _():
            zeros[...] = jnp.zeros_like(zeros)

        def start_clear(slot, carry):
            clear(slot).start()
            return carry

        lax.fori_loop(count, slots, start_clear, 0)

    load_block(device, True)
    valid_count = lax.fori_loop(0, devices, lambda at, total: total + table_ref[at], jnp.int32(0))
    scale = 1.0 / jnp.full((128, width), valid_count.astype(jnp.float32))

    def visit(partner, slot):
        mine = owned(partner)

        @pl.when(mine)
        def _():
            buffer = lax.rem(slot, BUFFERS)
            load_block(partner, False)

            @pl.when(slot >= BUFFERS)
            def _():
                wait_put(buffer, slot - BUFFERS)

            lower = (partner <= device).astype(jnp.int32)
            for piece, (top, bottom, left, right) in enumerate(pieces):
                for row in range(top, bottom, 128):
                    product = lax.dot_general(
                        pair[lower, :, row:row + 128], pair[1 - lower, :, left:right],
                        (((0,), (0,)), ((), ())), preferred_element_type=jnp.float32,
                    )
                    tiles[buffer, row:row + 128, left:right] = product * scale[:, left:right]
                    put(buffer, slot, piece, row, row + 128).start()

        return slot + mine.astype(jnp.int32)

    lax.fori_loop(0, devices, visit, jnp.int32(0))

    def drain(slot, carry):
        wait_put(lax.rem(slot, BUFFERS), slot)
        return carry

    lax.fori_loop(jnp.maximum(count - BUFFERS, 0), count, drain, 0)

    if not known:

        def end_clear(slot, carry):
            clear(slot).wait()
            return carry

        lax.fori_loop(count, slots, end_clear, 0)


def ring_form(tokens, slab_lengths, tile_owner, devices, device, slots):
    slab, units = tokens.shape
    width = units // devices
    first = -(-width // 256) * 128
    cuts = [(0, first), (first, width)]
    whole, by_cut = ring_gather(tokens, cuts, devices)
    table = jnp.concatenate([slab_lengths, tile_owner])
    result = None
    for known in range(len(cuts)):
        groups = whole + sum(by_cut[:known + 1], [])
        made = cuts[known][1] ** 2 - (cuts[known][0] ** 2 if known else 0)
        result = pl.pallas_call(
            functools.partial(ring_kernel, devices, slots, cuts, known),
            out_shape=jax.ShapeDtypeStruct((slots, width, width), jnp.float32),
            in_specs=[pl.BlockSpec(memory_space=pltpu.SMEM)] * 2
            + [pl.BlockSpec(memory_space=pltpu.VMEM)] * len(groups)
            + [pl.BlockSpec(memory_space=pl.ANY)] * (known > 0),
            out_specs=pl.BlockSpec(memory_space=pl.ANY),
            input_output_aliases={2 + len(groups): 0} if known else {},
            scratch_shapes=[
                pltpu.VMEM((2, slab * devices, width), jnp.bfloat16),
                pltpu.VMEM((BUFFERS, width, width), jnp.float32),
                pltpu.VMEM((width, width), jnp.float32),
                pltpu.SemaphoreType.DMA((BUFFERS, 2)),
                pltpu.SemaphoreType.DMA((slots,)),
            ],
            compiler_params=pltpu.CompilerParams(vmem_limit_bytes=32 * 1024 * 1024),
            cost_estimate=pl.CostEstimate(
                flops=2 * slots * slab * devices * made,
                bytes_accessed=4 * slots * made,
                transcendentals=0,
            ),
        )(device.reshape(1), table, *groups, *([result] if known else []))
    return result


def per_device(tokens, slab_lengths, tile_owner):
    devices = lax.axis_size("col")
    device = lax.axis_index("col").astype(jnp.int32)
    slots = devices // 2 + devices // 8 + 1
    width = tokens.shape[1] // devices
    form = ring_form if devices == RING_DEVICES and width % 128 == 0 and width > 128 else gathered_form
    return form(tokens, slab_lengths, tile_owner, devices, device, slots)


def solution(mesh):
    return jax.shard_map(
        per_device,
        mesh=mesh,
        in_specs=(P(("grp", "col"), None), P("grp"), P()),
        out_specs=P(("grp", "col"), None, None),
        check_vma=False,
    )
```

```python
import functools

import jax
import jax.numpy as jnp
from jax import lax
from jax.experimental import pallas as pl
from jax.experimental.pallas import tpu as pltpu
from jax.sharding import PartitionSpec as P

BUFFERS = 4
RING_DEVICES = 16


def tile_number(devices, device, partner):
    low = jnp.minimum(device, partner)
    high = jnp.maximum(device, partner)
    return low * devices - low * (low - 1) // 2 + (high - low)


def gathered_kernel(
    devices, slots, owner_ref, device_ref, scale_ref, x_ref, mask_ref,
    out_ref, blocks, mask, tiles, zeros, in_sems, mask_sem, out_sems, zero_sems,
):
    device = device_ref[0]
    width = blocks.shape[2]

    def owned(partner):
        return owner_ref[tile_number(devices, device, partner)] == device

    def fetch(partner):
        return pltpu.make_async_copy(x_ref.at[partner], blocks.at[partner], in_sems.at[partner])

    def put(buffer, slot):
        return pltpu.make_async_copy(tiles.at[buffer], out_ref.at[slot], out_sems.at[buffer])

    def clear(slot):
        return pltpu.make_async_copy(zeros, out_ref.at[slot], zero_sems.at[slot])

    mask_copy = pltpu.make_async_copy(mask_ref, mask, mask_sem)
    mask_copy.start()
    fetch(device).start()

    def start_fetch(partner, count):
        mine = owned(partner)

        @pl.when(mine & (partner != device))
        def _():
            fetch(partner).start()

        return count + mine.astype(jnp.int32)

    count = lax.fori_loop(0, devices, start_fetch, jnp.int32(0))

    zeros[...] = jnp.zeros_like(zeros)

    def start_clear(slot, carry):
        clear(slot).start()
        return carry

    lax.fori_loop(count, slots, start_clear, 0)

    mask_copy.wait()
    fetch(device).wait()
    blocks[devices] = blocks[device] * mask[...]
    scale = scale_ref[0]

    def visit(partner, slot):
        mine = owned(partner)

        @pl.when(mine)
        def _():
            @pl.when(partner != device)
            def _():
                fetch(partner).wait()

            buffer = lax.rem(slot, BUFFERS)

            @pl.when(slot >= BUFFERS)
            def _():
                put(buffer, slot - BUFFERS).wait()

            left = jnp.where(partner <= device, partner, devices)
            right = jnp.where(partner <= device, devices, partner)
            product = lax.dot_general(
                blocks[left], blocks[right], (((0,), (0,)), ((), ())),
                preferred_element_type=jnp.float32,
            )
            tiles[buffer] = product * scale
            put(buffer, slot).start()

        return slot + mine.astype(jnp.int32)

    lax.fori_loop(0, devices, visit, jnp.int32(0))

    def drain(slot, carry):
        put(lax.rem(slot, BUFFERS), slot).wait()
        return carry

    lax.fori_loop(jnp.maximum(count - BUFFERS, 0), count, drain, 0)

    def end_clear(slot, carry):
        clear(slot).wait()
        return carry

    lax.fori_loop(count, slots, end_clear, 0)


def gathered_form(tokens, slab_lengths, tile_owner, devices, device, slots):
    slab, units = tokens.shape
    rows = slab * devices
    width = units // devices
    x = lax.all_gather(tokens, "col", axis=0, tiled=True)
    x = x.reshape(rows, devices, width).transpose(1, 0, 2)
    scale = 1.0 / jnp.sum(slab_lengths).astype(jnp.float32)
    valid = jnp.arange(slab, dtype=jnp.int32)[None, :] < slab_lengths[:, None]
    mask = jnp.broadcast_to(valid.reshape(rows, 1), (rows, width)).astype(jnp.bfloat16)
    return pl.pallas_call(
        functools.partial(gathered_kernel, devices, slots),
        out_shape=jax.ShapeDtypeStruct((slots, width, width), jnp.float32),
        in_specs=[pl.BlockSpec(memory_space=pltpu.SMEM)] * 3 + [pl.BlockSpec(memory_space=pl.ANY)] * 2,
        out_specs=pl.BlockSpec(memory_space=pl.ANY),
        scratch_shapes=[
            pltpu.VMEM((devices + 1, rows, width), jnp.bfloat16),
            pltpu.VMEM((rows, width), jnp.bfloat16),
            pltpu.VMEM((BUFFERS, width, width), jnp.float32),
            pltpu.VMEM((width, width), jnp.float32),
            pltpu.SemaphoreType.DMA((devices,)),
            pltpu.SemaphoreType.DMA,
            pltpu.SemaphoreType.DMA((BUFFERS,)),
            pltpu.SemaphoreType.DMA((slots,)),
        ],
        compiler_params=pltpu.CompilerParams(vmem_limit_bytes=50 * 1024 * 1024),
    )(tile_owner, device.reshape(1), scale.reshape(1), x, mask)


def ring_plan(devices):
    chips = devices // 2
    order = list(range(0, chips, 2)) + list(range(1, chips, 2))[::-1]
    place = {chip: at for at, chip in enumerate(order)}
    onward = []
    for device in range(devices):
        chip, core = divmod(device, 2)
        step = 1 if core == 0 else -1
        onward.append(order[(place[chip] + step) % chips] * 2 + core)
    backward = [onward.index(device) for device in range(devices)]
    return onward, backward


GROUPS = ((0, 1, 2), (8, 9, 10), (3, 4, 7), (11, 12, 15), (5, 6), (13, 14))


def ring_gather(tokens, device, devices):
    onward, backward = ring_plan(devices)
    sibling = [device ^ 1 for device in range(devices)]
    across = [device ^ 2 for device in range(devices)]
    mirror = [(at, at ^ 12) for at in range(devices) if at // 4 in (0, 3)]

    def send(value, target):
        return lax.ppermute(value, "col", list(enumerate(target)))

    def after(value, *others):
        return lax.optimization_barrier((value, *others))[0]

    ahead, back = [tokens], [tokens]
    for _ in range(2):
        ahead.append(send(ahead[-1], onward))
        back.append(send(back[-1], backward))
    far = lax.ppermute(tokens, "col", mirror)
    chip, core = device // 2, device % 2
    at_end = (chip < 2) | (chip >= devices // 2 - 2)
    came_ahead = (((chip == 3) | (chip == 4)) == (core == 0)) & ~at_end
    held = jnp.where(at_end, far, jnp.where(came_ahead, ahead[1], back[1]))
    half = send(held, across)
    ahead.append(send(after(ahead[2], back[2]), onward))
    back.append(send(after(back[2], ahead[2]), backward))
    groups = []
    for group, others in (
        ((tokens, ahead[1], back[1]), (ahead[2], back[2])), ((ahead[2], back[2], half), (ahead[2], back[2])), ((ahead[3], back[3]), ()),
    ):
        group = jnp.concatenate(group, axis=0)
        groups += [group, send(after(group, *others) if others else group, sibling)]
    return groups

def slab_origin(devices, device, number):
    chips = devices // 2
    number, flip = number % chips, number // chips
    hops = (number + 1) // 2 if number % 2 else -(number // 2)
    chip, core = device // 2, device % 2
    core = 1 - core if flip else core
    place = jnp.where(chip % 2 == 0, chip // 2, chips - 1 - chip // 2)
    place = (place - (1 - 2 * core) * hops + chips) % chips
    chip = jnp.where(2 * place < chips, 2 * place, 2 * (chips - 1 - place) + 1)
    return 2 * chip + core


def ring_kernel(devices, slots, device_ref, table_ref, *refs):
    groups = refs[:len(GROUPS)]
    out_ref, pair, tiles, zeros, out_sems, zero_sems = refs[len(GROUPS):]
    device = device_ref[0]
    slab, width = pair.shape[1] // devices, pair.shape[2]

    def owned(partner):
        return table_ref[devices + tile_number(devices, device, partner)] == device

    def put(buffer, slot):
        return pltpu.make_async_copy(tiles.at[buffer], out_ref.at[slot], out_sems.at[buffer])

    def clear(slot):
        return pltpu.make_async_copy(zeros, out_ref.at[slot], zero_sems.at[slot])

    def load_block(partner, masked):
        columns = pl.ds(pl.multiple_of(partner * width, 128), width)
        parts = []
        for numbers, ref in zip(GROUPS, groups):
            group = ref[:, columns].astype(jnp.float32)
            for at, number in enumerate(numbers):
                part = group[at * slab:(at + 1) * slab]
                if masked:
                    row = lax.broadcasted_iota(jnp.int32, (slab, width), 0)
                    part = jnp.where(row < table_ref[slab_origin(devices, device, number)], part, 0.0)
                parts.append(part)
        pair[0 if masked else 1] = jnp.concatenate(parts, axis=0).astype(jnp.bfloat16)

    count = lax.fori_loop(
        0, devices, lambda partner, total: total + owned(partner).astype(jnp.int32), jnp.int32(0)
    )

    @pl.when(count < slots)
    def _():
        zeros[...] = jnp.zeros_like(zeros)

    def start_clear(slot, carry):
        clear(slot).start()
        return carry

    lax.fori_loop(count, slots, start_clear, 0)

    load_block(device, True)
    valid_count = lax.fori_loop(0, devices, lambda at, total: total + table_ref[at], jnp.int32(0))
    scale = 1.0 / jnp.full((128, width), valid_count.astype(jnp.float32))

    def visit(partner, slot):
        mine = owned(partner)

        @pl.when(mine)
        def _():
            buffer = lax.rem(slot, BUFFERS)
            load_block(partner, False)

            @pl.when(slot >= BUFFERS)
            def _():
                put(buffer, slot - BUFFERS).wait()

            left = (partner <= device).astype(jnp.int32)
            for row in range(0, width, 128):
                strip = pl.ds(row, 128)
                product = lax.dot_general(
                    pair[left, :, row:row + 128], pair[1 - left], (((0,), (0,)), ((), ())),
                    preferred_element_type=jnp.float32,
                )
                tiles[buffer, strip, :] = product * scale
                pltpu.make_async_copy(
                    tiles.at[buffer, strip], out_ref.at[slot, strip], out_sems.at[buffer]
                ).start()

        return slot + mine.astype(jnp.int32)

    lax.fori_loop(0, devices, visit, jnp.int32(0))

    def drain(slot, carry):
        put(lax.rem(slot, BUFFERS), slot).wait()
        return carry

    lax.fori_loop(jnp.maximum(count - BUFFERS, 0), count, drain, 0)

    def end_clear(slot, carry):
        clear(slot).wait()
        return carry

    lax.fori_loop(count, slots, end_clear, 0)


def ring_form(tokens, slab_lengths, tile_owner, devices, device, slots):
    slab, units = tokens.shape
    width = units // devices
    groups = ring_gather(tokens, device, devices)
    table = jnp.concatenate([slab_lengths, tile_owner])
    return pl.pallas_call(
        functools.partial(ring_kernel, devices, slots),
        out_shape=jax.ShapeDtypeStruct((slots, width, width), jnp.float32),
        in_specs=[pl.BlockSpec(memory_space=pltpu.SMEM)] * 2
        + [pl.BlockSpec(memory_space=pltpu.VMEM)] * len(groups),
        out_specs=pl.BlockSpec(memory_space=pl.ANY),
        scratch_shapes=[
            pltpu.VMEM((2, slab * devices, width), jnp.bfloat16),
            pltpu.VMEM((BUFFERS, width, width), jnp.float32),
            pltpu.VMEM((width, width), jnp.float32),
            pltpu.SemaphoreType.DMA((BUFFERS,)),
            pltpu.SemaphoreType.DMA((slots,)),
        ],
        compiler_params=pltpu.CompilerParams(vmem_limit_bytes=32 * 1024 * 1024),
        cost_estimate=pl.CostEstimate(
            flops=2 * slots * slab * devices * width * width,
            bytes_accessed=4 * slots * width * width,
            transcendentals=0,
        ),
    )(device.reshape(1), table, *groups)


def per_device(tokens, slab_lengths, tile_owner):
    devices = lax.axis_size("col")
    device = lax.axis_index("col").astype(jnp.int32)
    slots = devices // 2 + devices // 8 + 1
    width = tokens.shape[1] // devices
    form = ring_form if devices == RING_DEVICES and width % 128 == 0 else gathered_form
    return form(tokens, slab_lengths, tile_owner, devices, device, slots)


def solution(mesh):
    return jax.shard_map(
        per_device,
        mesh=mesh,
        in_specs=(P(("grp", "col"), None), P("grp"), P()),
        out_specs=P(("grp", "col"), None, None),
        check_vma=False,
    )
```

```python
import functools

import jax
import jax.numpy as jnp
from jax import lax
from jax.experimental import pallas as pl
from jax.experimental.pallas import tpu as pltpu
from jax.sharding import PartitionSpec as P

BUFFERS = 4
RING_DEVICES = 16


def tile_number(devices, device, partner):
    low = jnp.minimum(device, partner)
    high = jnp.maximum(device, partner)
    return low * devices - low * (low - 1) // 2 + (high - low)


def gathered_kernel(
    devices, slots, owner_ref, device_ref, scale_ref, x_ref, mask_ref,
    out_ref, blocks, mask, tiles, zeros, in_sems, mask_sem, out_sems, zero_sems,
):
    device = device_ref[0]
    width = blocks.shape[2]

    def owned(partner):
        return owner_ref[tile_number(devices, device, partner)] == device

    def fetch(partner):
        return pltpu.make_async_copy(x_ref.at[partner], blocks.at[partner], in_sems.at[partner])

    def put(buffer, slot):
        return pltpu.make_async_copy(tiles.at[buffer], out_ref.at[slot], out_sems.at[buffer])

    def clear(slot):
        return pltpu.make_async_copy(zeros, out_ref.at[slot], zero_sems.at[slot])

    mask_copy = pltpu.make_async_copy(mask_ref, mask, mask_sem)
    mask_copy.start()
    fetch(device).start()

    def start_fetch(partner, count):
        mine = owned(partner)

        @pl.when(mine & (partner != device))
        def _():
            fetch(partner).start()

        return count + mine.astype(jnp.int32)

    count = lax.fori_loop(0, devices, start_fetch, jnp.int32(0))

    zeros[...] = jnp.zeros_like(zeros)

    def start_clear(slot, carry):
        clear(slot).start()
        return carry

    lax.fori_loop(count, slots, start_clear, 0)

    mask_copy.wait()
    fetch(device).wait()
    blocks[devices] = blocks[device] * mask[...]
    scale = scale_ref[0]

    def visit(partner, slot):
        mine = owned(partner)

        @pl.when(mine)
        def _():
            @pl.when(partner != device)
            def _():
                fetch(partner).wait()

            buffer = lax.rem(slot, BUFFERS)

            @pl.when(slot >= BUFFERS)
            def _():
                put(buffer, slot - BUFFERS).wait()

            left = jnp.where(partner <= device, partner, devices)
            right = jnp.where(partner <= device, devices, partner)
            product = lax.dot_general(
                blocks[left], blocks[right], (((0,), (0,)), ((), ())),
                preferred_element_type=jnp.float32,
            )
            tiles[buffer] = product * scale
            put(buffer, slot).start()

        return slot + mine.astype(jnp.int32)

    lax.fori_loop(0, devices, visit, jnp.int32(0))

    def drain(slot, carry):
        put(lax.rem(slot, BUFFERS), slot).wait()
        return carry

    lax.fori_loop(jnp.maximum(count - BUFFERS, 0), count, drain, 0)

    def end_clear(slot, carry):
        clear(slot).wait()
        return carry

    lax.fori_loop(count, slots, end_clear, 0)


def gathered_form(tokens, slab_lengths, tile_owner, devices, device, slots):
    slab, units = tokens.shape
    rows = slab * devices
    width = units // devices
    x = lax.all_gather(tokens, "col", axis=0, tiled=True)
    x = x.reshape(rows, devices, width).transpose(1, 0, 2)
    scale = 1.0 / jnp.sum(slab_lengths).astype(jnp.float32)
    valid = jnp.arange(slab, dtype=jnp.int32)[None, :] < slab_lengths[:, None]
    mask = jnp.broadcast_to(valid.reshape(rows, 1), (rows, width)).astype(jnp.bfloat16)
    return pl.pallas_call(
        functools.partial(gathered_kernel, devices, slots),
        out_shape=jax.ShapeDtypeStruct((slots, width, width), jnp.float32),
        in_specs=[pl.BlockSpec(memory_space=pltpu.SMEM)] * 3 + [pl.BlockSpec(memory_space=pl.ANY)] * 2,
        out_specs=pl.BlockSpec(memory_space=pl.ANY),
        scratch_shapes=[
            pltpu.VMEM((devices + 1, rows, width), jnp.bfloat16),
            pltpu.VMEM((rows, width), jnp.bfloat16),
            pltpu.VMEM((BUFFERS, width, width), jnp.float32),
            pltpu.VMEM((width, width), jnp.float32),
            pltpu.SemaphoreType.DMA((devices,)),
            pltpu.SemaphoreType.DMA,
            pltpu.SemaphoreType.DMA((BUFFERS,)),
            pltpu.SemaphoreType.DMA((slots,)),
        ],
        compiler_params=pltpu.CompilerParams(vmem_limit_bytes=50 * 1024 * 1024),
    )(tile_owner, device.reshape(1), scale.reshape(1), x, mask)


def ring_plan(devices):
    chips = devices // 2
    order = list(range(0, chips, 2)) + list(range(1, chips, 2))[::-1]
    place = {chip: at for at, chip in enumerate(order)}
    onward = []
    for device in range(devices):
        chip, core = divmod(device, 2)
        step = 1 if core == 0 else -1
        onward.append(order[(place[chip] + step) % chips] * 2 + core)
    backward = [onward.index(device) for device in range(devices)]
    return onward, backward


GROUPS = ((0, 1, 2), (8, 9, 10), (3, 4, 7), (11, 12, 15), (5, 6), (13, 14))


def ring_gather(tokens, device, devices):
    onward, backward = ring_plan(devices)
    sibling = [device ^ 1 for device in range(devices)]
    across = [device ^ 2 for device in range(devices)]
    mirror = [(at, at ^ 12) for at in range(devices) if at // 4 in (0, 3)]

    def send(value, target):
        return lax.ppermute(value, "col", list(enumerate(target)))

    def after(value, *others):
        return lax.optimization_barrier((value, *others))[0]

    ahead, back = [tokens], [tokens]
    for _ in range(2):
        ahead.append(send(ahead[-1], onward))
        back.append(send(back[-1], backward))
    far = lax.ppermute(tokens, "col", mirror)
    chip, core = device // 2, device % 2
    at_end = (chip < 2) | (chip >= devices // 2 - 2)
    came_ahead = (((chip == 3) | (chip == 4)) == (core == 0)) & ~at_end
    held = jnp.where(at_end, far, jnp.where(came_ahead, ahead[1], back[1]))
    half = send(held, across)
    ahead.append(send(after(ahead[2], back[2]), onward))
    back.append(send(after(back[2], ahead[2]), backward))
    groups = []
    for group, others in (
        ((tokens, ahead[1], back[1]), (ahead[2], back[2])), ((ahead[2], back[2], half), (ahead[2], back[2])), ((ahead[3], back[3]), ()),
    ):
        group = jnp.concatenate(group, axis=0)
        groups += [group, send(after(group, *others) if others else group, sibling)]
    return groups

def slab_origin(devices, device, number):
    chips = devices // 2
    number, flip = number % chips, number // chips
    hops = (number + 1) // 2 if number % 2 else -(number // 2)
    chip, core = device // 2, device % 2
    core = 1 - core if flip else core
    place = jnp.where(chip % 2 == 0, chip // 2, chips - 1 - chip // 2)
    place = (place - (1 - 2 * core) * hops + chips) % chips
    chip = jnp.where(2 * place < chips, 2 * place, 2 * (chips - 1 - place) + 1)
    return 2 * chip + core


def ring_kernel(devices, slots, device_ref, table_ref, *refs):
    groups = refs[:len(GROUPS)]
    out_ref, pair, tiles, zeros, out_sems, zero_sems = refs[len(GROUPS):]
    device = device_ref[0]
    slab, width = pair.shape[1] // devices, pair.shape[2]

    def owned(partner):
        return table_ref[devices + tile_number(devices, device, partner)] == device

    def put(buffer, slot):
        return pltpu.make_async_copy(tiles.at[buffer], out_ref.at[slot], out_sems.at[buffer])

    def clear(slot):
        return pltpu.make_async_copy(zeros, out_ref.at[slot], zero_sems.at[slot])

    def load_block(partner, masked):
        columns = pl.ds(pl.multiple_of(partner * width, 128), width)
        parts = []
        for numbers, ref in zip(GROUPS, groups):
            group = ref[:, columns].astype(jnp.float32)
            for at, number in enumerate(numbers):
                part = group[at * slab:(at + 1) * slab]
                if masked:
                    row = lax.broadcasted_iota(jnp.int32, (slab, width), 0)
                    part = jnp.where(row < table_ref[slab_origin(devices, device, number)], part, 0.0)
                parts.append(part)
        pair[0 if masked else 1] = jnp.concatenate(parts, axis=0).astype(jnp.bfloat16)

    count = lax.fori_loop(
        0, devices, lambda partner, total: total + owned(partner).astype(jnp.int32), jnp.int32(0)
    )

    @pl.when(count < slots)
    def _():
        zeros[...] = jnp.zeros_like(zeros)

    def start_clear(slot, carry):
        clear(slot).start()
        return carry

    lax.fori_loop(count, slots, start_clear, 0)

    load_block(device, True)
    valid_count = lax.fori_loop(0, devices, lambda at, total: total + table_ref[at], jnp.int32(0))
    scale = 1.0 / jnp.full((128, width), valid_count.astype(jnp.float32))

    def visit(partner, slot):
        mine = owned(partner)

        @pl.when(mine)
        def _():
            buffer = lax.rem(slot, BUFFERS)
            load_block(partner, False)

            @pl.when(slot >= BUFFERS)
            def _():
                put(buffer, slot - BUFFERS).wait()

            left = (partner <= device).astype(jnp.int32)
            for row in range(0, width, 128):
                strip = pl.ds(row, 128)
                product = lax.dot_general(
                    pair[left, :, row:row + 128], pair[1 - left], (((0,), (0,)), ((), ())),
                    preferred_element_type=jnp.float32,
                )
                tiles[buffer, strip, :] = product * scale
                pltpu.make_async_copy(
                    tiles.at[buffer, strip], out_ref.at[slot, strip], out_sems.at[buffer]
                ).start(priority=row // 128 % 2)

        return slot + mine.astype(jnp.int32)

    lax.fori_loop(0, devices, visit, jnp.int32(0))

    def drain(slot, carry):
        put(lax.rem(slot, BUFFERS), slot).wait()
        return carry

    lax.fori_loop(jnp.maximum(count - BUFFERS, 0), count, drain, 0)

    def end_clear(slot, carry):
        clear(slot).wait()
        return carry

    lax.fori_loop(count, slots, end_clear, 0)


def ring_form(tokens, slab_lengths, tile_owner, devices, device, slots):
    slab, units = tokens.shape
    width = units // devices
    groups = ring_gather(tokens, device, devices)
    table = jnp.concatenate([slab_lengths, tile_owner])
    return pl.pallas_call(
        functools.partial(ring_kernel, devices, slots),
        out_shape=jax.ShapeDtypeStruct((slots, width, width), jnp.float32),
        in_specs=[pl.BlockSpec(memory_space=pltpu.SMEM)] * 2
        + [pl.BlockSpec(memory_space=pltpu.VMEM)] * len(groups),
        out_specs=pl.BlockSpec(memory_space=pl.ANY),
        scratch_shapes=[
            pltpu.VMEM((2, slab * devices, width), jnp.bfloat16),
            pltpu.VMEM((BUFFERS, width, width), jnp.float32),
            pltpu.VMEM((width, width), jnp.float32),
            pltpu.SemaphoreType.DMA((BUFFERS,)),
            pltpu.SemaphoreType.DMA((slots,)),
        ],
        compiler_params=pltpu.CompilerParams(vmem_limit_bytes=32 * 1024 * 1024),
        cost_estimate=pl.CostEstimate(
            flops=2 * slots * slab * devices * width * width,
            bytes_accessed=4 * slots * width * width,
            transcendentals=0,
        ),
    )(device.reshape(1), table, *groups)


def per_device(tokens, slab_lengths, tile_owner):
    devices = lax.axis_size("col")
    device = lax.axis_index("col").astype(jnp.int32)
    slots = devices // 2 + devices // 8 + 1
    width = tokens.shape[1] // devices
    form = ring_form if devices == RING_DEVICES and width % 128 == 0 else gathered_form
    return form(tokens, slab_lengths, tile_owner, devices, device, slots)


def solution(mesh):
    return jax.shard_map(
        per_device,
        mesh=mesh,
        in_specs=(P(("grp", "col"), None), P("grp"), P()),
        out_specs=P(("grp", "col"), None, None),
        check_vma=False,
    )
```

```python
import functools

import jax
import jax.numpy as jnp
from jax import lax
from jax.experimental import pallas as pl
from jax.experimental.pallas import tpu as pltpu
from jax.sharding import PartitionSpec as P

BUFFERS = 4
RING_DEVICES = 16


def tile_number(devices, device, partner):
    low = jnp.minimum(device, partner)
    high = jnp.maximum(device, partner)
    return low * devices - low * (low - 1) // 2 + (high - low)


def gathered_kernel(
    devices, slots, owner_ref, device_ref, scale_ref, x_ref, mask_ref,
    out_ref, blocks, mask, tiles, zeros, in_sems, mask_sem, out_sems, zero_sems,
):
    device = device_ref[0]
    width = blocks.shape[2]

    def owned(partner):
        return owner_ref[tile_number(devices, device, partner)] == device

    def fetch(partner):
        return pltpu.make_async_copy(x_ref.at[partner], blocks.at[partner], in_sems.at[partner])

    def put(buffer, slot):
        return pltpu.make_async_copy(tiles.at[buffer], out_ref.at[slot], out_sems.at[buffer])

    def clear(slot):
        return pltpu.make_async_copy(zeros, out_ref.at[slot], zero_sems.at[slot])

    mask_copy = pltpu.make_async_copy(mask_ref, mask, mask_sem)
    mask_copy.start()
    fetch(device).start()

    def start_fetch(partner, count):
        mine = owned(partner)

        @pl.when(mine & (partner != device))
        def _():
            fetch(partner).start()

        return count + mine.astype(jnp.int32)

    count = lax.fori_loop(0, devices, start_fetch, jnp.int32(0))

    zeros[...] = jnp.zeros_like(zeros)

    def start_clear(slot, carry):
        clear(slot).start()
        return carry

    lax.fori_loop(count, slots, start_clear, 0)

    mask_copy.wait()
    fetch(device).wait()
    blocks[devices] = blocks[device] * mask[...]
    scale = scale_ref[0]

    def visit(partner, slot):
        mine = owned(partner)

        @pl.when(mine)
        def _():
            @pl.when(partner != device)
            def _():
                fetch(partner).wait()

            buffer = lax.rem(slot, BUFFERS)

            @pl.when(slot >= BUFFERS)
            def _():
                put(buffer, slot - BUFFERS).wait()

            left = jnp.where(partner <= device, partner, devices)
            right = jnp.where(partner <= device, devices, partner)
            product = lax.dot_general(
                blocks[left], blocks[right], (((0,), (0,)), ((), ())),
                preferred_element_type=jnp.float32,
            )
            tiles[buffer] = product * scale
            put(buffer, slot).start()

        return slot + mine.astype(jnp.int32)

    lax.fori_loop(0, devices, visit, jnp.int32(0))

    def drain(slot, carry):
        put(lax.rem(slot, BUFFERS), slot).wait()
        return carry

    lax.fori_loop(jnp.maximum(count - BUFFERS, 0), count, drain, 0)

    def end_clear(slot, carry):
        clear(slot).wait()
        return carry

    lax.fori_loop(count, slots, end_clear, 0)


def gathered_form(tokens, slab_lengths, tile_owner, devices, device, slots):
    slab, units = tokens.shape
    rows = slab * devices
    width = units // devices
    x = lax.all_gather(tokens, "col", axis=0, tiled=True)
    x = x.reshape(rows, devices, width).transpose(1, 0, 2)
    scale = 1.0 / jnp.sum(slab_lengths).astype(jnp.float32)
    valid = jnp.arange(slab, dtype=jnp.int32)[None, :] < slab_lengths[:, None]
    mask = jnp.broadcast_to(valid.reshape(rows, 1), (rows, width)).astype(jnp.bfloat16)
    return pl.pallas_call(
        functools.partial(gathered_kernel, devices, slots),
        out_shape=jax.ShapeDtypeStruct((slots, width, width), jnp.float32),
        in_specs=[pl.BlockSpec(memory_space=pltpu.SMEM)] * 3 + [pl.BlockSpec(memory_space=pl.ANY)] * 2,
        out_specs=pl.BlockSpec(memory_space=pl.ANY),
        scratch_shapes=[
            pltpu.VMEM((devices + 1, rows, width), jnp.bfloat16),
            pltpu.VMEM((rows, width), jnp.bfloat16),
            pltpu.VMEM((BUFFERS, width, width), jnp.float32),
            pltpu.VMEM((width, width), jnp.float32),
            pltpu.SemaphoreType.DMA((devices,)),
            pltpu.SemaphoreType.DMA,
            pltpu.SemaphoreType.DMA((BUFFERS,)),
            pltpu.SemaphoreType.DMA((slots,)),
        ],
        compiler_params=pltpu.CompilerParams(vmem_limit_bytes=50 * 1024 * 1024),
    )(tile_owner, device.reshape(1), scale.reshape(1), x, mask)


def ring_plan(devices):
    chips = devices // 2
    order = list(range(0, chips, 2)) + list(range(1, chips, 2))[::-1]
    place = {chip: at for at, chip in enumerate(order)}
    onward = []
    for device in range(devices):
        chip, core = divmod(device, 2)
        step = 1 if core == 0 else -1
        onward.append(order[(place[chip] + step) % chips] * 2 + core)
    backward = [onward.index(device) for device in range(devices)]
    return onward, backward


GROUPS = ((0, 1, 2), (8, 9, 10), (3, 4), (11, 12), (5, 6), (13, 14), (7,), (15,))


def ring_gather(tokens, devices):
    onward, backward = ring_plan(devices)
    sibling = [device ^ 1 for device in range(devices)]
    middle = tokens.shape[1] // 2

    def send(value, target):
        return lax.ppermute(value, "col", list(enumerate(target)))

    def after(value, *others):
        return lax.optimization_barrier((value, *others))[0]

    def joined(*values_by_half):
        return jnp.concatenate([jnp.concatenate(values, axis=1) for values in values_by_half], axis=0)

    ahead, back = send(tokens, onward), send(tokens, backward)
    near = jnp.concatenate([tokens, ahead, back], axis=0)
    beside = send(near, sibling)
    hops = []
    for columns in (slice(0, middle), slice(middle, None)):
        ahead_2, back_2 = send(ahead[:, columns], onward), send(back[:, columns], backward)
        ahead_3, back_3 = send(ahead_2, onward), send(back_2, backward)
        ahead_3 = ahead_3 if columns.start else after(ahead_3, beside)
        ahead_4 = send(ahead_3, onward)
        hops.append((ahead_2, back_2, ahead_3, back_3, ahead_4))
    ahead_2, back_2, ahead_3, back_3, ahead_4 = zip(*hops)
    two, three, four = joined(ahead_2, back_2), joined(ahead_3, back_3), joined(ahead_4)
    return [
        near, beside, two, send(after(two, beside), sibling), three, send(three, sibling),
        four, send(four, sibling),
    ]

def slab_origin(devices, device, number):
    chips = devices // 2
    number, flip = number % chips, number // chips
    hops = (number + 1) // 2 if number % 2 else -(number // 2)
    chip, core = device // 2, device % 2
    core = 1 - core if flip else core
    place = jnp.where(chip % 2 == 0, chip // 2, chips - 1 - chip // 2)
    place = (place - (1 - 2 * core) * hops + chips) % chips
    chip = jnp.where(2 * place < chips, 2 * place, 2 * (chips - 1 - place) + 1)
    return 2 * chip + core


def ring_kernel(devices, slots, device_ref, table_ref, *refs):
    groups = refs[:len(GROUPS)]
    out_ref, pair, tiles, zeros, out_sems, zero_sems = refs[len(GROUPS):]
    device = device_ref[0]
    slab, width = pair.shape[1] // devices, pair.shape[2]

    def owned(partner):
        return table_ref[devices + tile_number(devices, device, partner)] == device

    def put(buffer, slot):
        return pltpu.make_async_copy(tiles.at[buffer], out_ref.at[slot], out_sems.at[buffer])

    def clear(slot):
        return pltpu.make_async_copy(zeros, out_ref.at[slot], zero_sems.at[slot])

    def load_block(partner, masked):
        columns = pl.ds(pl.multiple_of(partner * width, 128), width)
        parts = []
        for numbers, ref in zip(GROUPS, groups):
            group = ref[:, columns].astype(jnp.float32)
            for at, number in enumerate(numbers):
                part = group[at * slab:(at + 1) * slab]
                if masked:
                    row = lax.broadcasted_iota(jnp.int32, (slab, width), 0)
                    part = jnp.where(row < table_ref[slab_origin(devices, device, number)], part, 0.0)
                parts.append(part)
        pair[0 if masked else 1] = jnp.concatenate(parts, axis=0).astype(jnp.bfloat16)

    count = lax.fori_loop(
        0, devices, lambda partner, total: total + owned(partner).astype(jnp.int32), jnp.int32(0)
    )

    @pl.when(count < slots)
    def _():
        zeros[...] = jnp.zeros_like(zeros)

    def start_clear(slot, carry):
        clear(slot).start()
        return carry

    lax.fori_loop(count, slots, start_clear, 0)

    load_block(device, True)
    valid_count = lax.fori_loop(0, devices, lambda at, total: total + table_ref[at], jnp.int32(0))
    scale = 1.0 / jnp.full((128, width), valid_count.astype(jnp.float32))

    def visit(partner, slot):
        mine = owned(partner)

        @pl.when(mine)
        def _():
            buffer = lax.rem(slot, BUFFERS)
            load_block(partner, False)

            @pl.when(slot >= BUFFERS)
            def _():
                put(buffer, slot - BUFFERS).wait()

            left = (partner <= device).astype(jnp.int32)
            for row in range(0, width, 128):
                strip = pl.ds(row, 128)
                product = lax.dot_general(
                    pair[left, :, row:row + 128], pair[1 - left], (((0,), (0,)), ((), ())),
                    preferred_element_type=jnp.float32,
                )
                tiles[buffer, strip, :] = product * scale
                pltpu.make_async_copy(
                    tiles.at[buffer, strip], out_ref.at[slot, strip], out_sems.at[buffer]
                ).start()

        return slot + mine.astype(jnp.int32)

    lax.fori_loop(0, devices, visit, jnp.int32(0))

    def drain(slot, carry):
        put(lax.rem(slot, BUFFERS), slot).wait()
        return carry

    lax.fori_loop(jnp.maximum(count - BUFFERS, 0), count, drain, 0)

    def end_clear(slot, carry):
        clear(slot).wait()
        return carry

    lax.fori_loop(count, slots, end_clear, 0)


def ring_form(tokens, slab_lengths, tile_owner, devices, device, slots):
    slab, units = tokens.shape
    width = units // devices
    groups = ring_gather(tokens, devices)
    table = jnp.concatenate([slab_lengths, tile_owner])
    return pl.pallas_call(
        functools.partial(ring_kernel, devices, slots),
        out_shape=jax.ShapeDtypeStruct((slots, width, width), jnp.float32),
        in_specs=[pl.BlockSpec(memory_space=pltpu.SMEM)] * 2
        + [pl.BlockSpec(memory_space=pltpu.VMEM)] * len(groups),
        out_specs=pl.BlockSpec(memory_space=pl.ANY),
        scratch_shapes=[
            pltpu.VMEM((2, slab * devices, width), jnp.bfloat16),
            pltpu.VMEM((BUFFERS, width, width), jnp.float32),
            pltpu.VMEM((width, width), jnp.float32),
            pltpu.SemaphoreType.DMA((BUFFERS,)),
            pltpu.SemaphoreType.DMA((slots,)),
        ],
        compiler_params=pltpu.CompilerParams(vmem_limit_bytes=32 * 1024 * 1024),
        cost_estimate=pl.CostEstimate(
            flops=2 * slots * slab * devices * width * width,
            bytes_accessed=4 * slots * width * width,
            transcendentals=0,
        ),
    )(device.reshape(1), table, *groups)


def per_device(tokens, slab_lengths, tile_owner):
    devices = lax.axis_size("col")
    device = lax.axis_index("col").astype(jnp.int32)
    slots = devices // 2 + devices // 8 + 1
    width = tokens.shape[1] // devices
    form = ring_form if devices == RING_DEVICES and width % 128 == 0 else gathered_form
    return form(tokens, slab_lengths, tile_owner, devices, device, slots)


def solution(mesh):
    return jax.shard_map(
        per_device,
        mesh=mesh,
        in_specs=(P(("grp", "col"), None), P("grp"), P()),
        out_specs=P(("grp", "col"), None, None),
        check_vma=False,
    )
```

```python
import functools

import jax
import jax.numpy as jnp
from jax import lax
from jax.experimental import pallas as pl
from jax.experimental.pallas import tpu as pltpu
from jax.sharding import PartitionSpec as P

BUFFERS = 4
RING_DEVICES = 16


def tile_number(devices, device, partner):
    low = jnp.minimum(device, partner)
    high = jnp.maximum(device, partner)
    return low * devices - low * (low - 1) // 2 + (high - low)


def gathered_kernel(
    devices, slots, owner_ref, device_ref, scale_ref, x_ref, mask_ref,
    out_ref, blocks, mask, tiles, zeros, in_sems, mask_sem, out_sems, zero_sems,
):
    device = device_ref[0]
    width = blocks.shape[2]

    def owned(partner):
        return owner_ref[tile_number(devices, device, partner)] == device

    def fetch(partner):
        return pltpu.make_async_copy(x_ref.at[partner], blocks.at[partner], in_sems.at[partner])

    def put(buffer, slot):
        return pltpu.make_async_copy(tiles.at[buffer], out_ref.at[slot], out_sems.at[buffer])

    def clear(slot):
        return pltpu.make_async_copy(zeros, out_ref.at[slot], zero_sems.at[slot])

    mask_copy = pltpu.make_async_copy(mask_ref, mask, mask_sem)
    mask_copy.start()
    fetch(device).start()

    def start_fetch(partner, count):
        mine = owned(partner)

        @pl.when(mine & (partner != device))
        def _():
            fetch(partner).start()

        return count + mine.astype(jnp.int32)

    count = lax.fori_loop(0, devices, start_fetch, jnp.int32(0))

    zeros[...] = jnp.zeros_like(zeros)

    def start_clear(slot, carry):
        clear(slot).start()
        return carry

    lax.fori_loop(count, slots, start_clear, 0)

    mask_copy.wait()
    fetch(device).wait()
    blocks[devices] = blocks[device] * mask[...]
    scale = scale_ref[0]

    def visit(partner, slot):
        mine = owned(partner)

        @pl.when(mine)
        def _():
            @pl.when(partner != device)
            def _():
                fetch(partner).wait()

            buffer = lax.rem(slot, BUFFERS)

            @pl.when(slot >= BUFFERS)
            def _():
                put(buffer, slot - BUFFERS).wait()

            left = jnp.where(partner <= device, partner, devices)
            right = jnp.where(partner <= device, devices, partner)
            product = lax.dot_general(
                blocks[left], blocks[right], (((0,), (0,)), ((), ())),
                preferred_element_type=jnp.float32,
            )
            tiles[buffer] = product * scale
            put(buffer, slot).start()

        return slot + mine.astype(jnp.int32)

    lax.fori_loop(0, devices, visit, jnp.int32(0))

    def drain(slot, carry):
        put(lax.rem(slot, BUFFERS), slot).wait()
        return carry

    lax.fori_loop(jnp.maximum(count - BUFFERS, 0), count, drain, 0)

    def end_clear(slot, carry):
        clear(slot).wait()
        return carry

    lax.fori_loop(count, slots, end_clear, 0)


def gathered_form(tokens, slab_lengths, tile_owner, devices, device, slots):
    slab, units = tokens.shape
    rows = slab * devices
    width = units // devices
    x = lax.all_gather(tokens, "col", axis=0, tiled=True)
    x = x.reshape(rows, devices, width).transpose(1, 0, 2)
    scale = 1.0 / jnp.sum(slab_lengths).astype(jnp.float32)
    valid = jnp.arange(slab, dtype=jnp.int32)[None, :] < slab_lengths[:, None]
    mask = jnp.broadcast_to(valid.reshape(rows, 1), (rows, width)).astype(jnp.bfloat16)
    return pl.pallas_call(
        functools.partial(gathered_kernel, devices, slots),
        out_shape=jax.ShapeDtypeStruct((slots, width, width), jnp.float32),
        in_specs=[pl.BlockSpec(memory_space=pltpu.SMEM)] * 3 + [pl.BlockSpec(memory_space=pl.ANY)] * 2,
        out_specs=pl.BlockSpec(memory_space=pl.ANY),
        scratch_shapes=[
            pltpu.VMEM((devices + 1, rows, width), jnp.bfloat16),
            pltpu.VMEM((rows, width), jnp.bfloat16),
            pltpu.VMEM((BUFFERS, width, width), jnp.float32),
            pltpu.VMEM((width, width), jnp.float32),
            pltpu.SemaphoreType.DMA((devices,)),
            pltpu.SemaphoreType.DMA,
            pltpu.SemaphoreType.DMA((BUFFERS,)),
            pltpu.SemaphoreType.DMA((slots,)),
        ],
        compiler_params=pltpu.CompilerParams(vmem_limit_bytes=50 * 1024 * 1024),
    )(tile_owner, device.reshape(1), scale.reshape(1), x, mask)


def ring_plan(devices):
    chips = devices // 2
    order = list(range(0, chips, 2)) + list(range(1, chips, 2))[::-1]
    place = {chip: at for at, chip in enumerate(order)}
    onward = []
    for device in range(devices):
        chip, core = divmod(device, 2)
        step = 1 if core == 0 else -1
        onward.append(order[(place[chip] + step) % chips] * 2 + core)
    backward = [onward.index(device) for device in range(devices)]
    return onward, backward


GROUPS = ((0, 1, 2), (8, 9, 10), (3, 4, 7), (11, 12, 15), (5, 6), (13, 14))


def ring_gather(tokens, device, devices):
    onward, backward = ring_plan(devices)
    sibling = [device ^ 1 for device in range(devices)]
    over = [at ^ 12 if at // 4 in (0, 3) else at ^ 2 for at in range(devices)]

    def send(value, target):
        return lax.ppermute(value, "col", list(enumerate(target)))

    def after(value, *others):
        return lax.optimization_barrier((value, *others))[0]

    chip, core = device // 2, device % 2
    came_ahead = ((chip % 4 == 0) | (chip % 4 == 3)) == (core == 0)

    ahead, back = [tokens], [tokens]
    for _ in range(2):
        ahead.append(send(ahead[-1], onward))
        back.append(send(back[-1], backward))
    half = send(jnp.where(came_ahead, ahead[1], back[1]), over)
    ahead.append(send(after(ahead[2], back[2]), onward))
    back.append(send(after(back[2], ahead[2]), backward))
    groups = []
    for group, others in (((tokens, ahead[1], back[1]), ()), ((ahead[2], back[2], half), ()), ((ahead[3], back[3]), ())):
        group = jnp.concatenate(group, axis=0)
        groups += [group, send(after(group, *others) if others else group, sibling)]
    return groups

def slab_origin(devices, device, number):
    chips = devices // 2
    number, flip = number % chips, number // chips
    hops = (number + 1) // 2 if number % 2 else -(number // 2)
    chip, core = device // 2, device % 2
    core = 1 - core if flip else core
    place = jnp.where(chip % 2 == 0, chip // 2, chips - 1 - chip // 2)
    place = (place - (1 - 2 * core) * hops + chips) % chips
    chip = jnp.where(2 * place < chips, 2 * place, 2 * (chips - 1 - place) + 1)
    return 2 * chip + core


def ring_kernel(devices, slots, device_ref, table_ref, *refs):
    groups = refs[:len(GROUPS)]
    out_ref, pair, tiles, zeros, out_sems, zero_sems = refs[len(GROUPS):]
    device = device_ref[0]
    slab, width = pair.shape[1] // devices, pair.shape[2]

    def owned(partner):
        return table_ref[devices + tile_number(devices, device, partner)] == device

    def put(buffer, slot):
        return pltpu.make_async_copy(tiles.at[buffer], out_ref.at[slot], out_sems.at[buffer])

    def clear(slot):
        return pltpu.make_async_copy(zeros, out_ref.at[slot], zero_sems.at[slot])

    def load_block(partner, masked):
        columns = pl.ds(pl.multiple_of(partner * width, 128), width)
        parts = []
        for numbers, ref in zip(GROUPS, groups):
            group = ref[:, columns].astype(jnp.float32)
            for at, number in enumerate(numbers):
                part = group[at * slab:(at + 1) * slab]
                if masked:
                    row = lax.broadcasted_iota(jnp.int32, (slab, width), 0)
                    part = jnp.where(row < table_ref[slab_origin(devices, device, number)], part, 0.0)
                parts.append(part)
        pair[0 if masked else 1] = jnp.concatenate(parts, axis=0).astype(jnp.bfloat16)

    count = lax.fori_loop(
        0, devices, lambda partner, total: total + owned(partner).astype(jnp.int32), jnp.int32(0)
    )

    @pl.when(count < slots)
    def _():
        zeros[...] = jnp.zeros_like(zeros)

    def start_clear(slot, carry):
        clear(slot).start()
        return carry

    lax.fori_loop(count, slots, start_clear, 0)

    load_block(device, True)
    valid_count = lax.fori_loop(0, devices, lambda at, total: total + table_ref[at], jnp.int32(0))
    scale = 1.0 / jnp.full((128, width), valid_count.astype(jnp.float32))

    def visit(partner, slot):
        mine = owned(partner)

        @pl.when(mine)
        def _():
            buffer = lax.rem(slot, BUFFERS)
            load_block(partner, False)

            @pl.when(slot >= BUFFERS)
            def _():
                put(buffer, slot - BUFFERS).wait()

            left = (partner <= device).astype(jnp.int32)
            for row in range(0, width, 128):
                strip = pl.ds(row, 128)
                product = lax.dot_general(
                    pair[left, :, row:row + 128], pair[1 - left], (((0,), (0,)), ((), ())),
                    preferred_element_type=jnp.float32,
                )
                tiles[buffer, strip, :] = product * scale
                pltpu.make_async_copy(
                    tiles.at[buffer, strip], out_ref.at[slot, strip], out_sems.at[buffer]
                ).start()

        return slot + mine.astype(jnp.int32)

    lax.fori_loop(0, devices, visit, jnp.int32(0))

    def drain(slot, carry):
        put(lax.rem(slot, BUFFERS), slot).wait()
        return carry

    lax.fori_loop(jnp.maximum(count - BUFFERS, 0), count, drain, 0)

    def end_clear(slot, carry):
        clear(slot).wait()
        return carry

    lax.fori_loop(count, slots, end_clear, 0)


def ring_form(tokens, slab_lengths, tile_owner, devices, device, slots):
    slab, units = tokens.shape
    width = units // devices
    groups = ring_gather(tokens, device, devices)
    table = jnp.concatenate([slab_lengths, tile_owner])
    return pl.pallas_call(
        functools.partial(ring_kernel, devices, slots),
        out_shape=jax.ShapeDtypeStruct((slots, width, width), jnp.float32),
        in_specs=[pl.BlockSpec(memory_space=pltpu.SMEM)] * 2
        + [pl.BlockSpec(memory_space=pltpu.VMEM)] * len(groups),
        out_specs=pl.BlockSpec(memory_space=pl.ANY),
        scratch_shapes=[
            pltpu.VMEM((2, slab * devices, width), jnp.bfloat16),
            pltpu.VMEM((BUFFERS, width, width), jnp.float32),
            pltpu.VMEM((width, width), jnp.float32),
            pltpu.SemaphoreType.DMA((BUFFERS,)),
            pltpu.SemaphoreType.DMA((slots,)),
        ],
        compiler_params=pltpu.CompilerParams(vmem_limit_bytes=32 * 1024 * 1024),
        cost_estimate=pl.CostEstimate(
            flops=2 * slots * slab * devices * width * width,
            bytes_accessed=4 * slots * width * width,
            transcendentals=0,
        ),
    )(device.reshape(1), table, *groups)


def per_device(tokens, slab_lengths, tile_owner):
    devices = lax.axis_size("col")
    device = lax.axis_index("col").astype(jnp.int32)
    slots = devices // 2 + devices // 8 + 1
    width = tokens.shape[1] // devices
    form = ring_form if devices == RING_DEVICES and width % 128 == 0 else gathered_form
    return form(tokens, slab_lengths, tile_owner, devices, device, slots)


def solution(mesh):
    return jax.shard_map(
        per_device,
        mesh=mesh,
        in_specs=(P(("grp", "col"), None), P("grp"), P()),
        out_specs=P(("grp", "col"), None, None),
        check_vma=False,
    )
```

```python
import functools

import jax
import jax.numpy as jnp
from jax import lax
from jax.experimental import pallas as pl
from jax.experimental.pallas import tpu as pltpu
from jax.sharding import PartitionSpec as P

BUFFERS = 4
RING_DEVICES = 16


def tile_number(devices, device, partner):
    low = jnp.minimum(device, partner)
    high = jnp.maximum(device, partner)
    return low * devices - low * (low - 1) // 2 + (high - low)


def gathered_kernel(
    devices, slots, owner_ref, device_ref, scale_ref, x_ref, mask_ref,
    out_ref, blocks, mask, tiles, zeros, in_sems, mask_sem, out_sems, zero_sems,
):
    device = device_ref[0]
    width = blocks.shape[2]

    def owned(partner):
        return owner_ref[tile_number(devices, device, partner)] == device

    def fetch(partner):
        return pltpu.make_async_copy(x_ref.at[partner], blocks.at[partner], in_sems.at[partner])

    def put(buffer, slot):
        return pltpu.make_async_copy(tiles.at[buffer], out_ref.at[slot], out_sems.at[buffer])

    def clear(slot):
        return pltpu.make_async_copy(zeros, out_ref.at[slot], zero_sems.at[slot])

    mask_copy = pltpu.make_async_copy(mask_ref, mask, mask_sem)
    mask_copy.start()
    fetch(device).start()

    def start_fetch(partner, count):
        mine = owned(partner)

        @pl.when(mine & (partner != device))
        def _():
            fetch(partner).start()

        return count + mine.astype(jnp.int32)

    count = lax.fori_loop(0, devices, start_fetch, jnp.int32(0))

    zeros[...] = jnp.zeros_like(zeros)

    def start_clear(slot, carry):
        clear(slot).start()
        return carry

    lax.fori_loop(count, slots, start_clear, 0)

    mask_copy.wait()
    fetch(device).wait()
    blocks[devices] = blocks[device] * mask[...]
    scale = scale_ref[0]

    def visit(partner, slot):
        mine = owned(partner)

        @pl.when(mine)
        def _():
            @pl.when(partner != device)
            def _():
                fetch(partner).wait()

            buffer = lax.rem(slot, BUFFERS)

            @pl.when(slot >= BUFFERS)
            def _():
                put(buffer, slot - BUFFERS).wait()

            left = jnp.where(partner <= device, partner, devices)
            right = jnp.where(partner <= device, devices, partner)
            product = lax.dot_general(
                blocks[left], blocks[right], (((0,), (0,)), ((), ())),
                preferred_element_type=jnp.float32,
            )
            tiles[buffer] = product * scale
            put(buffer, slot).start()

        return slot + mine.astype(jnp.int32)

    lax.fori_loop(0, devices, visit, jnp.int32(0))

    def drain(slot, carry):
        put(lax.rem(slot, BUFFERS), slot).wait()
        return carry

    lax.fori_loop(jnp.maximum(count - BUFFERS, 0), count, drain, 0)

    def end_clear(slot, carry):
        clear(slot).wait()
        return carry

    lax.fori_loop(count, slots, end_clear, 0)


def gathered_form(tokens, slab_lengths, tile_owner, devices, device, slots):
    slab, units = tokens.shape
    rows = slab * devices
    width = units // devices
    x = lax.all_gather(tokens, "col", axis=0, tiled=True)
    x = x.reshape(rows, devices, width).transpose(1, 0, 2)
    scale = 1.0 / jnp.sum(slab_lengths).astype(jnp.float32)
    valid = jnp.arange(slab, dtype=jnp.int32)[None, :] < slab_lengths[:, None]
    mask = jnp.broadcast_to(valid.reshape(rows, 1), (rows, width)).astype(jnp.bfloat16)
    return pl.pallas_call(
        functools.partial(gathered_kernel, devices, slots),
        out_shape=jax.ShapeDtypeStruct((slots, width, width), jnp.float32),
        in_specs=[pl.BlockSpec(memory_space=pltpu.SMEM)] * 3 + [pl.BlockSpec(memory_space=pl.ANY)] * 2,
        out_specs=pl.BlockSpec(memory_space=pl.ANY),
        scratch_shapes=[
            pltpu.VMEM((devices + 1, rows, width), jnp.bfloat16),
            pltpu.VMEM((rows, width), jnp.bfloat16),
            pltpu.VMEM((BUFFERS, width, width), jnp.float32),
            pltpu.VMEM((width, width), jnp.float32),
            pltpu.SemaphoreType.DMA((devices,)),
            pltpu.SemaphoreType.DMA,
            pltpu.SemaphoreType.DMA((BUFFERS,)),
            pltpu.SemaphoreType.DMA((slots,)),
        ],
        compiler_params=pltpu.CompilerParams(vmem_limit_bytes=50 * 1024 * 1024),
    )(tile_owner, device.reshape(1), scale.reshape(1), x, mask)


def ring_plan(devices):
    chips = devices // 2
    order = list(range(0, chips, 2)) + list(range(1, chips, 2))[::-1]
    place = {chip: at for at, chip in enumerate(order)}
    onward = []
    for device in range(devices):
        chip, core = divmod(device, 2)
        step = 1 if core == 0 else -1
        onward.append(order[(place[chip] + step) % chips] * 2 + core)
    backward = [onward.index(device) for device in range(devices)]
    return onward, backward


GROUPS = ((0, 1, 2), (8, 9, 10), (3, 4), (11, 12), (5, 6, 7), (13, 14, 15))


def first_needed(devices, chip):
    return (2 * chip - devices // 2 - devices // 8 + devices) % devices


def ring_gather(tokens, device, devices):
    onward, backward = ring_plan(devices)
    sibling = [device ^ 1 for device in range(devices)]
    over = [at ^ 12 if at // 4 in (0, 3) else at ^ 2 for at in range(devices)]

    def send(value, target):
        return lax.ppermute(value, "col", list(enumerate(target)))

    def after(value, *others):
        return lax.optimization_barrier((value, *others))[0]

    chip, core = device // 2, device % 2
    chips = devices // 2
    even = chip % 2 == 0
    next_chip = jnp.where(even, jnp.where(chip == chips - 2, chips - 1, chip + 2), jnp.where(chip == 1, 0, chip - 2))
    last_chip = jnp.where(even, jnp.where(chip == 0, 1, chip - 2), jnp.where(chip == chips - 1, chips - 2, chip + 2))
    onward_chip = jnp.where(core == 0, next_chip, last_chip)
    backward_chip = jnp.where(core == 0, last_chip, next_chip)
    over_chip = jnp.where((chip < 2) | (chip >= chips - 2), chip ^ 6, chip ^ 1)
    chip, core = device // 2, device % 2
    chips = devices // 2
    even = chip % 2 == 0
    next_chip = jnp.where(even, jnp.where(chip == chips - 2, chips - 1, chip + 2), jnp.where(chip == 1, 0, chip - 2))
    last_chip = jnp.where(even, jnp.where(chip == 0, 1, chip - 2), jnp.where(chip == chips - 1, chips - 2, chip + 2))
    onward_chip = jnp.where(core == 0, next_chip, last_chip)
    backward_chip = jnp.where(core == 0, last_chip, next_chip)
    over_chip = jnp.where((chip < 2) | (chip >= chips - 2), chip ^ 6, chip ^ 1)
    came_ahead = ((chip % 4 == 0) | (chip % 4 == 3)) == (core == 0)
    slab, units = tokens.shape
    needed = devices // 2 + devices // 8 + 2

    def window(value, chip):
        blocks = value.reshape(slab, devices, units // devices)
        blocks = jnp.concatenate([blocks, blocks], axis=1)
        blocks = lax.dynamic_slice_in_dim(blocks, first_needed(devices, chip), needed, axis=1)
        return blocks.reshape(slab, -1)

    ahead, back = [tokens], [tokens]
    for _ in range(2):
        ahead.append(send(ahead[-1], onward))
        back.append(send(back[-1], backward))
    half = send(window(jnp.where(came_ahead, ahead[1], back[1]), over_chip), over)
    ahead.append(send(window(ahead[2], onward_chip), onward))
    back.append(send(window(back[2], backward_chip), backward))
    near = jnp.concatenate((tokens, ahead[1], back[1]), axis=0)
    middle = jnp.concatenate((ahead[2], back[2]), axis=0)
    last = jnp.concatenate((ahead[3], back[3], half), axis=0)
    near_beside = send(near, sibling)
    middle_beside = send(middle, sibling)
    last_beside = send(after(last, middle_beside), sibling)
    return [near, near_beside, middle, middle_beside, last, last_beside]

def slab_origin(devices, device, number):
    chips = devices // 2
    number, flip = number % chips, number // chips
    hops = (number + 1) // 2 if number % 2 else -(number // 2)
    chip, core = device // 2, device % 2
    core = 1 - core if flip else core
    place = jnp.where(chip % 2 == 0, chip // 2, chips - 1 - chip // 2)
    place = (place - (1 - 2 * core) * hops + chips) % chips
    chip = jnp.where(2 * place < chips, 2 * place, 2 * (chips - 1 - place) + 1)
    return 2 * chip + core


def ring_kernel(devices, slots, device_ref, table_ref, *refs):
    groups = refs[:len(GROUPS)]
    out_ref, pair, tiles, zeros, out_sems, zero_sems = refs[len(GROUPS):]
    device = device_ref[0]
    slab, width = pair.shape[1] // devices, pair.shape[2]

    def owned(partner):
        return table_ref[devices + tile_number(devices, device, partner)] == device

    def put(buffer, slot):
        return pltpu.make_async_copy(tiles.at[buffer], out_ref.at[slot], out_sems.at[buffer])

    def clear(slot):
        return pltpu.make_async_copy(zeros, out_ref.at[slot], zero_sems.at[slot])

    def load_block(partner, masked):
        parts = []
        for numbers, ref in zip(GROUPS, groups):
            whole = ref.shape[1] == devices * width
            place = partner if whole else (partner - first_needed(devices, device // 2) + devices) % devices
            columns = pl.ds(pl.multiple_of(place * width, 128), width)
            whole = ref.shape[1] == devices * width
            place = partner if whole else (partner - first_needed(devices, device // 2) + devices) % devices
            columns = pl.ds(pl.multiple_of(place * width, 128), width)
            group = ref[:, columns].astype(jnp.float32)
            for at, number in enumerate(numbers):
                part = group[at * slab:(at + 1) * slab]
                if masked:
                    row = lax.broadcasted_iota(jnp.int32, (slab, width), 0)
                    part = jnp.where(row < table_ref[slab_origin(devices, device, number)], part, 0.0)
                parts.append(part)
        pair[0 if masked else 1] = jnp.concatenate(parts, axis=0).astype(jnp.bfloat16)

    count = lax.fori_loop(
        0, devices, lambda partner, total: total + owned(partner).astype(jnp.int32), jnp.int32(0)
    )

    @pl.when(count < slots)
    def _():
        zeros[...] = jnp.zeros_like(zeros)

    def start_clear(slot, carry):
        clear(slot).start()
        return carry

    lax.fori_loop(count, slots, start_clear, 0)

    load_block(device, True)
    valid_count = lax.fori_loop(0, devices, lambda at, total: total + table_ref[at], jnp.int32(0))
    scale = 1.0 / jnp.full((128, width), valid_count.astype(jnp.float32))

    def visit(partner, slot):
        mine = owned(partner)

        @pl.when(mine)
        def _():
            buffer = lax.rem(slot, BUFFERS)
            load_block(partner, False)

            @pl.when(slot >= BUFFERS)
            def _():
                put(buffer, slot - BUFFERS).wait()

            left = (partner <= device).astype(jnp.int32)
            for row in range(0, width, 128):
                strip = pl.ds(row, 128)
                product = lax.dot_general(
                    pair[left, :, row:row + 128], pair[1 - left], (((0,), (0,)), ((), ())),
                    preferred_element_type=jnp.float32,
                )
                tiles[buffer, strip, :] = product * scale
                pltpu.make_async_copy(
                    tiles.at[buffer, strip], out_ref.at[slot, strip], out_sems.at[buffer]
                ).start()

        return slot + mine.astype(jnp.int32)

    lax.fori_loop(0, devices, visit, jnp.int32(0))

    def drain(slot, carry):
        put(lax.rem(slot, BUFFERS), slot).wait()
        return carry

    lax.fori_loop(jnp.maximum(count - BUFFERS, 0), count, drain, 0)

    def end_clear(slot, carry):
        clear(slot).wait()
        return carry

    lax.fori_loop(count, slots, end_clear, 0)


def ring_form(tokens, slab_lengths, tile_owner, devices, device, slots):
    slab, units = tokens.shape
    width = units // devices
    groups = ring_gather(tokens, device, devices)
    table = jnp.concatenate([slab_lengths, tile_owner])
    return pl.pallas_call(
        functools.partial(ring_kernel, devices, slots),
        out_shape=jax.ShapeDtypeStruct((slots, width, width), jnp.float32),
        in_specs=[pl.BlockSpec(memory_space=pltpu.SMEM)] * 2
        + [pl.BlockSpec(memory_space=pltpu.VMEM)] * len(groups),
        out_specs=pl.BlockSpec(memory_space=pl.ANY),
        scratch_shapes=[
            pltpu.VMEM((2, slab * devices, width), jnp.bfloat16),
            pltpu.VMEM((BUFFERS, width, width), jnp.float32),
            pltpu.VMEM((width, width), jnp.float32),
            pltpu.SemaphoreType.DMA((BUFFERS,)),
            pltpu.SemaphoreType.DMA((slots,)),
        ],
        compiler_params=pltpu.CompilerParams(vmem_limit_bytes=32 * 1024 * 1024),
        cost_estimate=pl.CostEstimate(
            flops=2 * slots * slab * devices * width * width,
            bytes_accessed=4 * slots * width * width,
            transcendentals=0,
        ),
    )(device.reshape(1), table, *groups)


def per_device(tokens, slab_lengths, tile_owner):
    devices = lax.axis_size("col")
    device = lax.axis_index("col").astype(jnp.int32)
    slots = devices // 2 + devices // 8 + 1
    width = tokens.shape[1] // devices
    form = ring_form if devices == RING_DEVICES and width % 128 == 0 else gathered_form
    return form(tokens, slab_lengths, tile_owner, devices, device, slots)


def solution(mesh):
    return jax.shard_map(
        per_device,
        mesh=mesh,
        in_specs=(P(("grp", "col"), None), P("grp"), P()),
        out_specs=P(("grp", "col"), None, None),
        check_vma=False,
    )
```

```python
import functools

import jax
import jax.numpy as jnp
from jax import lax
from jax.experimental import pallas as pl
from jax.experimental.pallas import tpu as pltpu
from jax.sharding import PartitionSpec as P

BUFFERS = 4
RING_DEVICES = 16


def tile_number(devices, device, partner):
    low = jnp.minimum(device, partner)
    high = jnp.maximum(device, partner)
    return low * devices - low * (low - 1) // 2 + (high - low)


def gathered_kernel(
    devices, slots, owner_ref, device_ref, scale_ref, x_ref, mask_ref,
    out_ref, blocks, mask, tiles, zeros, in_sems, mask_sem, out_sems, zero_sems,
):
    device = device_ref[0]
    width = blocks.shape[2]

    def owned(partner):
        return owner_ref[tile_number(devices, device, partner)] == device

    def fetch(partner):
        return pltpu.make_async_copy(x_ref.at[partner], blocks.at[partner], in_sems.at[partner])

    def put(buffer, slot):
        return pltpu.make_async_copy(tiles.at[buffer], out_ref.at[slot], out_sems.at[buffer])

    def clear(slot):
        return pltpu.make_async_copy(zeros, out_ref.at[slot], zero_sems.at[slot])

    mask_copy = pltpu.make_async_copy(mask_ref, mask, mask_sem)
    mask_copy.start()
    fetch(device).start()

    def start_fetch(partner, count):
        mine = owned(partner)

        @pl.when(mine & (partner != device))
        def _():
            fetch(partner).start()

        return count + mine.astype(jnp.int32)

    count = lax.fori_loop(0, devices, start_fetch, jnp.int32(0))

    zeros[...] = jnp.zeros_like(zeros)

    def start_clear(slot, carry):
        clear(slot).start()
        return carry

    lax.fori_loop(count, slots, start_clear, 0)

    mask_copy.wait()
    fetch(device).wait()
    blocks[devices] = blocks[device] * mask[...]
    scale = scale_ref[0]

    def visit(partner, slot):
        mine = owned(partner)

        @pl.when(mine)
        def _():
            @pl.when(partner != device)
            def _():
                fetch(partner).wait()

            buffer = lax.rem(slot, BUFFERS)

            @pl.when(slot >= BUFFERS)
            def _():
                put(buffer, slot - BUFFERS).wait()

            left = jnp.where(partner <= device, partner, devices)
            right = jnp.where(partner <= device, devices, partner)
            product = lax.dot_general(
                blocks[left], blocks[right], (((0,), (0,)), ((), ())),
                preferred_element_type=jnp.float32,
            )
            tiles[buffer] = product * scale
            put(buffer, slot).start()

        return slot + mine.astype(jnp.int32)

    lax.fori_loop(0, devices, visit, jnp.int32(0))

    def drain(slot, carry):
        put(lax.rem(slot, BUFFERS), slot).wait()
        return carry

    lax.fori_loop(jnp.maximum(count - BUFFERS, 0), count, drain, 0)

    def end_clear(slot, carry):
        clear(slot).wait()
        return carry

    lax.fori_loop(count, slots, end_clear, 0)


def gathered_form(tokens, slab_lengths, tile_owner, devices, device, slots):
    slab, units = tokens.shape
    rows = slab * devices
    width = units // devices
    x = lax.all_gather(tokens, "col", axis=0, tiled=True)
    x = x.reshape(rows, devices, width).transpose(1, 0, 2)
    scale = 1.0 / jnp.sum(slab_lengths).astype(jnp.float32)
    valid = jnp.arange(slab, dtype=jnp.int32)[None, :] < slab_lengths[:, None]
    mask = jnp.broadcast_to(valid.reshape(rows, 1), (rows, width)).astype(jnp.bfloat16)
    return pl.pallas_call(
        functools.partial(gathered_kernel, devices, slots),
        out_shape=jax.ShapeDtypeStruct((slots, width, width), jnp.float32),
        in_specs=[pl.BlockSpec(memory_space=pltpu.SMEM)] * 3 + [pl.BlockSpec(memory_space=pl.ANY)] * 2,
        out_specs=pl.BlockSpec(memory_space=pl.ANY),
        scratch_shapes=[
            pltpu.VMEM((devices + 1, rows, width), jnp.bfloat16),
            pltpu.VMEM((rows, width), jnp.bfloat16),
            pltpu.VMEM((BUFFERS, width, width), jnp.float32),
            pltpu.VMEM((width, width), jnp.float32),
            pltpu.SemaphoreType.DMA((devices,)),
            pltpu.SemaphoreType.DMA,
            pltpu.SemaphoreType.DMA((BUFFERS,)),
            pltpu.SemaphoreType.DMA((slots,)),
        ],
        compiler_params=pltpu.CompilerParams(vmem_limit_bytes=50 * 1024 * 1024),
    )(tile_owner, device.reshape(1), scale.reshape(1), x, mask)


def together(*values):
    return lax.optimization_barrier(values)


def ring_plan(devices):
    chips = devices // 2
    order = list(range(0, chips, 2)) + list(range(1, chips, 2))[::-1]
    place = {chip: at for at, chip in enumerate(order)}
    onward = []
    for device in range(devices):
        chip, core = divmod(device, 2)
        step = 1 if core == 0 else -1
        onward.append(order[(place[chip] + step) % chips] * 2 + core)
    backward = [onward.index(device) for device in range(devices)]
    return onward, backward


GROUPS = ((0, 1, 2), (8, 9, 10), (3, 4), (11, 12), (5, 6, 7), (13, 14, 15))


def first_needed(devices, chip):
    return (2 * chip - devices // 2 - devices // 8 + devices) % devices


def near_and_far(devices):
    needed = devices // 2 + devices // 8 + 2
    return (needed - needed // 2, needed), (0, needed - needed // 2)


def ring_gather(tokens, device, devices):
    onward, backward = ring_plan(devices)
    sibling = [device ^ 1 for device in range(devices)]
    over = [at ^ 12 if at // 4 in (0, 3) else at ^ 2 for at in range(devices)]

    def send(value, target):
        return lax.ppermute(value, "col", list(enumerate(target)))

    chip, core = device // 2, device % 2
    chips = devices // 2
    even = chip % 2 == 0
    next_chip = jnp.where(even, jnp.where(chip == chips - 2, chips - 1, chip + 2), jnp.where(chip == 1, 0, chip - 2))
    last_chip = jnp.where(even, jnp.where(chip == 0, 1, chip - 2), jnp.where(chip == chips - 1, chips - 2, chip + 2))
    onward_chip = jnp.where(core == 0, next_chip, last_chip)
    backward_chip = jnp.where(core == 0, last_chip, next_chip)
    over_chip = jnp.where((chip < 2) | (chip >= chips - 2), chip ^ 6, chip ^ 1)
    chip, core = device // 2, device % 2
    chips = devices // 2
    even = chip % 2 == 0
    next_chip = jnp.where(even, jnp.where(chip == chips - 2, chips - 1, chip + 2), jnp.where(chip == 1, 0, chip - 2))
    last_chip = jnp.where(even, jnp.where(chip == 0, 1, chip - 2), jnp.where(chip == chips - 1, chips - 2, chip + 2))
    onward_chip = jnp.where(core == 0, next_chip, last_chip)
    backward_chip = jnp.where(core == 0, last_chip, next_chip)
    over_chip = jnp.where((chip < 2) | (chip >= chips - 2), chip ^ 6, chip ^ 1)
    came_ahead = ((chip % 4 == 0) | (chip % 4 == 3)) == (core == 0)
    slab, units = tokens.shape

    def window(value, chip, run):
        start, stop = run
        blocks = value.reshape(slab, devices, units // devices)
        blocks = jnp.concatenate([blocks, blocks], axis=1)
        start_block = first_needed(devices, chip) + start
        blocks = lax.dynamic_slice_in_dim(blocks, start_block, stop - start, axis=1)
        return blocks.reshape(slab, -1)

    ahead, back = [tokens], [tokens]
    for _ in range(2):
        ahead.append(send(ahead[-1], onward))
        back.append(send(back[-1], backward))
    near_run, far_run = near_and_far(devices)
    held = jnp.where(came_ahead, ahead[1], back[1])
    half_near = send(window(held, over_chip, near_run), over)
    near = jnp.concatenate((tokens, ahead[1], back[1]), axis=0)
    near_beside = send(near, sibling)
    ahead_2, back_2, near_beside = together(ahead[2], back[2], near_beside)
    ahead_near = send(window(ahead_2, onward_chip, near_run), onward)
    back_near = send(window(back_2, backward_chip, near_run), backward)
    held, half_near = together(held, half_near)
    half_far = send(window(held, over_chip, far_run), over)
    ahead_far = send(window(ahead_2, onward_chip, far_run), onward)
    back_far = send(window(back_2, backward_chip, far_run), backward)
    middle = jnp.concatenate((ahead_2, back_2), axis=0)
    middle_beside = send(middle, sibling)
    last_near = jnp.concatenate((ahead_near, back_near, half_near), axis=0)
    last_far = (ahead_far, back_far, half_far)
    return [near, near_beside, middle, middle_beside], (last_near, last_far), lambda value: send(value, sibling)


def slab_origin(devices, device, number):
    chips = devices // 2
    number, flip = number % chips, number // chips
    hops = (number + 1) // 2 if number % 2 else -(number // 2)
    chip, core = device // 2, device % 2
    core = 1 - core if flip else core
    place = jnp.where(chip % 2 == 0, chip // 2, chips - 1 - chip // 2)
    place = (place - (1 - 2 * core) * hops + chips) % chips
    chip = jnp.where(2 * place < chips, 2 * place, 2 * (chips - 1 - place) + 1)
    return 2 * chip + core


def ring_kernel(devices, slots, spans, at, device_ref, table_ref, *refs):
    (near_run, far_run), refs = near_and_far(devices), list(refs)
    whole, near = refs[:4], refs[4:6]
    in_near = spans[at][0] >= near_run[0]
    far = None if in_near else refs[6:8]
    refs = refs[6 if in_near else 8:]
    if at:
        refs = refs[1:]
    out_ref, pair, tiles, zeros, out_sems, zero_sems = refs
    device = device_ref[0]
    slab, width = pair.shape[1] // devices, pair.shape[2]
    first = first_needed(devices, device // 2)

    def place_of(partner):
        return lax.rem(partner - first + devices, devices)

    def owned(partner):
        return table_ref[devices + tile_number(devices, device, partner)] == device

    def within(partner, span):
        place = place_of(partner)
        return (place >= span[0]) & (place < span[1])

    def put(buffer, slot):
        return pltpu.make_async_copy(tiles.at[buffer], out_ref.at[slot], out_sems.at[buffer])

    def clear(slot):
        return pltpu.make_async_copy(zeros, out_ref.at[slot], zero_sems.at[slot])

    def load_block(partner, masked):
        run, last = (near_run, near) if masked or in_near else (far_run, far)
        parts = []
        for numbers, ref in zip(GROUPS, (*whole, *last)):
            place = partner if ref.shape[1] == devices * width else place_of(partner) - run[0]
            group = ref[:, pl.ds(pl.multiple_of(place * width, 128), width)].astype(jnp.float32)
            for row, number in enumerate(numbers):
                part = group[row * slab:(row + 1) * slab]
                if masked:
                    line = lax.broadcasted_iota(jnp.int32, (slab, width), 0)
                    part = jnp.where(line < table_ref[slab_origin(devices, device, number)], part, 0.0)
                parts.append(part)
        pair[0 if masked else 1] = jnp.concatenate(parts, axis=0).astype(jnp.bfloat16)

    def add_owned(partner, counts):
        mine = owned(partner).astype(jnp.int32)
        spanned = [count + mine * within(partner, span).astype(jnp.int32) for count, span in zip(counts[1:], spans)]
        return (counts[0] + mine, *spanned)

    count, *in_span = lax.fori_loop(0, devices, add_owned, (jnp.int32(0),) * (1 + len(spans)))
    clear_from, clear_to = count, count
    for made, (start, stop) in zip(in_span[:at + 1], spans):
        clear_from = clear_to
        clear_to = jnp.minimum(clear_from + jnp.maximum(stop - start - made, 0), slots)
    if at == len(spans) - 1:
        clear_to = jnp.int32(slots)

    @pl.when(clear_from < clear_to)
    def _():
        zeros[...] = jnp.zeros_like(zeros)

    def start_clear(slot, carry):
        clear(slot).start()
        return carry

    lax.fori_loop(clear_from, clear_to, start_clear, 0)

    load_block(device, True)
    valid_count = lax.fori_loop(0, devices, lambda row, total: total + table_ref[row], jnp.int32(0))
    scale = 1.0 / jnp.full((128, width), valid_count.astype(jnp.float32))

    def visit(partner, carry):
        slot, made = carry
        mine = owned(partner)
        now = mine & within(partner, spans[at])

        @pl.when(now)
        def _():
            buffer = lax.rem(made, BUFFERS)
            load_block(partner, False)

            @pl.when(made >= BUFFERS)
            def _():
                put(buffer, slot).wait()

            left = (partner <= device).astype(jnp.int32)
            for row in range(0, width, 128):
                strip = pl.ds(row, 128)
                product = lax.dot_general(
                    pair[left, :, row:row + 128], pair[1 - left], (((0,), (0,)), ((), ())),
                    preferred_element_type=jnp.float32,
                )
                tiles[buffer, strip, :] = product * scale
                pltpu.make_async_copy(
                    tiles.at[buffer, strip], out_ref.at[slot, strip], out_sems.at[buffer]
                ).start()

        return slot + mine.astype(jnp.int32), made + now.astype(jnp.int32)

    _, made = lax.fori_loop(0, devices, visit, (jnp.int32(0), jnp.int32(0)))

    def drain(number, carry):
        put(lax.rem(number, BUFFERS), 0).wait()
        return carry

    lax.fori_loop(jnp.maximum(made - BUFFERS, 0), made, drain, 0)

    def end_clear(slot, carry):
        clear(slot).wait()
        return carry

    lax.fori_loop(clear_from, clear_to, end_clear, 0)


def ring_form(tokens, slab_lengths, tile_owner, devices, device, slots):
    slab, units = tokens.shape
    width = units // devices
    near_run, far_run = near_and_far(devices)
    early = near_run[0] + 2
    spans = ((early, near_run[1]), (near_run[0], early), far_run)
    whole, (near, far), beside = ring_gather(tokens, device, devices)
    table = jnp.concatenate([slab_lengths, tile_owner])

    def make(at, groups, result):
        given = [] if result is None else [result]
        length = spans[at][1] - spans[at][0]
        return pl.pallas_call(
            functools.partial(ring_kernel, devices, slots, spans, at),
            out_shape=jax.ShapeDtypeStruct((slots, width, width), jnp.float32),
            in_specs=[pl.BlockSpec(memory_space=pltpu.SMEM)] * 2
            + [pl.BlockSpec(memory_space=pltpu.VMEM)] * len(groups)
            + [pl.BlockSpec(memory_space=pl.ANY)] * len(given),
            out_specs=pl.BlockSpec(memory_space=pl.ANY),
            input_output_aliases={2 + len(groups): 0} if given else {},
            scratch_shapes=[
                pltpu.VMEM((2, slab * devices, width), jnp.bfloat16),
                pltpu.VMEM((BUFFERS, width, width), jnp.float32),
                pltpu.VMEM((width, width), jnp.float32),
                pltpu.SemaphoreType.DMA((BUFFERS,)),
                pltpu.SemaphoreType.DMA((slots,)),
            ],
            compiler_params=pltpu.CompilerParams(vmem_limit_bytes=32 * 1024 * 1024),
            cost_estimate=pl.CostEstimate(
                flops=2 * length * slab * devices * width * width,
                bytes_accessed=4 * length * width * width,
                transcendentals=0,
            ),
        )(device.reshape(1), table, *groups, *given)

    groups = whole + [near, beside(near)]
    result = make(0, groups, None)
    *far, result = together(*far, result)
    far = jnp.concatenate(far, axis=0)
    groups_far = groups + [far, beside(far)]
    for at in range(1, len(spans)):
        result = make(at, groups if spans[at][0] >= near_run[0] else groups_far, result)
    return result


def per_device(tokens, slab_lengths, tile_owner):
    devices = lax.axis_size("col")
    device = lax.axis_index("col").astype(jnp.int32)
    slots = devices // 2 + devices // 8 + 1
    width = tokens.shape[1] // devices
    form = ring_form if devices == RING_DEVICES and width % 128 == 0 else gathered_form
    return form(tokens, slab_lengths, tile_owner, devices, device, slots)


def solution(mesh):
    return jax.shard_map(
        per_device,
        mesh=mesh,
        in_specs=(P(("grp", "col"), None), P("grp"), P()),
        out_specs=P(("grp", "col"), None, None),
        check_vma=False,
    )
```

```python
import functools

import jax
import jax.numpy as jnp
from jax import lax
from jax.experimental import pallas as pl
from jax.experimental.pallas import tpu as pltpu
from jax.sharding import PartitionSpec as P

BUFFERS = 4
STRIP = 256
RING_DEVICES = 16


def tile_number(devices, device, partner):
    low = jnp.minimum(device, partner)
    high = jnp.maximum(device, partner)
    return low * devices - low * (low - 1) // 2 + (high - low)


def gathered_kernel(
    devices, slots, owner_ref, device_ref, scale_ref, x_ref, mask_ref,
    out_ref, blocks, mask, tiles, zeros, in_sems, mask_sem, out_sems, zero_sems,
):
    device = device_ref[0]
    width = blocks.shape[2]

    def owned(partner):
        return owner_ref[tile_number(devices, device, partner)] == device

    def fetch(partner):
        return pltpu.make_async_copy(x_ref.at[partner], blocks.at[partner], in_sems.at[partner])

    def put(buffer, slot):
        return pltpu.make_async_copy(tiles.at[buffer], out_ref.at[slot], out_sems.at[buffer])

    def clear(slot):
        return pltpu.make_async_copy(zeros, out_ref.at[slot], zero_sems.at[slot])

    mask_copy = pltpu.make_async_copy(mask_ref, mask, mask_sem)
    mask_copy.start()
    fetch(device).start()

    def start_fetch(partner, count):
        mine = owned(partner)

        @pl.when(mine & (partner != device))
        def _():
            fetch(partner).start()

        return count + mine.astype(jnp.int32)

    count = lax.fori_loop(0, devices, start_fetch, jnp.int32(0))

    zeros[...] = jnp.zeros_like(zeros)

    def start_clear(slot, carry):
        clear(slot).start()
        return carry

    lax.fori_loop(count, slots, start_clear, 0)

    mask_copy.wait()
    fetch(device).wait()
    blocks[devices] = blocks[device] * mask[...]
    scale = scale_ref[0]

    def visit(partner, slot):
        mine = owned(partner)

        @pl.when(mine)
        def _():
            @pl.when(partner != device)
            def _():
                fetch(partner).wait()

            buffer = lax.rem(slot, BUFFERS)

            @pl.when(slot >= BUFFERS)
            def _():
                put(buffer, slot - BUFFERS).wait()

            left = jnp.where(partner <= device, partner, devices)
            right = jnp.where(partner <= device, devices, partner)
            product = lax.dot_general(
                blocks[left], blocks[right], (((0,), (0,)), ((), ())),
                preferred_element_type=jnp.float32,
            )
            tiles[buffer] = product * scale
            put(buffer, slot).start()

        return slot + mine.astype(jnp.int32)

    lax.fori_loop(0, devices, visit, jnp.int32(0))

    def drain(slot, carry):
        put(lax.rem(slot, BUFFERS), slot).wait()
        return carry

    lax.fori_loop(jnp.maximum(count - BUFFERS, 0), count, drain, 0)

    def end_clear(slot, carry):
        clear(slot).wait()
        return carry

    lax.fori_loop(count, slots, end_clear, 0)


def gathered_form(tokens, slab_lengths, tile_owner, devices, device, slots):
    slab, units = tokens.shape
    rows = slab * devices
    width = units // devices
    x = lax.all_gather(tokens, "col", axis=0, tiled=True)
    x = x.reshape(rows, devices, width).transpose(1, 0, 2)
    scale = 1.0 / jnp.sum(slab_lengths).astype(jnp.float32)
    valid = jnp.arange(slab, dtype=jnp.int32)[None, :] < slab_lengths[:, None]
    mask = jnp.broadcast_to(valid.reshape(rows, 1), (rows, width)).astype(jnp.bfloat16)
    return pl.pallas_call(
        functools.partial(gathered_kernel, devices, slots),
        out_shape=jax.ShapeDtypeStruct((slots, width, width), jnp.float32),
        in_specs=[pl.BlockSpec(memory_space=pltpu.SMEM)] * 3 + [pl.BlockSpec(memory_space=pl.ANY)] * 2,
        out_specs=pl.BlockSpec(memory_space=pl.ANY),
        scratch_shapes=[
            pltpu.VMEM((devices + 1, rows, width), jnp.bfloat16),
            pltpu.VMEM((rows, width), jnp.bfloat16),
            pltpu.VMEM((BUFFERS, width, width), jnp.float32),
            pltpu.VMEM((width, width), jnp.float32),
            pltpu.SemaphoreType.DMA((devices,)),
            pltpu.SemaphoreType.DMA,
            pltpu.SemaphoreType.DMA((BUFFERS,)),
            pltpu.SemaphoreType.DMA((slots,)),
        ],
        compiler_params=pltpu.CompilerParams(vmem_limit_bytes=50 * 1024 * 1024),
    )(tile_owner, device.reshape(1), scale.reshape(1), x, mask)


def ring_plan(devices):
    chips = devices // 2
    order = list(range(0, chips, 2)) + list(range(1, chips, 2))[::-1]
    place = {chip: at for at, chip in enumerate(order)}
    onward = []
    for device in range(devices):
        chip, core = divmod(device, 2)
        step = 1 if core == 0 else -1
        onward.append(order[(place[chip] + step) % chips] * 2 + core)
    backward = [onward.index(device) for device in range(devices)]
    return onward, backward


GROUPS = ((0, 1, 2), (8, 9, 10), (3, 4), (11, 12), (5, 7), (13, 15), (6,), (14,))


def first_needed(devices, chip):
    return (2 * chip - devices // 2 - devices // 8 + devices) % devices


def ring_gather(tokens, device, devices):
    onward, backward = ring_plan(devices)
    sibling = [device ^ 1 for device in range(devices)]
    over = [at ^ 12 if at // 4 in (0, 3) else at ^ 2 for at in range(devices)]

    def send(value, target):
        return lax.ppermute(value, "col", list(enumerate(target)))

    def after(value, *others):
        return lax.optimization_barrier((value, *others))[0]

    chip, core = device // 2, device % 2
    chips = devices // 2
    even = chip % 2 == 0
    next_chip = jnp.where(even, jnp.where(chip == chips - 2, chips - 1, chip + 2), jnp.where(chip == 1, 0, chip - 2))
    last_chip = jnp.where(even, jnp.where(chip == 0, 1, chip - 2), jnp.where(chip == chips - 1, chips - 2, chip + 2))
    onward_chip = jnp.where(core == 0, next_chip, last_chip)
    backward_chip = jnp.where(core == 0, last_chip, next_chip)
    over_chip = jnp.where((chip < 2) | (chip >= chips - 2), chip ^ 6, chip ^ 1)
    chip, core = device // 2, device % 2
    chips = devices // 2
    even = chip % 2 == 0
    next_chip = jnp.where(even, jnp.where(chip == chips - 2, chips - 1, chip + 2), jnp.where(chip == 1, 0, chip - 2))
    last_chip = jnp.where(even, jnp.where(chip == 0, 1, chip - 2), jnp.where(chip == chips - 1, chips - 2, chip + 2))
    onward_chip = jnp.where(core == 0, next_chip, last_chip)
    backward_chip = jnp.where(core == 0, last_chip, next_chip)
    over_chip = jnp.where((chip < 2) | (chip >= chips - 2), chip ^ 6, chip ^ 1)
    came_ahead = ((chip % 4 == 0) | (chip % 4 == 3)) == (core == 0)
    slab, units = tokens.shape
    needed = devices // 2 + devices // 8 + 2

    def window(value, chip):
        blocks = value.reshape(slab, devices, units // devices)
        blocks = jnp.concatenate([blocks, blocks], axis=1)
        blocks = lax.dynamic_slice_in_dim(blocks, first_needed(devices, chip), needed, axis=1)
        return blocks.reshape(slab, -1)

    ahead, back = [tokens], [tokens]
    for _ in range(2):
        ahead.append(send(ahead[-1], onward))
        back.append(send(back[-1], backward))
    half = send(window(jnp.where(came_ahead, ahead[1], back[1]), over_chip), over)
    ahead.append(send(window(ahead[2], onward_chip), onward))
    back.append(send(window(back[2], backward_chip), backward))
    near = jnp.concatenate((tokens, ahead[1], back[1]), axis=0)
    middle = jnp.concatenate((ahead[2], back[2]), axis=0)
    last = jnp.concatenate((ahead[3], half), axis=0)
    near_beside = send(near, sibling)
    middle_beside = send(middle, sibling)
    last_beside = send(after(last, middle_beside), sibling)
    return [near, near_beside, middle, middle_beside, last, last_beside, back[3], send(back[3], sibling)]

def slab_origin(devices, device, number):
    chips = devices // 2
    number, flip = number % chips, number // chips
    hops = (number + 1) // 2 if number % 2 else -(number // 2)
    chip, core = device // 2, device % 2
    core = 1 - core if flip else core
    place = jnp.where(chip % 2 == 0, chip // 2, chips - 1 - chip // 2)
    place = (place - (1 - 2 * core) * hops + chips) % chips
    chip = jnp.where(2 * place < chips, 2 * place, 2 * (chips - 1 - place) + 1)
    return 2 * chip + core


def ring_kernel(devices, slots, device_ref, table_ref, *refs):
    groups = refs[:len(GROUPS)]
    out_ref, pair, tiles, zeros, out_sems, zero_sems = refs[len(GROUPS):]
    device = device_ref[0]
    slab, width = pair.shape[1] // devices, pair.shape[2]
    first = first_needed(devices, device // 2)

    def owned(partner):
        return table_ref[devices + tile_number(devices, device, partner)] == device

    def put(buffer, slot):
        return pltpu.make_async_copy(tiles.at[buffer], out_ref.at[slot], out_sems.at[buffer])

    def clear(slot):
        return pltpu.make_async_copy(zeros, out_ref.at[slot], zero_sems.at[slot])

    def load_block(partner, masked):
        parts = []
        for numbers, ref in zip(GROUPS, groups):
            place = partner
            if ref.shape[1] < devices * width:
                place = lax.rem(partner - first + devices, devices)
            group = ref[:, pl.ds(pl.multiple_of(place * width, 128), width)].astype(jnp.float32)
            for at, number in enumerate(numbers):
                part = group[at * slab:(at + 1) * slab]
                if masked:
                    row = lax.broadcasted_iota(jnp.int32, (slab, width), 0)
                    part = jnp.where(row < table_ref[slab_origin(devices, device, number)], part, 0.0)
                parts.append(part)
        pair[0 if masked else 1] = jnp.concatenate(parts, axis=0).astype(jnp.bfloat16)

    load_block(device, True)
    valid_count = table_ref[0]
    for at in range(1, devices):
        valid_count = valid_count + table_ref[at]
    scale = 1.0 / jnp.full((8, width), valid_count.astype(jnp.float32))

    def visit(partner, slot):
        mine = owned(partner)

        @pl.when(mine)
        def _():
            buffer = lax.rem(slot, BUFFERS)
            load_block(partner, False)

            @pl.when(slot >= BUFFERS)
            def _():
                put(buffer, slot - BUFFERS).wait()

            left = (partner <= device).astype(jnp.int32)
            for row in range(0, width, STRIP):
                rows = min(STRIP, width - row)
                strip = pl.ds(row, rows)
                product = lax.dot_general(
                    pair[left, :, row:row + rows], pair[1 - left], (((0,), (0,)), ((), ())),
                    preferred_element_type=jnp.float32,
                )
                tiles[buffer, strip, :] = product * scale[:1]
                pltpu.make_async_copy(
                    tiles.at[buffer, strip], out_ref.at[slot, strip], out_sems.at[buffer]
                ).start()

        return slot + mine.astype(jnp.int32)

    count = lax.fori_loop(0, devices, visit, jnp.int32(0))

    @pl.when(count < slots)
    def _():
        zeros[...] = jnp.zeros_like(zeros)

    def start_clear(slot, carry):
        clear(slot).start()
        return carry

    lax.fori_loop(count, slots, start_clear, 0)

    def drain(slot, carry):
        put(lax.rem(slot, BUFFERS), slot).wait()
        return carry

    lax.fori_loop(jnp.maximum(count - BUFFERS, 0), count, drain, 0)

    def end_clear(slot, carry):
        clear(slot).wait()
        return carry

    lax.fori_loop(count, slots, end_clear, 0)


def ring_form(tokens, slab_lengths, tile_owner, devices, device, slots):
    slab, units = tokens.shape
    width = units // devices
    groups = ring_gather(tokens, device, devices)
    table = jnp.concatenate([slab_lengths, tile_owner])
    return pl.pallas_call(
        functools.partial(ring_kernel, devices, slots),
        out_shape=jax.ShapeDtypeStruct((slots, width, width), jnp.float32),
        in_specs=[pl.BlockSpec(memory_space=pltpu.SMEM)] * 2
        + [pl.BlockSpec(memory_space=pltpu.VMEM)] * len(groups),
        out_specs=pl.BlockSpec(memory_space=pl.ANY),
        scratch_shapes=[
            pltpu.VMEM((2, slab * devices, width), jnp.bfloat16),
            pltpu.VMEM((BUFFERS, width, width), jnp.float32),
            pltpu.VMEM((width, width), jnp.float32),
            pltpu.SemaphoreType.DMA((BUFFERS,)),
            pltpu.SemaphoreType.DMA((slots,)),
        ],
        compiler_params=pltpu.CompilerParams(vmem_limit_bytes=32 * 1024 * 1024),
        cost_estimate=pl.CostEstimate(
            flops=2 * slots * slab * devices * width * width,
            bytes_accessed=4 * slots * width * width,
            transcendentals=0,
        ),
    )(device.reshape(1), table, *groups)


def per_device(tokens, slab_lengths, tile_owner):
    devices = lax.axis_size("col")
    device = lax.axis_index("col").astype(jnp.int32)
    slots = devices // 2 + devices // 8 + 1
    width = tokens.shape[1] // devices
    form = ring_form if devices == RING_DEVICES and width % 128 == 0 else gathered_form
    return form(tokens, slab_lengths, tile_owner, devices, device, slots)


def solution(mesh):
    return jax.shard_map(
        per_device,
        mesh=mesh,
        in_specs=(P(("grp", "col"), None), P("grp"), P()),
        out_specs=P(("grp", "col"), None, None),
        check_vma=False,
    )
```

```python
import functools

import jax
import jax.numpy as jnp
from jax import lax
from jax.experimental import pallas as pl
from jax.experimental.pallas import tpu as pltpu
from jax.sharding import PartitionSpec as P

BUFFERS = 4
STRIP = 256
RING_DEVICES = 16


def tile_number(devices, device, partner):
    low = jnp.minimum(device, partner)
    high = jnp.maximum(device, partner)
    return low * devices - low * (low - 1) // 2 + (high - low)


def gathered_kernel(
    devices, slots, owner_ref, device_ref, scale_ref, x_ref, mask_ref,
    out_ref, blocks, mask, tiles, zeros, in_sems, mask_sem, out_sems, zero_sems,
):
    device = device_ref[0]
    width = blocks.shape[2]

    def owned(partner):
        return owner_ref[tile_number(devices, device, partner)] == device

    def fetch(partner):
        return pltpu.make_async_copy(x_ref.at[partner], blocks.at[partner], in_sems.at[partner])

    def put(buffer, slot):
        return pltpu.make_async_copy(tiles.at[buffer], out_ref.at[slot], out_sems.at[buffer])

    def clear(slot):
        return pltpu.make_async_copy(zeros, out_ref.at[slot], zero_sems.at[slot])

    mask_copy = pltpu.make_async_copy(mask_ref, mask, mask_sem)
    mask_copy.start()
    fetch(device).start()

    def start_fetch(partner, count):
        mine = owned(partner)

        @pl.when(mine & (partner != device))
        def _():
            fetch(partner).start()

        return count + mine.astype(jnp.int32)

    count = lax.fori_loop(0, devices, start_fetch, jnp.int32(0))

    zeros[...] = jnp.zeros_like(zeros)

    def start_clear(slot, carry):
        clear(slot).start()
        return carry

    lax.fori_loop(count, slots, start_clear, 0)

    mask_copy.wait()
    fetch(device).wait()
    blocks[devices] = blocks[device] * mask[...]
    scale = scale_ref[0]

    def visit(partner, slot):
        mine = owned(partner)

        @pl.when(mine)
        def _():
            @pl.when(partner != device)
            def _():
                fetch(partner).wait()

            buffer = lax.rem(slot, BUFFERS)

            @pl.when(slot >= BUFFERS)
            def _():
                put(buffer, slot - BUFFERS).wait()

            left = jnp.where(partner <= device, partner, devices)
            right = jnp.where(partner <= device, devices, partner)
            product = lax.dot_general(
                blocks[left], blocks[right], (((0,), (0,)), ((), ())),
                preferred_element_type=jnp.float32,
            )
            tiles[buffer] = product * scale
            put(buffer, slot).start()

        return slot + mine.astype(jnp.int32)

    lax.fori_loop(0, devices, visit, jnp.int32(0))

    def drain(slot, carry):
        put(lax.rem(slot, BUFFERS), slot).wait()
        return carry

    lax.fori_loop(jnp.maximum(count - BUFFERS, 0), count, drain, 0)

    def end_clear(slot, carry):
        clear(slot).wait()
        return carry

    lax.fori_loop(count, slots, end_clear, 0)


def gathered_form(tokens, slab_lengths, tile_owner, devices, device, slots):
    slab, units = tokens.shape
    rows = slab * devices
    width = units // devices
    x = lax.all_gather(tokens, "col", axis=0, tiled=True)
    x = x.reshape(rows, devices, width).transpose(1, 0, 2)
    scale = 1.0 / jnp.sum(slab_lengths).astype(jnp.float32)
    valid = jnp.arange(slab, dtype=jnp.int32)[None, :] < slab_lengths[:, None]
    mask = jnp.broadcast_to(valid.reshape(rows, 1), (rows, width)).astype(jnp.bfloat16)
    return pl.pallas_call(
        functools.partial(gathered_kernel, devices, slots),
        out_shape=jax.ShapeDtypeStruct((slots, width, width), jnp.float32),
        in_specs=[pl.BlockSpec(memory_space=pltpu.SMEM)] * 3 + [pl.BlockSpec(memory_space=pl.ANY)] * 2,
        out_specs=pl.BlockSpec(memory_space=pl.ANY),
        scratch_shapes=[
            pltpu.VMEM((devices + 1, rows, width), jnp.bfloat16),
            pltpu.VMEM((rows, width), jnp.bfloat16),
            pltpu.VMEM((BUFFERS, width, width), jnp.float32),
            pltpu.VMEM((width, width), jnp.float32),
            pltpu.SemaphoreType.DMA((devices,)),
            pltpu.SemaphoreType.DMA,
            pltpu.SemaphoreType.DMA((BUFFERS,)),
            pltpu.SemaphoreType.DMA((slots,)),
        ],
        compiler_params=pltpu.CompilerParams(vmem_limit_bytes=50 * 1024 * 1024),
    )(tile_owner, device.reshape(1), scale.reshape(1), x, mask)


def ring_plan(devices):
    chips = devices // 2
    order = list(range(0, chips, 2)) + list(range(1, chips, 2))[::-1]
    place = {chip: at for at, chip in enumerate(order)}
    onward = []
    for device in range(devices):
        chip, core = divmod(device, 2)
        step = 1 if core == 0 else -1
        onward.append(order[(place[chip] + step) % chips] * 2 + core)
    backward = [onward.index(device) for device in range(devices)]
    return onward, backward


GROUPS = ((0, 1, 2), (8, 9, 10), (3, 4), (11, 12), (7, 15), (5,), (13,), (6,), (14,))


def first_needed(devices, chip):
    return (2 * chip - devices // 2 - devices // 8 + devices) % devices


def ring_gather(tokens, device, devices):
    onward, backward = ring_plan(devices)
    sibling = [device ^ 1 for device in range(devices)]
    over = [at ^ 12 if at // 4 in (0, 3) else at ^ 2 for at in range(devices)]

    def send(value, target):
        return lax.ppermute(value, "col", list(enumerate(target)))

    def after(value, *others):
        return lax.optimization_barrier((value, *others))[0]

    chip, core = device // 2, device % 2
    chips = devices // 2
    even = chip % 2 == 0
    next_chip = jnp.where(even, jnp.where(chip == chips - 2, chips - 1, chip + 2), jnp.where(chip == 1, 0, chip - 2))
    last_chip = jnp.where(even, jnp.where(chip == 0, 1, chip - 2), jnp.where(chip == chips - 1, chips - 2, chip + 2))
    onward_chip = jnp.where(core == 0, next_chip, last_chip)
    backward_chip = jnp.where(core == 0, last_chip, next_chip)
    over_chip = jnp.where((chip < 2) | (chip >= chips - 2), chip ^ 6, chip ^ 1)
    chip, core = device // 2, device % 2
    chips = devices // 2
    even = chip % 2 == 0
    next_chip = jnp.where(even, jnp.where(chip == chips - 2, chips - 1, chip + 2), jnp.where(chip == 1, 0, chip - 2))
    last_chip = jnp.where(even, jnp.where(chip == 0, 1, chip - 2), jnp.where(chip == chips - 1, chips - 2, chip + 2))
    onward_chip = jnp.where(core == 0, next_chip, last_chip)
    backward_chip = jnp.where(core == 0, last_chip, next_chip)
    over_chip = jnp.where((chip < 2) | (chip >= chips - 2), chip ^ 6, chip ^ 1)
    came_ahead = ((chip % 4 == 0) | (chip % 4 == 3)) == (core == 0)
    slab, units = tokens.shape
    needed = devices // 2 + devices // 8 + 2

    def window(value, chip):
        blocks = value.reshape(slab, devices, units // devices)
        blocks = jnp.concatenate([blocks, blocks], axis=1)
        blocks = lax.dynamic_slice_in_dim(blocks, first_needed(devices, chip), needed, axis=1)
        return blocks.reshape(slab, -1)

    ahead, back = [tokens], [tokens]
    for _ in range(2):
        ahead.append(send(ahead[-1], onward))
        back.append(send(back[-1], backward))
    near = jnp.concatenate((tokens, ahead[1], back[1]), axis=0)
    near_beside = send(near, sibling)
    ours = jnp.where(came_ahead, ahead[1], back[1])
    theirs = jnp.where(came_ahead, near_beside[2 * slab:], near_beside[slab:2 * slab])
    both = jnp.concatenate((window(ours, over_chip), window(theirs, over_chip)), axis=0)
    arrived = lax.ppermute(both, "col", [(at, over[at]) for at in range(1, devices, 2)])
    handed = lax.ppermute(arrived, "col", [(at, at - 1) for at in range(1, devices, 2)])
    half = jnp.concatenate((
        jnp.where(core == 1, arrived[:slab], handed[slab:]),
        jnp.where(core == 1, arrived[slab:], handed[:slab]),
    ), axis=0)
    ahead.append(send(window(after(ahead[2], both), onward_chip), onward))
    back.append(send(window(after(back[2], both), backward_chip), backward))
    middle = jnp.concatenate((ahead[2], back[2]), axis=0)
    middle_beside = send(middle, sibling)
    return [
        near, near_beside, middle, middle_beside, half,
        ahead[3], send(ahead[3], sibling), back[3], send(back[3], sibling),
    ]


def slab_origin(devices, device, number):
    chips = devices // 2
    number, flip = number % chips, number // chips
    hops = (number + 1) // 2 if number % 2 else -(number // 2)
    chip, core = device // 2, device % 2
    core = 1 - core if flip else core
    place = jnp.where(chip % 2 == 0, chip // 2, chips - 1 - chip // 2)
    place = (place - (1 - 2 * core) * hops + chips) % chips
    chip = jnp.where(2 * place < chips, 2 * place, 2 * (chips - 1 - place) + 1)
    return 2 * chip + core


def ring_kernel(devices, slots, device_ref, table_ref, *refs):
    groups = refs[:len(GROUPS)]
    out_ref, pair, tiles, zeros, out_sems, zero_sems = refs[len(GROUPS):]
    device = device_ref[0]
    slab, width = pair.shape[1] // devices, pair.shape[2]
    first = first_needed(devices, device // 2)

    def owned(partner):
        return table_ref[devices + tile_number(devices, device, partner)] == device

    def put(buffer, slot):
        return pltpu.make_async_copy(tiles.at[buffer], out_ref.at[slot], out_sems.at[buffer])

    def clear(slot):
        return pltpu.make_async_copy(zeros, out_ref.at[slot], zero_sems.at[slot])

    def load_block(partner, masked):
        parts = []
        for numbers, ref in zip(GROUPS, groups):
            place = partner
            if ref.shape[1] < devices * width:
                place = lax.rem(partner - first + devices, devices)
            group = ref[:, pl.ds(pl.multiple_of(place * width, 128), width)].astype(jnp.float32)
            for at, number in enumerate(numbers):
                part = group[at * slab:(at + 1) * slab]
                if masked:
                    row = lax.broadcasted_iota(jnp.int32, (slab, width), 0)
                    part = jnp.where(row < table_ref[slab_origin(devices, device, number)], part, 0.0)
                parts.append(part)
        pair[0 if masked else 1] = jnp.concatenate(parts, axis=0).astype(jnp.bfloat16)

    load_block(device, True)
    valid_count = table_ref[0]
    for at in range(1, devices):
        valid_count = valid_count + table_ref[at]
    scale = 1.0 / jnp.full((8, width), valid_count.astype(jnp.float32))

    def visit(partner, slot):
        mine = owned(partner)

        @pl.when(mine)
        def _():
            buffer = lax.rem(slot, BUFFERS)
            load_block(partner, False)

            @pl.when(slot >= BUFFERS)
            def _():
                put(buffer, slot - BUFFERS).wait()

            left = (partner <= device).astype(jnp.int32)
            for row in range(0, width, STRIP):
                rows = min(STRIP, width - row)
                strip = pl.ds(row, rows)
                product = lax.dot_general(
                    pair[left, :, row:row + rows], pair[1 - left], (((0,), (0,)), ((), ())),
                    preferred_element_type=jnp.float32,
                )
                tiles[buffer, strip, :] = product * scale[:1]
                pltpu.make_async_copy(
                    tiles.at[buffer, strip], out_ref.at[slot, strip], out_sems.at[buffer]
                ).start()

        return slot + mine.astype(jnp.int32)

    count = lax.fori_loop(0, devices, visit, jnp.int32(0))

    @pl.when(count < slots)
    def _():
        zeros[...] = jnp.zeros_like(zeros)

    def start_clear(slot, carry):
        clear(slot).start()
        return carry

    lax.fori_loop(count, slots, start_clear, 0)

    def drain(slot, carry):
        put(lax.rem(slot, BUFFERS), slot).wait()
        return carry

    lax.fori_loop(jnp.maximum(count - BUFFERS, 0), count, drain, 0)

    def end_clear(slot, carry):
        clear(slot).wait()
        return carry

    lax.fori_loop(count, slots, end_clear, 0)


def ring_form(tokens, slab_lengths, tile_owner, devices, device, slots):
    slab, units = tokens.shape
    width = units // devices
    groups = ring_gather(tokens, device, devices)
    table = jnp.concatenate([slab_lengths, tile_owner])
    return pl.pallas_call(
        functools.partial(ring_kernel, devices, slots),
        out_shape=jax.ShapeDtypeStruct((slots, width, width), jnp.float32),
        in_specs=[pl.BlockSpec(memory_space=pltpu.SMEM)] * 2
        + [pl.BlockSpec(memory_space=pltpu.VMEM)] * len(groups),
        out_specs=pl.BlockSpec(memory_space=pl.ANY),
        scratch_shapes=[
            pltpu.VMEM((2, slab * devices, width), jnp.bfloat16),
            pltpu.VMEM((BUFFERS, width, width), jnp.float32),
            pltpu.VMEM((width, width), jnp.float32),
            pltpu.SemaphoreType.DMA((BUFFERS,)),
            pltpu.SemaphoreType.DMA((slots,)),
        ],
        compiler_params=pltpu.CompilerParams(vmem_limit_bytes=32 * 1024 * 1024),
        cost_estimate=pl.CostEstimate(
            flops=2 * slots * slab * devices * width * width,
            bytes_accessed=4 * slots * width * width,
            transcendentals=0,
        ),
    )(device.reshape(1), table, *groups)


def per_device(tokens, slab_lengths, tile_owner):
    devices = lax.axis_size("col")
    device = lax.axis_index("col").astype(jnp.int32)
    slots = devices // 2 + devices // 8 + 1
    width = tokens.shape[1] // devices
    form = ring_form if devices == RING_DEVICES and width % 128 == 0 else gathered_form
    return form(tokens, slab_lengths, tile_owner, devices, device, slots)


def solution(mesh):
    return jax.shard_map(
        per_device,
        mesh=mesh,
        in_specs=(P(("grp", "col"), None), P("grp"), P()),
        out_specs=P(("grp", "col"), None, None),
        check_vma=False,
    )
```

```python
import functools

import jax
import jax.numpy as jnp
from jax import lax
from jax.experimental import pallas as pl
from jax.experimental.pallas import tpu as pltpu
from jax.sharding import PartitionSpec as P

BUFFERS = 4
STRIP = 256
RING_DEVICES = 16


def tile_number(devices, device, partner):
    low = jnp.minimum(device, partner)
    high = jnp.maximum(device, partner)
    return low * devices - low * (low - 1) // 2 + (high - low)


def gathered_kernel(
    devices, slots, owner_ref, device_ref, scale_ref, x_ref, mask_ref,
    out_ref, blocks, mask, tiles, zeros, in_sems, mask_sem, out_sems, zero_sems,
):
    device = device_ref[0]
    width = blocks.shape[2]

    def owned(partner):
        return owner_ref[tile_number(devices, device, partner)] == device

    def fetch(partner):
        return pltpu.make_async_copy(x_ref.at[partner], blocks.at[partner], in_sems.at[partner])

    def put(buffer, slot):
        return pltpu.make_async_copy(tiles.at[buffer], out_ref.at[slot], out_sems.at[buffer])

    def clear(slot):
        return pltpu.make_async_copy(zeros, out_ref.at[slot], zero_sems.at[slot])

    mask_copy = pltpu.make_async_copy(mask_ref, mask, mask_sem)
    mask_copy.start()
    fetch(device).start()

    def start_fetch(partner, count):
        mine = owned(partner)

        @pl.when(mine & (partner != device))
        def _():
            fetch(partner).start()

        return count + mine.astype(jnp.int32)

    count = lax.fori_loop(0, devices, start_fetch, jnp.int32(0))

    zeros[...] = jnp.zeros_like(zeros)

    def start_clear(slot, carry):
        clear(slot).start()
        return carry

    lax.fori_loop(count, slots, start_clear, 0)

    mask_copy.wait()
    fetch(device).wait()
    blocks[devices] = blocks[device] * mask[...]
    scale = scale_ref[0]

    def visit(partner, slot):
        mine = owned(partner)

        @pl.when(mine)
        def _():
            @pl.when(partner != device)
            def _():
                fetch(partner).wait()

            buffer = lax.rem(slot, BUFFERS)

            @pl.when(slot >= BUFFERS)
            def _():
                put(buffer, slot - BUFFERS).wait()

            left = jnp.where(partner <= device, partner, devices)
            right = jnp.where(partner <= device, devices, partner)
            product = lax.dot_general(
                blocks[left], blocks[right], (((0,), (0,)), ((), ())),
                preferred_element_type=jnp.float32,
            )
            tiles[buffer] = product * scale
            put(buffer, slot).start()

        return slot + mine.astype(jnp.int32)

    lax.fori_loop(0, devices, visit, jnp.int32(0))

    def drain(slot, carry):
        put(lax.rem(slot, BUFFERS), slot).wait()
        return carry

    lax.fori_loop(jnp.maximum(count - BUFFERS, 0), count, drain, 0)

    def end_clear(slot, carry):
        clear(slot).wait()
        return carry

    lax.fori_loop(count, slots, end_clear, 0)


def gathered_form(tokens, slab_lengths, tile_owner, devices, device, slots):
    slab, units = tokens.shape
    rows = slab * devices
    width = units // devices
    x = lax.all_gather(tokens, "col", axis=0, tiled=True)
    x = x.reshape(rows, devices, width).transpose(1, 0, 2)
    scale = 1.0 / jnp.sum(slab_lengths).astype(jnp.float32)
    valid = jnp.arange(slab, dtype=jnp.int32)[None, :] < slab_lengths[:, None]
    mask = jnp.broadcast_to(valid.reshape(rows, 1), (rows, width)).astype(jnp.bfloat16)
    return pl.pallas_call(
        functools.partial(gathered_kernel, devices, slots),
        out_shape=jax.ShapeDtypeStruct((slots, width, width), jnp.float32),
        in_specs=[pl.BlockSpec(memory_space=pltpu.SMEM)] * 3 + [pl.BlockSpec(memory_space=pl.ANY)] * 2,
        out_specs=pl.BlockSpec(memory_space=pl.ANY),
        scratch_shapes=[
            pltpu.VMEM((devices + 1, rows, width), jnp.bfloat16),
            pltpu.VMEM((rows, width), jnp.bfloat16),
            pltpu.VMEM((BUFFERS, width, width), jnp.float32),
            pltpu.VMEM((width, width), jnp.float32),
            pltpu.SemaphoreType.DMA((devices,)),
            pltpu.SemaphoreType.DMA,
            pltpu.SemaphoreType.DMA((BUFFERS,)),
            pltpu.SemaphoreType.DMA((slots,)),
        ],
        compiler_params=pltpu.CompilerParams(vmem_limit_bytes=50 * 1024 * 1024),
    )(tile_owner, device.reshape(1), scale.reshape(1), x, mask)


def ring_plan(devices):
    chips = devices // 2
    order = list(range(0, chips, 2)) + list(range(1, chips, 2))[::-1]
    place = {chip: at for at, chip in enumerate(order)}
    onward = []
    for device in range(devices):
        chip, core = divmod(device, 2)
        step = 1 if core == 0 else -1
        onward.append(order[(place[chip] + step) % chips] * 2 + core)
    backward = [onward.index(device) for device in range(devices)]
    return onward, backward


GROUPS = ((0, 1, 2), (8, 9, 10), (3, 4), (11, 12), (5, 6), (13, 14), (7,), (15,))


def first_needed(devices, chip):
    return (2 * chip - devices // 2 - devices // 8 + devices) % devices


def ring_gather(tokens, device, devices):
    onward, backward = ring_plan(devices)
    sibling = [device ^ 1 for device in range(devices)]
    over = [at ^ 12 if at // 4 in (0, 3) else at ^ 2 for at in range(devices)]

    def send(value, target):
        return lax.ppermute(value, "col", list(enumerate(target)))

    def after(value, *others):
        return lax.optimization_barrier((value, *others))[0]

    chip, core = device // 2, device % 2
    chips = devices // 2
    even = chip % 2 == 0
    next_chip = jnp.where(even, jnp.where(chip == chips - 2, chips - 1, chip + 2), jnp.where(chip == 1, 0, chip - 2))
    last_chip = jnp.where(even, jnp.where(chip == 0, 1, chip - 2), jnp.where(chip == chips - 1, chips - 2, chip + 2))
    onward_chip = jnp.where(core == 0, next_chip, last_chip)
    backward_chip = jnp.where(core == 0, last_chip, next_chip)
    over_chip = jnp.where((chip < 2) | (chip >= chips - 2), chip ^ 6, chip ^ 1)
    chip, core = device // 2, device % 2
    chips = devices // 2
    even = chip % 2 == 0
    next_chip = jnp.where(even, jnp.where(chip == chips - 2, chips - 1, chip + 2), jnp.where(chip == 1, 0, chip - 2))
    last_chip = jnp.where(even, jnp.where(chip == 0, 1, chip - 2), jnp.where(chip == chips - 1, chips - 2, chip + 2))
    onward_chip = jnp.where(core == 0, next_chip, last_chip)
    backward_chip = jnp.where(core == 0, last_chip, next_chip)
    over_chip = jnp.where((chip < 2) | (chip >= chips - 2), chip ^ 6, chip ^ 1)
    came_ahead = ((chip % 4 == 0) | (chip % 4 == 3)) == (core == 0)
    slab, units = tokens.shape
    needed = devices // 2 + devices // 8 + 2

    def window(value, chip):
        blocks = value.reshape(slab, devices, units // devices)
        blocks = jnp.concatenate([blocks, blocks], axis=1)
        blocks = lax.dynamic_slice_in_dim(blocks, first_needed(devices, chip), needed, axis=1)
        return blocks.reshape(slab, -1)

    ahead, back = [tokens], [tokens]
    for _ in range(2):
        ahead.append(send(ahead[-1], onward))
        back.append(send(back[-1], backward))
    ahead.append(send(window(ahead[2], onward_chip), onward))
    back.append(send(window(back[2], backward_chip), backward))
    held = after(jnp.where(came_ahead, ahead[1], back[1]), ahead[2], back[2])
    half = send(window(held, over_chip), over)
    groups = []
    for group in ((tokens, ahead[1], back[1]), (ahead[2], back[2]), (ahead[3], back[3]), (half,)):
        group = jnp.concatenate(group, axis=0)
        groups += [group, send(group, sibling)]
    return groups


def slab_origin(devices, device, number):
    chips = devices // 2
    number, flip = number % chips, number // chips
    hops = (number + 1) // 2 if number % 2 else -(number // 2)
    chip, core = device // 2, device % 2
    core = 1 - core if flip else core
    place = jnp.where(chip % 2 == 0, chip // 2, chips - 1 - chip // 2)
    place = (place - (1 - 2 * core) * hops + chips) % chips
    chip = jnp.where(2 * place < chips, 2 * place, 2 * (chips - 1 - place) + 1)
    return 2 * chip + core


def ring_kernel(devices, slots, device_ref, table_ref, *refs):
    groups = refs[:len(GROUPS)]
    out_ref, pair, tiles, zeros, out_sems, zero_sems = refs[len(GROUPS):]
    device = device_ref[0]
    slab, width = pair.shape[1] // devices, pair.shape[2]
    first = first_needed(devices, device // 2)

    def owned(partner):
        return table_ref[devices + tile_number(devices, device, partner)] == device

    def put(buffer, slot):
        return pltpu.make_async_copy(tiles.at[buffer], out_ref.at[slot], out_sems.at[buffer])

    def clear(slot):
        return pltpu.make_async_copy(zeros, out_ref.at[slot], zero_sems.at[slot])

    def load_block(partner, masked):
        parts = []
        for numbers, ref in zip(GROUPS, groups):
            place = partner
            if ref.shape[1] < devices * width:
                place = lax.rem(partner - first + devices, devices)
            group = ref[:, pl.ds(pl.multiple_of(place * width, 128), width)].astype(jnp.float32)
            for at, number in enumerate(numbers):
                part = group[at * slab:(at + 1) * slab]
                if masked:
                    row = lax.broadcasted_iota(jnp.int32, (slab, width), 0)
                    part = jnp.where(row < table_ref[slab_origin(devices, device, number)], part, 0.0)
                parts.append(part)
        pair[0 if masked else 1] = jnp.concatenate(parts, axis=0).astype(jnp.bfloat16)

    load_block(device, True)
    valid_count = table_ref[0]
    for at in range(1, devices):
        valid_count = valid_count + table_ref[at]
    scale = 1.0 / jnp.full((8, width), valid_count.astype(jnp.float32))

    def visit(partner, slot):
        mine = owned(partner)

        @pl.when(mine)
        def _():
            buffer = lax.rem(slot, BUFFERS)
            load_block(partner, False)

            @pl.when(slot >= BUFFERS)
            def _():
                put(buffer, slot - BUFFERS).wait()

            left = (partner <= device).astype(jnp.int32)
            for row in range(0, width, STRIP):
                rows = min(STRIP, width - row)
                strip = pl.ds(row, rows)
                product = lax.dot_general(
                    pair[left, :, row:row + rows], pair[1 - left], (((0,), (0,)), ((), ())),
                    preferred_element_type=jnp.float32,
                )
                tiles[buffer, strip, :] = product * scale[:1]
                pltpu.make_async_copy(
                    tiles.at[buffer, strip], out_ref.at[slot, strip], out_sems.at[buffer]
                ).start()

        return slot + mine.astype(jnp.int32)

    count = lax.fori_loop(0, devices, visit, jnp.int32(0))

    @pl.when(count < slots)
    def _():
        zeros[...] = jnp.zeros_like(zeros)

    def start_clear(slot, carry):
        clear(slot).start()
        return carry

    lax.fori_loop(count, slots, start_clear, 0)

    def drain(slot, carry):
        put(lax.rem(slot, BUFFERS), slot).wait()
        return carry

    lax.fori_loop(jnp.maximum(count - BUFFERS, 0), count, drain, 0)

    def end_clear(slot, carry):
        clear(slot).wait()
        return carry

    lax.fori_loop(count, slots, end_clear, 0)


def ring_form(tokens, slab_lengths, tile_owner, devices, device, slots):
    slab, units = tokens.shape
    width = units // devices
    groups = ring_gather(tokens, device, devices)
    table = jnp.concatenate([slab_lengths, tile_owner])
    return pl.pallas_call(
        functools.partial(ring_kernel, devices, slots),
        out_shape=jax.ShapeDtypeStruct((slots, width, width), jnp.float32),
        in_specs=[pl.BlockSpec(memory_space=pltpu.SMEM)] * 2
        + [pl.BlockSpec(memory_space=pltpu.VMEM)] * len(groups),
        out_specs=pl.BlockSpec(memory_space=pl.ANY),
        scratch_shapes=[
            pltpu.VMEM((2, slab * devices, width), jnp.bfloat16),
            pltpu.VMEM((BUFFERS, width, width), jnp.float32),
            pltpu.VMEM((width, width), jnp.float32),
            pltpu.SemaphoreType.DMA((BUFFERS,)),
            pltpu.SemaphoreType.DMA((slots,)),
        ],
        compiler_params=pltpu.CompilerParams(vmem_limit_bytes=32 * 1024 * 1024),
        cost_estimate=pl.CostEstimate(
            flops=2 * slots * slab * devices * width * width,
            bytes_accessed=4 * slots * width * width,
            transcendentals=0,
        ),
    )(device.reshape(1), table, *groups)


def per_device(tokens, slab_lengths, tile_owner):
    devices = lax.axis_size("col")
    device = lax.axis_index("col").astype(jnp.int32)
    slots = devices // 2 + devices // 8 + 1
    width = tokens.shape[1] // devices
    form = ring_form if devices == RING_DEVICES and width % 128 == 0 else gathered_form
    return form(tokens, slab_lengths, tile_owner, devices, device, slots)


def solution(mesh):
    return jax.shard_map(
        per_device,
        mesh=mesh,
        in_specs=(P(("grp", "col"), None), P("grp"), P()),
        out_specs=P(("grp", "col"), None, None),
        check_vma=False,
    )
```

```python
import functools

import jax
import jax.numpy as jnp
from jax import lax
from jax.experimental import pallas as pl
from jax.experimental.pallas import tpu as pltpu
from jax.sharding import PartitionSpec as P

BUFFERS = 4
STRIP = 256
RING_DEVICES = 16


def tile_number(devices, device, partner):
    low = jnp.minimum(device, partner)
    high = jnp.maximum(device, partner)
    return low * devices - low * (low - 1) // 2 + (high - low)


def gathered_kernel(
    devices, slots, owner_ref, device_ref, scale_ref, x_ref, mask_ref,
    out_ref, blocks, mask, tiles, zeros, in_sems, mask_sem, out_sems, zero_sems,
):
    device = device_ref[0]
    width = blocks.shape[2]

    def owned(partner):
        return owner_ref[tile_number(devices, device, partner)] == device

    def fetch(partner):
        return pltpu.make_async_copy(x_ref.at[partner], blocks.at[partner], in_sems.at[partner])

    def put(buffer, slot):
        return pltpu.make_async_copy(tiles.at[buffer], out_ref.at[slot], out_sems.at[buffer])

    def clear(slot):
        return pltpu.make_async_copy(zeros, out_ref.at[slot], zero_sems.at[slot])

    mask_copy = pltpu.make_async_copy(mask_ref, mask, mask_sem)
    mask_copy.start()
    fetch(device).start()

    def start_fetch(partner, count):
        mine = owned(partner)

        @pl.when(mine & (partner != device))
        def _():
            fetch(partner).start()

        return count + mine.astype(jnp.int32)

    count = lax.fori_loop(0, devices, start_fetch, jnp.int32(0))

    zeros[...] = jnp.zeros_like(zeros)

    def start_clear(slot, carry):
        clear(slot).start()
        return carry

    lax.fori_loop(count, slots, start_clear, 0)

    mask_copy.wait()
    fetch(device).wait()
    blocks[devices] = blocks[device] * mask[...]
    scale = scale_ref[0]

    def visit(partner, slot):
        mine = owned(partner)

        @pl.when(mine)
        def _():
            @pl.when(partner != device)
            def _():
                fetch(partner).wait()

            buffer = lax.rem(slot, BUFFERS)

            @pl.when(slot >= BUFFERS)
            def _():
                put(buffer, slot - BUFFERS).wait()

            left = jnp.where(partner <= device, partner, devices)
            right = jnp.where(partner <= device, devices, partner)
            product = lax.dot_general(
                blocks[left], blocks[right], (((0,), (0,)), ((), ())),
                preferred_element_type=jnp.float32,
            )
            tiles[buffer] = product * scale
            put(buffer, slot).start()

        return slot + mine.astype(jnp.int32)

    lax.fori_loop(0, devices, visit, jnp.int32(0))

    def drain(slot, carry):
        put(lax.rem(slot, BUFFERS), slot).wait()
        return carry

    lax.fori_loop(jnp.maximum(count - BUFFERS, 0), count, drain, 0)

    def end_clear(slot, carry):
        clear(slot).wait()
        return carry

    lax.fori_loop(count, slots, end_clear, 0)


def gathered_form(tokens, slab_lengths, tile_owner, devices, device, slots):
    slab, units = tokens.shape
    rows = slab * devices
    width = units // devices
    x = lax.all_gather(tokens, "col", axis=0, tiled=True)
    x = x.reshape(rows, devices, width).transpose(1, 0, 2)
    scale = 1.0 / jnp.sum(slab_lengths).astype(jnp.float32)
    valid = jnp.arange(slab, dtype=jnp.int32)[None, :] < slab_lengths[:, None]
    mask = jnp.broadcast_to(valid.reshape(rows, 1), (rows, width)).astype(jnp.bfloat16)
    return pl.pallas_call(
        functools.partial(gathered_kernel, devices, slots),
        out_shape=jax.ShapeDtypeStruct((slots, width, width), jnp.float32),
        in_specs=[pl.BlockSpec(memory_space=pltpu.SMEM)] * 3 + [pl.BlockSpec(memory_space=pl.ANY)] * 2,
        out_specs=pl.BlockSpec(memory_space=pl.ANY),
        scratch_shapes=[
            pltpu.VMEM((devices + 1, rows, width), jnp.bfloat16),
            pltpu.VMEM((rows, width), jnp.bfloat16),
            pltpu.VMEM((BUFFERS, width, width), jnp.float32),
            pltpu.VMEM((width, width), jnp.float32),
            pltpu.SemaphoreType.DMA((devices,)),
            pltpu.SemaphoreType.DMA,
            pltpu.SemaphoreType.DMA((BUFFERS,)),
            pltpu.SemaphoreType.DMA((slots,)),
        ],
        compiler_params=pltpu.CompilerParams(vmem_limit_bytes=50 * 1024 * 1024),
    )(tile_owner, device.reshape(1), scale.reshape(1), x, mask)


def ring_plan(devices):
    chips = devices // 2
    order = list(range(0, chips, 2)) + list(range(1, chips, 2))[::-1]
    place = {chip: at for at, chip in enumerate(order)}
    onward = []
    for device in range(devices):
        chip, core = divmod(device, 2)
        step = 1 if core == 0 else -1
        onward.append(order[(place[chip] + step) % chips] * 2 + core)
    backward = [onward.index(device) for device in range(devices)]
    return onward, backward


GROUPS = ((0, 1, 2), (8, 9, 10), (3, 4), (11, 12), (5, 7), (13, 15), (6,), (14,))


def first_needed(devices, chip):
    return (2 * chip - devices // 2 - devices // 8 + devices) % devices


def ring_gather(tokens, device, devices):
    onward, backward = ring_plan(devices)
    sibling = [device ^ 1 for device in range(devices)]
    over = [at ^ 12 if at // 4 in (0, 3) else at ^ 2 for at in range(devices)]

    def send(value, target):
        return lax.ppermute(value, "col", list(enumerate(target)))

    def after(value, *others):
        return lax.optimization_barrier((value, *others))[0]

    chip, core = device // 2, device % 2
    chips = devices // 2
    even = chip % 2 == 0
    next_chip = jnp.where(even, jnp.where(chip == chips - 2, chips - 1, chip + 2), jnp.where(chip == 1, 0, chip - 2))
    last_chip = jnp.where(even, jnp.where(chip == 0, 1, chip - 2), jnp.where(chip == chips - 1, chips - 2, chip + 2))
    onward_chip = jnp.where(core == 0, next_chip, last_chip)
    backward_chip = jnp.where(core == 0, last_chip, next_chip)
    over_chip = jnp.where((chip < 2) | (chip >= chips - 2), chip ^ 6, chip ^ 1)
    chip, core = device // 2, device % 2
    chips = devices // 2
    even = chip % 2 == 0
    next_chip = jnp.where(even, jnp.where(chip == chips - 2, chips - 1, chip + 2), jnp.where(chip == 1, 0, chip - 2))
    last_chip = jnp.where(even, jnp.where(chip == 0, 1, chip - 2), jnp.where(chip == chips - 1, chips - 2, chip + 2))
    onward_chip = jnp.where(core == 0, next_chip, last_chip)
    backward_chip = jnp.where(core == 0, last_chip, next_chip)
    over_chip = jnp.where((chip < 2) | (chip >= chips - 2), chip ^ 6, chip ^ 1)
    came_ahead = ((chip % 4 == 0) | (chip % 4 == 3)) == (core == 0)
    slab, units = tokens.shape
    needed = devices // 2 + devices // 8 + 2

    def window(value, chip):
        blocks = value.reshape(slab, devices, units // devices)
        blocks = jnp.concatenate([blocks, blocks], axis=1)
        blocks = lax.dynamic_slice_in_dim(blocks, first_needed(devices, chip), needed, axis=1)
        return blocks.reshape(slab, -1)

    ahead, back = [tokens], [tokens]
    for _ in range(2):
        ahead.append(send(ahead[-1], onward))
        back.append(send(back[-1], backward))
    half = send(window(jnp.where(came_ahead, ahead[1], back[1]), over_chip), over)
    ahead.append(send(window(ahead[2], onward_chip), onward))
    back.append(send(window(back[2], backward_chip), backward))
    near = jnp.concatenate((tokens, ahead[1], back[1]), axis=0)
    middle = jnp.concatenate((ahead[2], back[2]), axis=0)
    last = jnp.concatenate((ahead[3], half), axis=0)
    near_beside = send(near, sibling)
    middle_beside = send(jnp.concatenate((window(ahead[2], chip), window(back[2], chip)), axis=0), sibling)
    last_beside = send(after(last, middle_beside), sibling)
    return [near, near_beside, middle, middle_beside, last, last_beside, back[3], send(back[3], sibling)]


def slab_origin(devices, device, number):
    chips = devices // 2
    number, flip = number % chips, number // chips
    hops = (number + 1) // 2 if number % 2 else -(number // 2)
    chip, core = device // 2, device % 2
    core = 1 - core if flip else core
    place = jnp.where(chip % 2 == 0, chip // 2, chips - 1 - chip // 2)
    place = (place - (1 - 2 * core) * hops + chips) % chips
    chip = jnp.where(2 * place < chips, 2 * place, 2 * (chips - 1 - place) + 1)
    return 2 * chip + core


def ring_kernel(devices, slots, table_ref, *refs):
    groups = refs[:len(GROUPS)]
    out_ref, pair, tiles, zeros, out_sems, zero_sems = refs[len(GROUPS):]
    device = table_ref[table_ref.shape[0] - 1]
    slab, width = pair.shape[1] // devices, pair.shape[2]
    first = first_needed(devices, device // 2)

    def owned(partner):
        return table_ref[devices + tile_number(devices, device, partner)] == device

    def put(buffer, slot):
        return pltpu.make_async_copy(tiles.at[buffer], out_ref.at[slot], out_sems.at[buffer])

    def clear(slot):
        return pltpu.make_async_copy(zeros, out_ref.at[slot], zero_sems.at[slot])

    def load_block(partner, masked):
        parts = []
        for numbers, ref in zip(GROUPS, groups):
            place = partner
            if ref.shape[1] < devices * width:
                place = lax.rem(partner - first + devices, devices)
            group = ref[:, pl.ds(pl.multiple_of(place * width, 128), width)].astype(jnp.float32)
            for at, number in enumerate(numbers):
                part = group[at * slab:(at + 1) * slab]
                if masked:
                    row = lax.broadcasted_iota(jnp.int32, (slab, width), 0)
                    part = jnp.where(row < table_ref[slab_origin(devices, device, number)], part, 0.0)
                parts.append(part)
        pair[0 if masked else 1] = jnp.concatenate(parts, axis=0).astype(jnp.bfloat16)

    load_block(device, True)
    valid_count = table_ref[0]
    for at in range(1, devices):
        valid_count = valid_count + table_ref[at]
    scale = 1.0 / jnp.full((8, width), valid_count.astype(jnp.float32))

    def visit(partner, slot):
        mine = owned(partner)

        @pl.when(mine)
        def _():
            buffer = lax.rem(slot, BUFFERS)
            load_block(partner, False)

            @pl.when(slot >= BUFFERS)
            def _():
                put(buffer, slot - BUFFERS).wait()

            left = (partner <= device).astype(jnp.int32)
            for row in range(0, width, STRIP):
                rows = min(STRIP, width - row)
                strip = pl.ds(row, rows)
                product = lax.dot_general(
                    pair[left, :, row:row + rows], pair[1 - left], (((0,), (0,)), ((), ())),
                    preferred_element_type=jnp.float32,
                )
                tiles[buffer, strip, :] = product * scale[:1]
                pltpu.make_async_copy(
                    tiles.at[buffer, strip], out_ref.at[slot, strip], out_sems.at[buffer]
                ).start()

        return slot + mine.astype(jnp.int32)

    count = lax.fori_loop(0, devices, visit, jnp.int32(0))

    @pl.when(count < slots)
    def _():
        zeros[...] = jnp.zeros_like(zeros)

    def start_clear(slot, carry):
        clear(slot).start()
        return carry

    lax.fori_loop(count, slots, start_clear, 0)

    def drain(slot, carry):
        put(lax.rem(slot, BUFFERS), slot).wait()
        return carry

    lax.fori_loop(jnp.maximum(count - BUFFERS, 0), count, drain, 0)

    def end_clear(slot, carry):
        clear(slot).wait()
        return carry

    lax.fori_loop(count, slots, end_clear, 0)


def ring_form(tokens, slab_lengths, tile_owner, devices, device, slots):
    slab, units = tokens.shape
    width = units // devices
    groups = ring_gather(tokens, device, devices)
    table = jnp.concatenate([slab_lengths, tile_owner, device.reshape(1)])
    return pl.pallas_call(
        functools.partial(ring_kernel, devices, slots),
        out_shape=jax.ShapeDtypeStruct((slots, width, width), jnp.float32),
        in_specs=[pl.BlockSpec(memory_space=pltpu.SMEM)]
        + [pl.BlockSpec(memory_space=pltpu.VMEM)] * len(groups),
        out_specs=pl.BlockSpec(memory_space=pl.ANY),
        scratch_shapes=[
            pltpu.VMEM((2, slab * devices, width), jnp.bfloat16),
            pltpu.VMEM((BUFFERS, width, width), jnp.float32),
            pltpu.VMEM((width, width), jnp.float32),
            pltpu.SemaphoreType.DMA((BUFFERS,)),
            pltpu.SemaphoreType.DMA((slots,)),
        ],
        compiler_params=pltpu.CompilerParams(vmem_limit_bytes=32 * 1024 * 1024),
        cost_estimate=pl.CostEstimate(
            flops=2 * slots * slab * devices * width * width,
            bytes_accessed=4 * slots * width * width,
            transcendentals=0,
        ),
    )(table, *groups)


def per_device(tokens, slab_lengths, tile_owner):
    devices = lax.axis_size("col")
    device = lax.axis_index("col").astype(jnp.int32)
    slots = devices // 2 + devices // 8 + 1
    width = tokens.shape[1] // devices
    form = ring_form if devices == RING_DEVICES and width % 128 == 0 else gathered_form
    return form(tokens, slab_lengths, tile_owner, devices, device, slots)


def solution(mesh):
    return jax.shard_map(
        per_device,
        mesh=mesh,
        in_specs=(P(("grp", "col"), None), P("grp"), P()),
        out_specs=P(("grp", "col"), None, None),
        check_vma=False,
    )
```

```python
import functools

import jax
import jax.numpy as jnp
from jax import lax
from jax.experimental import pallas as pl
from jax.experimental.pallas import tpu as pltpu
from jax.sharding import PartitionSpec as P

BUFFERS = 4
STRIP = 256
RING_DEVICES = 16


def tile_number(devices, device, partner):
    low = jnp.minimum(device, partner)
    high = jnp.maximum(device, partner)
    return low * devices - low * (low - 1) // 2 + (high - low)


def gathered_kernel(
    devices, slots, owner_ref, device_ref, scale_ref, x_ref, mask_ref,
    out_ref, blocks, mask, tiles, zeros, in_sems, mask_sem, out_sems, zero_sems,
):
    device = device_ref[0]
    width = blocks.shape[2]

    def owned(partner):
        return owner_ref[tile_number(devices, device, partner)] == device

    def fetch(partner):
        return pltpu.make_async_copy(x_ref.at[partner], blocks.at[partner], in_sems.at[partner])

    def put(buffer, slot):
        return pltpu.make_async_copy(tiles.at[buffer], out_ref.at[slot], out_sems.at[buffer])

    def clear(slot):
        return pltpu.make_async_copy(zeros, out_ref.at[slot], zero_sems.at[slot])

    mask_copy = pltpu.make_async_copy(mask_ref, mask, mask_sem)
    mask_copy.start()
    fetch(device).start()

    def start_fetch(partner, count):
        mine = owned(partner)

        @pl.when(mine & (partner != device))
        def _():
            fetch(partner).start()

        return count + mine.astype(jnp.int32)

    count = lax.fori_loop(0, devices, start_fetch, jnp.int32(0))

    zeros[...] = jnp.zeros_like(zeros)

    def start_clear(slot, carry):
        clear(slot).start()
        return carry

    lax.fori_loop(count, slots, start_clear, 0)

    mask_copy.wait()
    fetch(device).wait()
    blocks[devices] = blocks[device] * mask[...]
    scale = scale_ref[0]

    def visit(partner, slot):
        mine = owned(partner)

        @pl.when(mine)
        def _():
            @pl.when(partner != device)
            def _():
                fetch(partner).wait()

            buffer = lax.rem(slot, BUFFERS)

            @pl.when(slot >= BUFFERS)
            def _():
                put(buffer, slot - BUFFERS).wait()

            left = jnp.where(partner <= device, partner, devices)
            right = jnp.where(partner <= device, devices, partner)
            product = lax.dot_general(
                blocks[left], blocks[right], (((0,), (0,)), ((), ())),
                preferred_element_type=jnp.float32,
            )
            tiles[buffer] = product * scale
            put(buffer, slot).start()

        return slot + mine.astype(jnp.int32)

    lax.fori_loop(0, devices, visit, jnp.int32(0))

    def drain(slot, carry):
        put(lax.rem(slot, BUFFERS), slot).wait()
        return carry

    lax.fori_loop(jnp.maximum(count - BUFFERS, 0), count, drain, 0)

    def end_clear(slot, carry):
        clear(slot).wait()
        return carry

    lax.fori_loop(count, slots, end_clear, 0)


def gathered_form(tokens, slab_lengths, tile_owner, devices, device, slots):
    slab, units = tokens.shape
    rows = slab * devices
    width = units // devices
    x = lax.all_gather(tokens, "col", axis=0, tiled=True)
    x = x.reshape(rows, devices, width).transpose(1, 0, 2)
    scale = 1.0 / jnp.sum(slab_lengths).astype(jnp.float32)
    valid = jnp.arange(slab, dtype=jnp.int32)[None, :] < slab_lengths[:, None]
    mask = jnp.broadcast_to(valid.reshape(rows, 1), (rows, width)).astype(jnp.bfloat16)
    return pl.pallas_call(
        functools.partial(gathered_kernel, devices, slots),
        out_shape=jax.ShapeDtypeStruct((slots, width, width), jnp.float32),
        in_specs=[pl.BlockSpec(memory_space=pltpu.SMEM)] * 3 + [pl.BlockSpec(memory_space=pl.ANY)] * 2,
        out_specs=pl.BlockSpec(memory_space=pl.ANY),
        scratch_shapes=[
            pltpu.VMEM((devices + 1, rows, width), jnp.bfloat16),
            pltpu.VMEM((rows, width), jnp.bfloat16),
            pltpu.VMEM((BUFFERS, width, width), jnp.float32),
            pltpu.VMEM((width, width), jnp.float32),
            pltpu.SemaphoreType.DMA((devices,)),
            pltpu.SemaphoreType.DMA,
            pltpu.SemaphoreType.DMA((BUFFERS,)),
            pltpu.SemaphoreType.DMA((slots,)),
        ],
        compiler_params=pltpu.CompilerParams(vmem_limit_bytes=50 * 1024 * 1024),
    )(tile_owner, device.reshape(1), scale.reshape(1), x, mask)


def ring_plan(devices):
    chips = devices // 2
    order = list(range(0, chips, 2)) + list(range(1, chips, 2))[::-1]
    place = {chip: at for at, chip in enumerate(order)}
    onward = []
    for device in range(devices):
        chip, core = divmod(device, 2)
        step = 1 if core == 0 else -1
        onward.append(order[(place[chip] + step) % chips] * 2 + core)
    backward = [onward.index(device) for device in range(devices)]
    return onward, backward


GROUPS = ((0, 1, 2), (8, 9, 10), (3, 4), (11, 12), (5, 7), (13, 15), (6,), (14,))


def first_needed(devices, chip):
    return (2 * chip - devices // 2 - devices // 8 + devices) % devices


def ring_gather(tokens, device, devices):
    onward, backward = ring_plan(devices)
    sibling = [device ^ 1 for device in range(devices)]
    over = [at ^ 12 if at // 4 in (0, 3) else at ^ 2 for at in range(devices)]

    def send(value, target):
        return lax.ppermute(value, "col", list(enumerate(target)))

    def after(value, *others):
        return lax.optimization_barrier((value, *others))[0]

    chip, core = device // 2, device % 2
    chips = devices // 2
    even = chip % 2 == 0
    next_chip = jnp.where(even, jnp.where(chip == chips - 2, chips - 1, chip + 2), jnp.where(chip == 1, 0, chip - 2))
    last_chip = jnp.where(even, jnp.where(chip == 0, 1, chip - 2), jnp.where(chip == chips - 1, chips - 2, chip + 2))
    onward_chip = jnp.where(core == 0, next_chip, last_chip)
    backward_chip = jnp.where(core == 0, last_chip, next_chip)
    over_chip = jnp.where((chip < 2) | (chip >= chips - 2), chip ^ 6, chip ^ 1)
    chip, core = device // 2, device % 2
    chips = devices // 2
    even = chip % 2 == 0
    next_chip = jnp.where(even, jnp.where(chip == chips - 2, chips - 1, chip + 2), jnp.where(chip == 1, 0, chip - 2))
    last_chip = jnp.where(even, jnp.where(chip == 0, 1, chip - 2), jnp.where(chip == chips - 1, chips - 2, chip + 2))
    onward_chip = jnp.where(core == 0, next_chip, last_chip)
    backward_chip = jnp.where(core == 0, last_chip, next_chip)
    over_chip = jnp.where((chip < 2) | (chip >= chips - 2), chip ^ 6, chip ^ 1)
    came_ahead = ((chip % 4 == 0) | (chip % 4 == 3)) == (core == 0)
    slab, units = tokens.shape
    needed = devices // 2 + devices // 8 + 2

    def window(value, chip):
        blocks = value.reshape(slab, devices, units // devices)
        blocks = jnp.concatenate([blocks, blocks], axis=1)
        blocks = lax.dynamic_slice_in_dim(blocks, first_needed(devices, chip), needed, axis=1)
        return blocks.reshape(slab, -1)

    ahead, back = [tokens], [tokens]
    for _ in range(2):
        ahead.append(send(ahead[-1], onward))
        back.append(send(back[-1], backward))
    half = send(window(jnp.where(came_ahead, ahead[1], back[1]), over_chip), over)
    middle_chips = range(2, chips - 2)
    across = [(at, at ^ 2) for at in range(devices) if at // 2 in middle_chips]
    neighbor = lax.ppermute(window(tokens, over_chip), "col", across)

    def last_hop(value, target, chip):
        far = [target[target[target[at]]] for at in range(devices)]
        pairs = [
            (at, to) for at, to in enumerate(target)
            if not (to // 2 in middle_chips and far[to ^ 2] == to)
        ]
        return lax.ppermute(window(value, chip), "col", pairs)

    is_middle = (chip >= 2) & (chip < chips - 2)
    by_ahead = is_middle & (((chip == 2) | (chip == 5)) == (core == 0))
    by_back = is_middle & (((chip == 3) | (chip == 4)) == (core == 0))
    ahead.append(jnp.where(by_ahead, neighbor, last_hop(ahead[2], onward, onward_chip)))
    back.append(jnp.where(by_back, neighbor, last_hop(back[2], backward, backward_chip)))
    near = jnp.concatenate((tokens, ahead[1], back[1]), axis=0)
    middle = jnp.concatenate((ahead[2], back[2]), axis=0)
    last = jnp.concatenate((ahead[3], half), axis=0)
    near_beside = send(near, sibling)
    middle_beside = send(middle, sibling)
    last_beside = send(after(last, middle_beside), sibling)
    return [near, near_beside, middle, middle_beside, last, last_beside, back[3], send(back[3], sibling)]


def slab_origin(devices, device, number):
    chips = devices // 2
    number, flip = number % chips, number // chips
    hops = (number + 1) // 2 if number % 2 else -(number // 2)
    chip, core = device // 2, device % 2
    core = 1 - core if flip else core
    place = jnp.where(chip % 2 == 0, chip // 2, chips - 1 - chip // 2)
    place = (place - (1 - 2 * core) * hops + chips) % chips
    chip = jnp.where(2 * place < chips, 2 * place, 2 * (chips - 1 - place) + 1)
    return 2 * chip + core


def ring_kernel(devices, slots, table_ref, *refs):
    groups = refs[:len(GROUPS)]
    out_ref, pair, tiles, zeros, out_sems, zero_sems = refs[len(GROUPS):]
    device = table_ref[table_ref.shape[0] - 1]
    slab, width = pair.shape[1] // devices, pair.shape[2]
    first = first_needed(devices, device // 2)

    def owned(partner):
        return table_ref[devices + tile_number(devices, device, partner)] == device

    def put(buffer, slot):
        return pltpu.make_async_copy(tiles.at[buffer], out_ref.at[slot], out_sems.at[buffer])

    def clear(slot):
        return pltpu.make_async_copy(zeros, out_ref.at[slot], zero_sems.at[slot])

    def load_block(partner, masked):
        parts = []
        for numbers, ref in zip(GROUPS, groups):
            place = partner
            if ref.shape[1] < devices * width:
                place = lax.rem(partner - first + devices, devices)
            group = ref[:, pl.ds(pl.multiple_of(place * width, 128), width)].astype(jnp.float32)
            for at, number in enumerate(numbers):
                part = group[at * slab:(at + 1) * slab]
                if masked:
                    row = lax.broadcasted_iota(jnp.int32, (slab, width), 0)
                    part = jnp.where(row < table_ref[slab_origin(devices, device, number)], part, 0.0)
                parts.append(part)
        pair[0 if masked else 1] = jnp.concatenate(parts, axis=0).astype(jnp.bfloat16)

    load_block(device, True)
    valid_count = table_ref[0]
    for at in range(1, devices):
        valid_count = valid_count + table_ref[at]
    scale = 1.0 / jnp.full((8, width), valid_count.astype(jnp.float32))

    def visit(partner, slot):
        mine = owned(partner)

        @pl.when(mine)
        def _():
            buffer = lax.rem(slot, BUFFERS)
            load_block(partner, False)

            @pl.when(slot >= BUFFERS)
            def _():
                put(buffer, slot - BUFFERS).wait()

            left = (partner <= device).astype(jnp.int32)
            for row in range(0, width, STRIP):
                rows = min(STRIP, width - row)
                strip = pl.ds(row, rows)
                product = lax.dot_general(
                    pair[left, :, row:row + rows], pair[1 - left], (((0,), (0,)), ((), ())),
                    preferred_element_type=jnp.float32,
                )
                tiles[buffer, strip, :] = product * scale[:1]
                pltpu.make_async_copy(
                    tiles.at[buffer, strip], out_ref.at[slot, strip], out_sems.at[buffer]
                ).start()

        return slot + mine.astype(jnp.int32)

    count = lax.fori_loop(0, devices, visit, jnp.int32(0))

    @pl.when(count < slots)
    def _():
        zeros[...] = jnp.zeros_like(zeros)

    def start_clear(slot, carry):
        clear(slot).start()
        return carry

    lax.fori_loop(count, slots, start_clear, 0)

    def drain(slot, carry):
        put(lax.rem(slot, BUFFERS), slot).wait()
        return carry

    lax.fori_loop(jnp.maximum(count - BUFFERS, 0), count, drain, 0)

    def end_clear(slot, carry):
        clear(slot).wait()
        return carry

    lax.fori_loop(count, slots, end_clear, 0)


def ring_form(tokens, slab_lengths, tile_owner, devices, device, slots):
    slab, units = tokens.shape
    width = units // devices
    groups = ring_gather(tokens, device, devices)
    table = jnp.concatenate([slab_lengths, tile_owner, device.reshape(1)])
    return pl.pallas_call(
        functools.partial(ring_kernel, devices, slots),
        out_shape=jax.ShapeDtypeStruct((slots, width, width), jnp.float32),
        in_specs=[pl.BlockSpec(memory_space=pltpu.SMEM)]
        + [pl.BlockSpec(memory_space=pltpu.VMEM)] * len(groups),
        out_specs=pl.BlockSpec(memory_space=pl.ANY),
        scratch_shapes=[
            pltpu.VMEM((2, slab * devices, width), jnp.bfloat16),
            pltpu.VMEM((BUFFERS, width, width), jnp.float32),
            pltpu.VMEM((width, width), jnp.float32),
            pltpu.SemaphoreType.DMA((BUFFERS,)),
            pltpu.SemaphoreType.DMA((slots,)),
        ],
        compiler_params=pltpu.CompilerParams(vmem_limit_bytes=32 * 1024 * 1024),
        cost_estimate=pl.CostEstimate(
            flops=2 * slots * slab * devices * width * width,
            bytes_accessed=4 * slots * width * width,
            transcendentals=0,
        ),
    )(table, *groups)


def per_device(tokens, slab_lengths, tile_owner):
    devices = lax.axis_size("col")
    device = lax.axis_index("col").astype(jnp.int32)
    slots = devices // 2 + devices // 8 + 1
    width = tokens.shape[1] // devices
    form = ring_form if devices == RING_DEVICES and width % 128 == 0 else gathered_form
    return form(tokens, slab_lengths, tile_owner, devices, device, slots)


def solution(mesh):
    return jax.shard_map(
        per_device,
        mesh=mesh,
        in_specs=(P(("grp", "col"), None), P("grp"), P()),
        out_specs=P(("grp", "col"), None, None),
        check_vma=False,
    )
```

```python
import functools

import jax
import jax.numpy as jnp
from jax import lax
from jax.experimental import pallas as pl
from jax.experimental.pallas import tpu as pltpu
from jax.sharding import PartitionSpec as P

BUFFERS = 4
STRIP = 256
RING_DEVICES = 16


def tile_number(devices, device, partner):
    low = jnp.minimum(device, partner)
    high = jnp.maximum(device, partner)
    return low * devices - low * (low - 1) // 2 + (high - low)


def gathered_kernel(
    devices, slots, owner_ref, device_ref, scale_ref, x_ref, mask_ref,
    out_ref, blocks, mask, tiles, zeros, in_sems, mask_sem, out_sems, zero_sems,
):
    device = device_ref[0]
    width = blocks.shape[2]

    def owned(partner):
        return owner_ref[tile_number(devices, device, partner)] == device

    def fetch(partner):
        return pltpu.make_async_copy(x_ref.at[partner], blocks.at[partner], in_sems.at[partner])

    def put(buffer, slot):
        return pltpu.make_async_copy(tiles.at[buffer], out_ref.at[slot], out_sems.at[buffer])

    def clear(slot):
        return pltpu.make_async_copy(zeros, out_ref.at[slot], zero_sems.at[slot])

    mask_copy = pltpu.make_async_copy(mask_ref, mask, mask_sem)
    mask_copy.start()
    fetch(device).start()

    def start_fetch(partner, count):
        mine = owned(partner)

        @pl.when(mine & (partner != device))
        def _():
            fetch(partner).start()

        return count + mine.astype(jnp.int32)

    count = lax.fori_loop(0, devices, start_fetch, jnp.int32(0))

    zeros[...] = jnp.zeros_like(zeros)

    def start_clear(slot, carry):
        clear(slot).start()
        return carry

    lax.fori_loop(count, slots, start_clear, 0)

    mask_copy.wait()
    fetch(device).wait()
    blocks[devices] = blocks[device] * mask[...]
    scale = scale_ref[0]

    def visit(partner, slot):
        mine = owned(partner)

        @pl.when(mine)
        def _():
            @pl.when(partner != device)
            def _():
                fetch(partner).wait()

            buffer = lax.rem(slot, BUFFERS)

            @pl.when(slot >= BUFFERS)
            def _():
                put(buffer, slot - BUFFERS).wait()

            left = jnp.where(partner <= device, partner, devices)
            right = jnp.where(partner <= device, devices, partner)
            product = lax.dot_general(
                blocks[left], blocks[right], (((0,), (0,)), ((), ())),
                preferred_element_type=jnp.float32,
            )
            tiles[buffer] = product * scale
            put(buffer, slot).start()

        return slot + mine.astype(jnp.int32)

    lax.fori_loop(0, devices, visit, jnp.int32(0))

    def drain(slot, carry):
        put(lax.rem(slot, BUFFERS), slot).wait()
        return carry

    lax.fori_loop(jnp.maximum(count - BUFFERS, 0), count, drain, 0)

    def end_clear(slot, carry):
        clear(slot).wait()
        return carry

    lax.fori_loop(count, slots, end_clear, 0)


def gathered_form(tokens, slab_lengths, tile_owner, devices, device, slots):
    slab, units = tokens.shape
    rows = slab * devices
    width = units // devices
    x = lax.all_gather(tokens, "col", axis=0, tiled=True)
    x = x.reshape(rows, devices, width).transpose(1, 0, 2)
    scale = 1.0 / jnp.sum(slab_lengths).astype(jnp.float32)
    valid = jnp.arange(slab, dtype=jnp.int32)[None, :] < slab_lengths[:, None]
    mask = jnp.broadcast_to(valid.reshape(rows, 1), (rows, width)).astype(jnp.bfloat16)
    return pl.pallas_call(
        functools.partial(gathered_kernel, devices, slots),
        out_shape=jax.ShapeDtypeStruct((slots, width, width), jnp.float32),
        in_specs=[pl.BlockSpec(memory_space=pltpu.SMEM)] * 3 + [pl.BlockSpec(memory_space=pl.ANY)] * 2,
        out_specs=pl.BlockSpec(memory_space=pl.ANY),
        scratch_shapes=[
            pltpu.VMEM((devices + 1, rows, width), jnp.bfloat16),
            pltpu.VMEM((rows, width), jnp.bfloat16),
            pltpu.VMEM((BUFFERS, width, width), jnp.float32),
            pltpu.VMEM((width, width), jnp.float32),
            pltpu.SemaphoreType.DMA((devices,)),
            pltpu.SemaphoreType.DMA,
            pltpu.SemaphoreType.DMA((BUFFERS,)),
            pltpu.SemaphoreType.DMA((slots,)),
        ],
        compiler_params=pltpu.CompilerParams(vmem_limit_bytes=50 * 1024 * 1024),
    )(tile_owner, device.reshape(1), scale.reshape(1), x, mask)


def ring_plan(devices):
    chips = devices // 2
    order = list(range(0, chips, 2)) + list(range(1, chips, 2))[::-1]
    place = {chip: at for at, chip in enumerate(order)}
    onward = []
    for device in range(devices):
        chip, core = divmod(device, 2)
        step = 1 if core == 0 else -1
        onward.append(order[(place[chip] + step) % chips] * 2 + core)
    backward = [onward.index(device) for device in range(devices)]
    return onward, backward


GROUPS = ((0, 1, 2), (8, 9, 10), (3, 4), (11, 12), (6,), (14,), (7,), (15,), (5,), (13,))


def first_needed(devices, chip):
    return (2 * chip - devices // 2 - devices // 8 + devices) % devices


def ring_gather(tokens, device, devices):
    onward, backward = ring_plan(devices)
    sibling = [device ^ 1 for device in range(devices)]
    over = [at ^ 12 if at // 4 in (0, 3) else at ^ 2 for at in range(devices)]

    def send(value, target):
        return lax.ppermute(value, "col", list(enumerate(target)))

    def after(value, *others):
        return lax.optimization_barrier((value, *others))[0]

    chip, core = device // 2, device % 2
    chips = devices // 2
    even = chip % 2 == 0
    next_chip = jnp.where(even, jnp.where(chip == chips - 2, chips - 1, chip + 2), jnp.where(chip == 1, 0, chip - 2))
    last_chip = jnp.where(even, jnp.where(chip == 0, 1, chip - 2), jnp.where(chip == chips - 1, chips - 2, chip + 2))
    onward_chip = jnp.where(core == 0, next_chip, last_chip)
    backward_chip = jnp.where(core == 0, last_chip, next_chip)
    over_chip = jnp.where((chip < 2) | (chip >= chips - 2), chip ^ 6, chip ^ 1)
    chip, core = device // 2, device % 2
    chips = devices // 2
    even = chip % 2 == 0
    next_chip = jnp.where(even, jnp.where(chip == chips - 2, chips - 1, chip + 2), jnp.where(chip == 1, 0, chip - 2))
    last_chip = jnp.where(even, jnp.where(chip == 0, 1, chip - 2), jnp.where(chip == chips - 1, chips - 2, chip + 2))
    onward_chip = jnp.where(core == 0, next_chip, last_chip)
    backward_chip = jnp.where(core == 0, last_chip, next_chip)
    over_chip = jnp.where((chip < 2) | (chip >= chips - 2), chip ^ 6, chip ^ 1)
    came_ahead = ((chip % 4 == 0) | (chip % 4 == 3)) == (core == 0)
    slab, units = tokens.shape
    needed = devices // 2 + devices // 8 + 2

    def window(value, chip):
        blocks = value.reshape(slab, devices, units // devices)
        blocks = jnp.concatenate([blocks, blocks], axis=1)
        blocks = lax.dynamic_slice_in_dim(blocks, first_needed(devices, chip), needed, axis=1)
        return blocks.reshape(slab, -1)

    ahead, back = [tokens], [tokens]
    for _ in range(2):
        ahead.append(send(ahead[-1], onward))
        back.append(send(back[-1], backward))
    half = send(window(jnp.where(came_ahead, ahead[1], back[1]), over_chip), over)
    ahead.append(send(window(ahead[2], onward_chip), onward))
    back.append(send(window(back[2], backward_chip), backward))
    near = jnp.concatenate((tokens, ahead[1], back[1]), axis=0)
    middle = jnp.concatenate((ahead[2], back[2]), axis=0)
    near_beside = send(near, sibling)
    middle_beside = send(jnp.concatenate((window(ahead[2], chip), window(back[2], chip)), axis=0), sibling)
    groups = [near, near_beside, middle, middle_beside]
    for value in (back[3], half, ahead[3]):
        groups += [value, send(after(value, back[3]) if value is half else value, sibling)]
    return groups


def slab_origin(devices, device, number):
    chips = devices // 2
    number, flip = number % chips, number // chips
    hops = (number + 1) // 2 if number % 2 else -(number // 2)
    chip, core = device // 2, device % 2
    core = 1 - core if flip else core
    place = jnp.where(chip % 2 == 0, chip // 2, chips - 1 - chip // 2)
    place = (place - (1 - 2 * core) * hops + chips) % chips
    chip = jnp.where(2 * place < chips, 2 * place, 2 * (chips - 1 - place) + 1)
    return 2 * chip + core


def ring_kernel(devices, slots, table_ref, *refs):
    groups = refs[:len(GROUPS)]
    out_ref, pair, tiles, zeros, out_sems, zero_sems = refs[len(GROUPS):]
    device = table_ref[table_ref.shape[0] - 1]
    slab, width = pair.shape[1] // devices, pair.shape[2]
    first = first_needed(devices, device // 2)

    def owned(partner):
        return table_ref[devices + tile_number(devices, device, partner)] == device

    def put(buffer, slot):
        return pltpu.make_async_copy(tiles.at[buffer], out_ref.at[slot], out_sems.at[buffer])

    def clear(slot):
        return pltpu.make_async_copy(zeros, out_ref.at[slot], zero_sems.at[slot])

    def load_block(partner, masked):
        parts = []
        for numbers, ref in zip(GROUPS, groups):
            place = partner
            if ref.shape[1] < devices * width:
                place = lax.rem(partner - first + devices, devices)
            group = ref[:, pl.ds(pl.multiple_of(place * width, 128), width)].astype(jnp.float32)
            for at, number in enumerate(numbers):
                part = group[at * slab:(at + 1) * slab]
                if masked:
                    row = lax.broadcasted_iota(jnp.int32, (slab, width), 0)
                    part = jnp.where(row < table_ref[slab_origin(devices, device, number)], part, 0.0)
                parts.append(part)
        pair[0 if masked else 1] = jnp.concatenate(parts, axis=0).astype(jnp.bfloat16)

    load_block(device, True)
    valid_count = table_ref[0]
    for at in range(1, devices):
        valid_count = valid_count + table_ref[at]
    scale = 1.0 / jnp.full((8, width), valid_count.astype(jnp.float32))

    def visit(partner, slot):
        mine = owned(partner)

        @pl.when(mine)
        def _():
            buffer = lax.rem(slot, BUFFERS)
            load_block(partner, False)

            @pl.when(slot >= BUFFERS)
            def _():
                put(buffer, slot - BUFFERS).wait()

            left = (partner <= device).astype(jnp.int32)
            for row in range(0, width, STRIP):
                rows = min(STRIP, width - row)
                strip = pl.ds(row, rows)
                product = lax.dot_general(
                    pair[left, :, row:row + rows], pair[1 - left], (((0,), (0,)), ((), ())),
                    preferred_element_type=jnp.float32,
                )
                tiles[buffer, strip, :] = product * scale[:1]
                pltpu.make_async_copy(
                    tiles.at[buffer, strip], out_ref.at[slot, strip], out_sems.at[buffer]
                ).start()

        return slot + mine.astype(jnp.int32)

    count = lax.fori_loop(0, devices, visit, jnp.int32(0))

    @pl.when(count < slots)
    def _():
        zeros[...] = jnp.zeros_like(zeros)

    def start_clear(slot, carry):
        clear(slot).start()
        return carry

    lax.fori_loop(count, slots, start_clear, 0)

    def drain(slot, carry):
        put(lax.rem(slot, BUFFERS), slot).wait()
        return carry

    lax.fori_loop(jnp.maximum(count - BUFFERS, 0), count, drain, 0)

    def end_clear(slot, carry):
        clear(slot).wait()
        return carry

    lax.fori_loop(count, slots, end_clear, 0)


def ring_form(tokens, slab_lengths, tile_owner, devices, device, slots):
    slab, units = tokens.shape
    width = units // devices
    groups = ring_gather(tokens, device, devices)
    table = jnp.concatenate([slab_lengths, tile_owner, device.reshape(1)])
    return pl.pallas_call(
        functools.partial(ring_kernel, devices, slots),
        out_shape=jax.ShapeDtypeStruct((slots, width, width), jnp.float32),
        in_specs=[pl.BlockSpec(memory_space=pltpu.SMEM)]
        + [pl.BlockSpec(memory_space=pltpu.VMEM)] * len(groups),
        out_specs=pl.BlockSpec(memory_space=pl.ANY),
        scratch_shapes=[
            pltpu.VMEM((2, slab * devices, width), jnp.bfloat16),
            pltpu.VMEM((BUFFERS, width, width), jnp.float32),
            pltpu.VMEM((width, width), jnp.float32),
            pltpu.SemaphoreType.DMA((BUFFERS,)),
            pltpu.SemaphoreType.DMA((slots,)),
        ],
        compiler_params=pltpu.CompilerParams(vmem_limit_bytes=32 * 1024 * 1024),
        cost_estimate=pl.CostEstimate(
            flops=2 * slots * slab * devices * width * width,
            bytes_accessed=4 * slots * width * width,
            transcendentals=0,
        ),
    )(table, *groups)


def per_device(tokens, slab_lengths, tile_owner):
    devices = lax.axis_size("col")
    device = lax.axis_index("col").astype(jnp.int32)
    slots = devices // 2 + devices // 8 + 1
    width = tokens.shape[1] // devices
    form = ring_form if devices == RING_DEVICES and width % 128 == 0 else gathered_form
    return form(tokens, slab_lengths, tile_owner, devices, device, slots)


def solution(mesh):
    return jax.shard_map(
        per_device,
        mesh=mesh,
        in_specs=(P(("grp", "col"), None), P("grp"), P()),
        out_specs=P(("grp", "col"), None, None),
        check_vma=False,
    )
```

```python
import functools

import jax
import jax.numpy as jnp
from jax import lax
from jax.experimental import pallas as pl
from jax.experimental.pallas import tpu as pltpu
from jax.sharding import PartitionSpec as P

BUFFERS = 4
STRIP = 256
RING_DEVICES = 16


def tile_number(devices, device, partner):
    low = jnp.minimum(device, partner)
    high = jnp.maximum(device, partner)
    return low * devices - low * (low - 1) // 2 + (high - low)


def gathered_kernel(
    devices, slots, owner_ref, device_ref, scale_ref, x_ref, mask_ref,
    out_ref, blocks, mask, tiles, zeros, in_sems, mask_sem, out_sems, zero_sems,
):
    device = device_ref[0]
    width = blocks.shape[2]

    def owned(partner):
        return owner_ref[tile_number(devices, device, partner)] == device

    def fetch(partner):
        return pltpu.make_async_copy(x_ref.at[partner], blocks.at[partner], in_sems.at[partner])

    def put(buffer, slot):
        return pltpu.make_async_copy(tiles.at[buffer], out_ref.at[slot], out_sems.at[buffer])

    def clear(slot):
        return pltpu.make_async_copy(zeros, out_ref.at[slot], zero_sems.at[slot])

    mask_copy = pltpu.make_async_copy(mask_ref, mask, mask_sem)
    mask_copy.start()
    fetch(device).start()

    def start_fetch(partner, count):
        mine = owned(partner)

        @pl.when(mine & (partner != device))
        def _():
            fetch(partner).start()

        return count + mine.astype(jnp.int32)

    count = lax.fori_loop(0, devices, start_fetch, jnp.int32(0))

    zeros[...] = jnp.zeros_like(zeros)

    def start_clear(slot, carry):
        clear(slot).start()
        return carry

    lax.fori_loop(count, slots, start_clear, 0)

    mask_copy.wait()
    fetch(device).wait()
    blocks[devices] = blocks[device] * mask[...]
    scale = scale_ref[0]

    def visit(partner, slot):
        mine = owned(partner)

        @pl.when(mine)
        def _():
            @pl.when(partner != device)
            def _():
                fetch(partner).wait()

            buffer = lax.rem(slot, BUFFERS)

            @pl.when(slot >= BUFFERS)
            def _():
                put(buffer, slot - BUFFERS).wait()

            left = jnp.where(partner <= device, partner, devices)
            right = jnp.where(partner <= device, devices, partner)
            product = lax.dot_general(
                blocks[left], blocks[right], (((0,), (0,)), ((), ())),
                preferred_element_type=jnp.float32,
            )
            tiles[buffer] = product * scale
            put(buffer, slot).start()

        return slot + mine.astype(jnp.int32)

    lax.fori_loop(0, devices, visit, jnp.int32(0))

    def drain(slot, carry):
        put(lax.rem(slot, BUFFERS), slot).wait()
        return carry

    lax.fori_loop(jnp.maximum(count - BUFFERS, 0), count, drain, 0)

    def end_clear(slot, carry):
        clear(slot).wait()
        return carry

    lax.fori_loop(count, slots, end_clear, 0)


def gathered_form(tokens, slab_lengths, tile_owner, devices, device, slots):
    slab, units = tokens.shape
    rows = slab * devices
    width = units // devices
    x = lax.all_gather(tokens, "col", axis=0, tiled=True)
    x = x.reshape(rows, devices, width).transpose(1, 0, 2)
    scale = 1.0 / jnp.sum(slab_lengths).astype(jnp.float32)
    valid = jnp.arange(slab, dtype=jnp.int32)[None, :] < slab_lengths[:, None]
    mask = jnp.broadcast_to(valid.reshape(rows, 1), (rows, width)).astype(jnp.bfloat16)
    return pl.pallas_call(
        functools.partial(gathered_kernel, devices, slots),
        out_shape=jax.ShapeDtypeStruct((slots, width, width), jnp.float32),
        in_specs=[pl.BlockSpec(memory_space=pltpu.SMEM)] * 3 + [pl.BlockSpec(memory_space=pl.ANY)] * 2,
        out_specs=pl.BlockSpec(memory_space=pl.ANY),
        scratch_shapes=[
            pltpu.VMEM((devices + 1, rows, width), jnp.bfloat16),
            pltpu.VMEM((rows, width), jnp.bfloat16),
            pltpu.VMEM((BUFFERS, width, width), jnp.float32),
            pltpu.VMEM((width, width), jnp.float32),
            pltpu.SemaphoreType.DMA((devices,)),
            pltpu.SemaphoreType.DMA,
            pltpu.SemaphoreType.DMA((BUFFERS,)),
            pltpu.SemaphoreType.DMA((slots,)),
        ],
        compiler_params=pltpu.CompilerParams(vmem_limit_bytes=50 * 1024 * 1024),
    )(tile_owner, device.reshape(1), scale.reshape(1), x, mask)


def ring_plan(devices):
    chips = devices // 2
    order = list(range(0, chips, 2)) + list(range(1, chips, 2))[::-1]
    place = {chip: at for at, chip in enumerate(order)}
    onward = []
    for device in range(devices):
        chip, core = divmod(device, 2)
        onward.append(order[(place[chip] + 1) % chips] * 2 + core)
    backward = [onward.index(device) for device in range(devices)]
    return onward, backward


GROUPS = ((0, 1, 2), (8, 9, 10), (3, 4), (11, 12), (5, 7), (13, 15), (6,), (14,))


def first_needed(devices, chip):
    return (2 * chip - devices // 2 - devices // 8 + devices) % devices


def ring_gather(tokens, device, devices):
    onward, backward = ring_plan(devices)
    sibling = [device ^ 1 for device in range(devices)]
    over = [at ^ 12 if at // 4 in (0, 3) else at ^ 2 for at in range(devices)]

    def send(value, target):
        return lax.ppermute(value, "col", list(enumerate(target)))

    def after(value, *others):
        return lax.optimization_barrier((value, *others))[0]

    chip, chips = device // 2, devices // 2
    even = chip % 2 == 0
    next_chip = jnp.where(even, jnp.where(chip == chips - 2, chips - 1, chip + 2), jnp.where(chip == 1, 0, chip - 2))
    last_chip = jnp.where(even, jnp.where(chip == 0, 1, chip - 2), jnp.where(chip == chips - 1, chips - 2, chip + 2))
    over_chip = jnp.where((chip < 2) | (chip >= chips - 2), chip ^ 6, chip ^ 1)
    chip, chips = device // 2, devices // 2
    even = chip % 2 == 0
    next_chip = jnp.where(even, jnp.where(chip == chips - 2, chips - 1, chip + 2), jnp.where(chip == 1, 0, chip - 2))
    last_chip = jnp.where(even, jnp.where(chip == 0, 1, chip - 2), jnp.where(chip == chips - 1, chips - 2, chip + 2))
    over_chip = jnp.where((chip < 2) | (chip >= chips - 2), chip ^ 6, chip ^ 1)
    came_ahead = (chip % 4 == 0) | (chip % 4 == 3)
    slab, units = tokens.shape
    needed = devices // 2 + devices // 8 + 2

    def window(value, chip):
        blocks = value.reshape(slab, devices, units // devices)
        blocks = jnp.concatenate([blocks, blocks], axis=1)
        blocks = lax.dynamic_slice_in_dim(blocks, first_needed(devices, chip), needed, axis=1)
        return blocks.reshape(slab, -1)

    ahead, back = [tokens], [tokens]
    for _ in range(2):
        ahead.append(send(ahead[-1], onward))
        back.append(send(back[-1], backward))
    half = send(window(jnp.where(came_ahead, ahead[1], back[1]), over_chip), over)
    ahead.append(send(window(ahead[2], next_chip), onward))
    back.append(send(window(back[2], last_chip), backward))
    near = jnp.concatenate((tokens, ahead[1], back[1]), axis=0)
    middle = jnp.concatenate((ahead[2], back[2]), axis=0)
    last = jnp.concatenate((ahead[3], half), axis=0)
    near_beside = send(near, sibling)
    middle_beside = send(middle, sibling)
    last_beside = send(after(last, middle_beside), sibling)
    return [near, near_beside, middle, middle_beside, last, last_beside, back[3], send(back[3], sibling)]

def slab_origin(devices, device, number):
    chips = devices // 2
    number, flip = number % chips, number // chips
    hops = (number + 1) // 2 if number % 2 else -(number // 2)
    chip, core = device // 2, device % 2
    core = 1 - core if flip else core
    place = jnp.where(chip % 2 == 0, chip // 2, chips - 1 - chip // 2)
    place = (place - hops + chips) % chips
    chip = jnp.where(2 * place < chips, 2 * place, 2 * (chips - 1 - place) + 1)
    return 2 * chip + core


def ring_kernel(devices, slots, device_ref, table_ref, *refs):
    groups = refs[:len(GROUPS)]
    out_ref, pair, tiles, zeros, out_sems, zero_sems = refs[len(GROUPS):]
    device = device_ref[0]
    slab, width = pair.shape[1] // devices, pair.shape[2]
    first = first_needed(devices, device // 2)

    def owned(partner):
        return table_ref[devices + tile_number(devices, device, partner)] == device

    def put(buffer, slot):
        return pltpu.make_async_copy(tiles.at[buffer], out_ref.at[slot], out_sems.at[buffer])

    def clear(slot):
        return pltpu.make_async_copy(zeros, out_ref.at[slot], zero_sems.at[slot])

    def load_block(partner, masked):
        parts = []
        for numbers, ref in zip(GROUPS, groups):
            place = partner
            if ref.shape[1] < devices * width:
                place = lax.rem(partner - first + devices, devices)
            group = ref[:, pl.ds(pl.multiple_of(place * width, 128), width)].astype(jnp.float32)
            for at, number in enumerate(numbers):
                part = group[at * slab:(at + 1) * slab]
                if masked:
                    row = lax.broadcasted_iota(jnp.int32, (slab, width), 0)
                    part = jnp.where(row < table_ref[slab_origin(devices, device, number)], part, 0.0)
                parts.append(part)
        pair[0 if masked else 1] = jnp.concatenate(parts, axis=0).astype(jnp.bfloat16)

    load_block(device, True)
    valid_count = table_ref[0]
    for at in range(1, devices):
        valid_count = valid_count + table_ref[at]
    scale = 1.0 / jnp.full((8, width), valid_count.astype(jnp.float32))

    def visit(partner, slot):
        mine = owned(partner)

        @pl.when(mine)
        def _():
            buffer = lax.rem(slot, BUFFERS)
            load_block(partner, False)

            @pl.when(slot >= BUFFERS)
            def _():
                put(buffer, slot - BUFFERS).wait()

            left = (partner <= device).astype(jnp.int32)
            for row in range(0, width, STRIP):
                rows = min(STRIP, width - row)
                strip = pl.ds(row, rows)
                product = lax.dot_general(
                    pair[left, :, row:row + rows], pair[1 - left], (((0,), (0,)), ((), ())),
                    preferred_element_type=jnp.float32,
                )
                tiles[buffer, strip, :] = product * scale[:1]
                pltpu.make_async_copy(
                    tiles.at[buffer, strip], out_ref.at[slot, strip], out_sems.at[buffer]
                ).start()

        return slot + mine.astype(jnp.int32)

    count = lax.fori_loop(0, devices, visit, jnp.int32(0))

    @pl.when(count < slots)
    def _():
        zeros[...] = jnp.zeros_like(zeros)

    def start_clear(slot, carry):
        clear(slot).start()
        return carry

    lax.fori_loop(count, slots, start_clear, 0)

    def drain(slot, carry):
        put(lax.rem(slot, BUFFERS), slot).wait()
        return carry

    lax.fori_loop(jnp.maximum(count - BUFFERS, 0), count, drain, 0)

    def end_clear(slot, carry):
        clear(slot).wait()
        return carry

    lax.fori_loop(count, slots, end_clear, 0)


def ring_form(tokens, slab_lengths, tile_owner, devices, device, slots):
    slab, units = tokens.shape
    width = units // devices
    groups = ring_gather(tokens, device, devices)
    table = jnp.concatenate([slab_lengths, tile_owner])
    return pl.pallas_call(
        functools.partial(ring_kernel, devices, slots),
        out_shape=jax.ShapeDtypeStruct((slots, width, width), jnp.float32),
        in_specs=[pl.BlockSpec(memory_space=pltpu.SMEM)] * 2
        + [pl.BlockSpec(memory_space=pltpu.VMEM)] * len(groups),
        out_specs=pl.BlockSpec(memory_space=pl.ANY),
        scratch_shapes=[
            pltpu.VMEM((2, slab * devices, width), jnp.bfloat16),
            pltpu.VMEM((BUFFERS, width, width), jnp.float32),
            pltpu.VMEM((width, width), jnp.float32),
            pltpu.SemaphoreType.DMA((BUFFERS,)),
            pltpu.SemaphoreType.DMA((slots,)),
        ],
        compiler_params=pltpu.CompilerParams(vmem_limit_bytes=32 * 1024 * 1024),
        cost_estimate=pl.CostEstimate(
            flops=2 * slots * slab * devices * width * width,
            bytes_accessed=4 * slots * width * width,
            transcendentals=0,
        ),
    )(device.reshape(1), table, *groups)


def per_device(tokens, slab_lengths, tile_owner):
    devices = lax.axis_size("col")
    device = lax.axis_index("col").astype(jnp.int32)
    slots = devices // 2 + devices // 8 + 1
    width = tokens.shape[1] // devices
    form = ring_form if devices == RING_DEVICES and width % 128 == 0 else gathered_form
    return form(tokens, slab_lengths, tile_owner, devices, device, slots)


def solution(mesh):
    return jax.shard_map(
        per_device,
        mesh=mesh,
        in_specs=(P(("grp", "col"), None), P("grp"), P()),
        out_specs=P(("grp", "col"), None, None),
        check_vma=False,
    )
```

```python
import functools

import jax
import jax.numpy as jnp
from jax import lax
from jax.experimental import pallas as pl
from jax.experimental.pallas import tpu as pltpu
from jax.sharding import PartitionSpec as P

BUFFERS = 4
STRIP = 256
RING_DEVICES = 16


def tile_number(devices, device, partner):
    low = jnp.minimum(device, partner)
    high = jnp.maximum(device, partner)
    return low * devices - low * (low - 1) // 2 + (high - low)


def gathered_kernel(
    devices, slots, owner_ref, device_ref, scale_ref, x_ref, mask_ref,
    out_ref, blocks, mask, tiles, zeros, in_sems, mask_sem, out_sems, zero_sems,
):
    device = device_ref[0]
    width = blocks.shape[2]

    def owned(partner):
        return owner_ref[tile_number(devices, device, partner)] == device

    def fetch(partner):
        return pltpu.make_async_copy(x_ref.at[partner], blocks.at[partner], in_sems.at[partner])

    def put(buffer, slot):
        return pltpu.make_async_copy(tiles.at[buffer], out_ref.at[slot], out_sems.at[buffer])

    def clear(slot):
        return pltpu.make_async_copy(zeros, out_ref.at[slot], zero_sems.at[slot])

    mask_copy = pltpu.make_async_copy(mask_ref, mask, mask_sem)
    mask_copy.start()
    fetch(device).start()

    def start_fetch(partner, count):
        mine = owned(partner)

        @pl.when(mine & (partner != device))
        def _():
            fetch(partner).start()

        return count + mine.astype(jnp.int32)

    count = lax.fori_loop(0, devices, start_fetch, jnp.int32(0))

    zeros[...] = jnp.zeros_like(zeros)

    def start_clear(slot, carry):
        clear(slot).start()
        return carry

    lax.fori_loop(count, slots, start_clear, 0)

    mask_copy.wait()
    fetch(device).wait()
    blocks[devices] = blocks[device] * mask[...]
    scale = scale_ref[0]

    def visit(partner, slot):
        mine = owned(partner)

        @pl.when(mine)
        def _():
            @pl.when(partner != device)
            def _():
                fetch(partner).wait()

            buffer = lax.rem(slot, BUFFERS)

            @pl.when(slot >= BUFFERS)
            def _():
                put(buffer, slot - BUFFERS).wait()

            left = jnp.where(partner <= device, partner, devices)
            right = jnp.where(partner <= device, devices, partner)
            product = lax.dot_general(
                blocks[left], blocks[right], (((0,), (0,)), ((), ())),
                preferred_element_type=jnp.float32,
            )
            tiles[buffer] = product * scale
            put(buffer, slot).start()

        return slot + mine.astype(jnp.int32)

    lax.fori_loop(0, devices, visit, jnp.int32(0))

    def drain(slot, carry):
        put(lax.rem(slot, BUFFERS), slot).wait()
        return carry

    lax.fori_loop(jnp.maximum(count - BUFFERS, 0), count, drain, 0)

    def end_clear(slot, carry):
        clear(slot).wait()
        return carry

    lax.fori_loop(count, slots, end_clear, 0)


def gathered_form(tokens, slab_lengths, tile_owner, devices, device, slots):
    slab, units = tokens.shape
    rows = slab * devices
    width = units // devices
    x = lax.all_gather(tokens, "col", axis=0, tiled=True)
    x = x.reshape(rows, devices, width).transpose(1, 0, 2)
    scale = 1.0 / jnp.sum(slab_lengths).astype(jnp.float32)
    valid = jnp.arange(slab, dtype=jnp.int32)[None, :] < slab_lengths[:, None]
    mask = jnp.broadcast_to(valid.reshape(rows, 1), (rows, width)).astype(jnp.bfloat16)
    return pl.pallas_call(
        functools.partial(gathered_kernel, devices, slots),
        out_shape=jax.ShapeDtypeStruct((slots, width, width), jnp.float32),
        in_specs=[pl.BlockSpec(memory_space=pltpu.SMEM)] * 3 + [pl.BlockSpec(memory_space=pl.ANY)] * 2,
        out_specs=pl.BlockSpec(memory_space=pl.ANY),
        scratch_shapes=[
            pltpu.VMEM((devices + 1, rows, width), jnp.bfloat16),
            pltpu.VMEM((rows, width), jnp.bfloat16),
            pltpu.VMEM((BUFFERS, width, width), jnp.float32),
            pltpu.VMEM((width, width), jnp.float32),
            pltpu.SemaphoreType.DMA((devices,)),
            pltpu.SemaphoreType.DMA,
            pltpu.SemaphoreType.DMA((BUFFERS,)),
            pltpu.SemaphoreType.DMA((slots,)),
        ],
        compiler_params=pltpu.CompilerParams(vmem_limit_bytes=50 * 1024 * 1024),
    )(tile_owner, device.reshape(1), scale.reshape(1), x, mask)


def ring_plan(devices):
    chips = devices // 2
    order = list(range(0, chips, 2)) + list(range(1, chips, 2))[::-1]
    place = {chip: at for at, chip in enumerate(order)}
    onward = []
    for device in range(devices):
        chip, core = divmod(device, 2)
        onward.append(order[(place[chip] + 1) % chips] * 2 + core)
    backward = [onward.index(device) for device in range(devices)]
    return onward, backward


GROUPS = ((0, 1, 2), (8, 9, 10), (3, 4), (11, 12), (6,), (14,), (7,), (15,), (5,), (13,))


def first_needed(devices, chip):
    return (2 * chip - devices // 2 - devices // 8 + devices) % devices


def ring_gather(tokens, device, devices):
    onward, backward = ring_plan(devices)
    sibling = [device ^ 1 for device in range(devices)]
    over = [at ^ 12 if at // 4 in (0, 3) else at ^ 2 for at in range(devices)]

    def send(value, target):
        return lax.ppermute(value, "col", list(enumerate(target)))

    def after(value, *others):
        return lax.optimization_barrier((value, *others))[0]

    chip, chips = device // 2, devices // 2
    even = chip % 2 == 0
    next_chip = jnp.where(even, jnp.where(chip == chips - 2, chips - 1, chip + 2), jnp.where(chip == 1, 0, chip - 2))
    last_chip = jnp.where(even, jnp.where(chip == 0, 1, chip - 2), jnp.where(chip == chips - 1, chips - 2, chip + 2))
    over_chip = jnp.where((chip < 2) | (chip >= chips - 2), chip ^ 6, chip ^ 1)
    chip, chips = device // 2, devices // 2
    even = chip % 2 == 0
    next_chip = jnp.where(even, jnp.where(chip == chips - 2, chips - 1, chip + 2), jnp.where(chip == 1, 0, chip - 2))
    last_chip = jnp.where(even, jnp.where(chip == 0, 1, chip - 2), jnp.where(chip == chips - 1, chips - 2, chip + 2))
    over_chip = jnp.where((chip < 2) | (chip >= chips - 2), chip ^ 6, chip ^ 1)
    came_ahead = (chip % 4 == 0) | (chip % 4 == 3)
    slab, units = tokens.shape
    needed = devices // 2 + devices // 8 + 2

    def window(value, chip):
        blocks = value.reshape(slab, devices, units // devices)
        blocks = jnp.concatenate([blocks, blocks], axis=1)
        blocks = lax.dynamic_slice_in_dim(blocks, first_needed(devices, chip), needed, axis=1)
        return blocks.reshape(slab, -1)

    ahead, back = [tokens], [tokens]
    for _ in range(2):
        ahead.append(send(ahead[-1], onward))
        back.append(send(back[-1], backward))
    half = send(window(jnp.where(came_ahead, ahead[1], back[1]), over_chip), over)
    ahead.append(send(window(ahead[2], next_chip), onward))
    back.append(send(window(back[2], last_chip), backward))
    near = jnp.concatenate((tokens, ahead[1], back[1]), axis=0)
    middle = jnp.concatenate((ahead[2], back[2]), axis=0)
    near_beside = send(near, sibling)
    middle_beside = send(jnp.concatenate((window(ahead[2], chip), window(back[2], chip)), axis=0), sibling)
    groups = [near, near_beside, middle, middle_beside]
    for value in (back[3], half, ahead[3]):
        groups += [value, send(after(value, back[3]) if value is half else value, sibling)]
    return groups


def slab_origin(devices, device, number):
    chips = devices // 2
    number, flip = number % chips, number // chips
    hops = (number + 1) // 2 if number % 2 else -(number // 2)
    chip, core = device // 2, device % 2
    core = 1 - core if flip else core
    place = jnp.where(chip % 2 == 0, chip // 2, chips - 1 - chip // 2)
    place = (place - hops + chips) % chips
    chip = jnp.where(2 * place < chips, 2 * place, 2 * (chips - 1 - place) + 1)
    return 2 * chip + core


def ring_kernel(devices, slots, table_ref, *refs):
    groups = refs[:len(GROUPS)]
    out_ref, pair, tiles, zeros, out_sems, zero_sems = refs[len(GROUPS):]
    device = table_ref[table_ref.shape[0] - 1]
    slab, width = pair.shape[1] // devices, pair.shape[2]
    first = first_needed(devices, device // 2)

    def owned(partner):
        return table_ref[devices + tile_number(devices, device, partner)] == device

    def put(buffer, slot):
        return pltpu.make_async_copy(tiles.at[buffer], out_ref.at[slot], out_sems.at[buffer])

    def clear(slot):
        return pltpu.make_async_copy(zeros, out_ref.at[slot], zero_sems.at[slot])

    def load_block(partner, masked):
        parts = []
        for numbers, ref in zip(GROUPS, groups):
            place = partner
            if ref.shape[1] < devices * width:
                place = lax.rem(partner - first + devices, devices)
            group = ref[:, pl.ds(pl.multiple_of(place * width, 128), width)].astype(jnp.float32)
            for at, number in enumerate(numbers):
                part = group[at * slab:(at + 1) * slab]
                if masked:
                    row = lax.broadcasted_iota(jnp.int32, (slab, width), 0)
                    part = jnp.where(row < table_ref[slab_origin(devices, device, number)], part, 0.0)
                parts.append(part)
        pair[0 if masked else 1] = jnp.concatenate(parts, axis=0).astype(jnp.bfloat16)

    load_block(device, True)
    valid_count = table_ref[0]
    for at in range(1, devices):
        valid_count = valid_count + table_ref[at]
    scale = 1.0 / jnp.full((8, width), valid_count.astype(jnp.float32))

    def visit(partner, slot):
        mine = owned(partner)

        @pl.when(mine)
        def _():
            buffer = lax.rem(slot, BUFFERS)
            load_block(partner, False)

            @pl.when(slot >= BUFFERS)
            def _():
                put(buffer, slot - BUFFERS).wait()

            left = (partner <= device).astype(jnp.int32)
            for row in range(0, width, STRIP):
                rows = min(STRIP, width - row)
                strip = pl.ds(row, rows)
                product = lax.dot_general(
                    pair[left, :, row:row + rows], pair[1 - left], (((0,), (0,)), ((), ())),
                    preferred_element_type=jnp.float32,
                )
                tiles[buffer, strip, :] = product * scale[:1]
                pltpu.make_async_copy(
                    tiles.at[buffer, strip], out_ref.at[slot, strip], out_sems.at[buffer]
                ).start()

        return slot + mine.astype(jnp.int32)

    count = lax.fori_loop(0, devices, visit, jnp.int32(0))

    @pl.when(count < slots)
    def _():
        zeros[...] = jnp.zeros_like(zeros)

    def start_clear(slot, carry):
        clear(slot).start()
        return carry

    lax.fori_loop(count, slots, start_clear, 0)

    def drain(slot, carry):
        put(lax.rem(slot, BUFFERS), slot).wait()
        return carry

    lax.fori_loop(jnp.maximum(count - BUFFERS, 0), count, drain, 0)

    def end_clear(slot, carry):
        clear(slot).wait()
        return carry

    lax.fori_loop(count, slots, end_clear, 0)


def ring_form(tokens, slab_lengths, tile_owner, devices, device, slots):
    slab, units = tokens.shape
    width = units // devices
    groups = ring_gather(tokens, device, devices)
    table = jnp.concatenate([slab_lengths, tile_owner, device.reshape(1)])
    return pl.pallas_call(
        functools.partial(ring_kernel, devices, slots),
        out_shape=jax.ShapeDtypeStruct((slots, width, width), jnp.float32),
        in_specs=[pl.BlockSpec(memory_space=pltpu.SMEM)]
        + [pl.BlockSpec(memory_space=pltpu.VMEM)] * len(groups),
        out_specs=pl.BlockSpec(memory_space=pl.ANY),
        scratch_shapes=[
            pltpu.VMEM((2, slab * devices, width), jnp.bfloat16),
            pltpu.VMEM((BUFFERS, width, width), jnp.float32),
            pltpu.VMEM((width, width), jnp.float32),
            pltpu.SemaphoreType.DMA((BUFFERS,)),
            pltpu.SemaphoreType.DMA((slots,)),
        ],
        compiler_params=pltpu.CompilerParams(vmem_limit_bytes=32 * 1024 * 1024),
        cost_estimate=pl.CostEstimate(
            flops=2 * slots * slab * devices * width * width,
            bytes_accessed=4 * slots * width * width,
            transcendentals=0,
        ),
    )(table, *groups)


def per_device(tokens, slab_lengths, tile_owner):
    devices = lax.axis_size("col")
    device = lax.axis_index("col").astype(jnp.int32)
    slots = devices // 2 + devices // 8 + 1
    width = tokens.shape[1] // devices
    form = ring_form if devices == RING_DEVICES and width % 128 == 0 else gathered_form
    return form(tokens, slab_lengths, tile_owner, devices, device, slots)


def solution(mesh):
    return jax.shard_map(
        per_device,
        mesh=mesh,
        in_specs=(P(("grp", "col"), None), P("grp"), P()),
        out_specs=P(("grp", "col"), None, None),
        check_vma=False,
    )
```

```python
import functools

import jax
import jax.numpy as jnp
from jax import lax
from jax.experimental import pallas as pl
from jax.experimental.pallas import tpu as pltpu
from jax.sharding import PartitionSpec as P

BUFFERS = 4
STRIP = 256
RING_DEVICES = 16


def tile_number(devices, device, partner):
    low = jnp.minimum(device, partner)
    high = jnp.maximum(device, partner)
    return low * devices - low * (low - 1) // 2 + (high - low)


def gathered_kernel(
    devices, slots, owner_ref, device_ref, scale_ref, x_ref, mask_ref,
    out_ref, blocks, mask, tiles, zeros, in_sems, mask_sem, out_sems, zero_sems,
):
    device = device_ref[0]
    width = blocks.shape[2]

    def owned(partner):
        return owner_ref[tile_number(devices, device, partner)] == device

    def fetch(partner):
        return pltpu.make_async_copy(x_ref.at[partner], blocks.at[partner], in_sems.at[partner])

    def put(buffer, slot):
        return pltpu.make_async_copy(tiles.at[buffer], out_ref.at[slot], out_sems.at[buffer])

    def clear(slot):
        return pltpu.make_async_copy(zeros, out_ref.at[slot], zero_sems.at[slot])

    mask_copy = pltpu.make_async_copy(mask_ref, mask, mask_sem)
    mask_copy.start()
    fetch(device).start()

    def start_fetch(partner, count):
        mine = owned(partner)

        @pl.when(mine & (partner != device))
        def _():
            fetch(partner).start()

        return count + mine.astype(jnp.int32)

    count = lax.fori_loop(0, devices, start_fetch, jnp.int32(0))

    zeros[...] = jnp.zeros_like(zeros)

    def start_clear(slot, carry):
        clear(slot).start()
        return carry

    lax.fori_loop(count, slots, start_clear, 0)

    mask_copy.wait()
    fetch(device).wait()
    blocks[devices] = blocks[device] * mask[...]
    scale = scale_ref[0]

    def visit(partner, slot):
        mine = owned(partner)

        @pl.when(mine)
        def _():
            @pl.when(partner != device)
            def _():
                fetch(partner).wait()

            buffer = lax.rem(slot, BUFFERS)

            @pl.when(slot >= BUFFERS)
            def _():
                put(buffer, slot - BUFFERS).wait()

            left = jnp.where(partner <= device, partner, devices)
            right = jnp.where(partner <= device, devices, partner)
            product = lax.dot_general(
                blocks[left], blocks[right], (((0,), (0,)), ((), ())),
                preferred_element_type=jnp.float32,
            )
            tiles[buffer] = product * scale
            put(buffer, slot).start()

        return slot + mine.astype(jnp.int32)

    lax.fori_loop(0, devices, visit, jnp.int32(0))

    def drain(slot, carry):
        put(lax.rem(slot, BUFFERS), slot).wait()
        return carry

    lax.fori_loop(jnp.maximum(count - BUFFERS, 0), count, drain, 0)

    def end_clear(slot, carry):
        clear(slot).wait()
        return carry

    lax.fori_loop(count, slots, end_clear, 0)


def gathered_form(tokens, slab_lengths, tile_owner, devices, device, slots):
    slab, units = tokens.shape
    rows = slab * devices
    width = units // devices
    x = lax.all_gather(tokens, "col", axis=0, tiled=True)
    x = x.reshape(rows, devices, width).transpose(1, 0, 2)
    scale = 1.0 / jnp.sum(slab_lengths).astype(jnp.float32)
    valid = jnp.arange(slab, dtype=jnp.int32)[None, :] < slab_lengths[:, None]
    mask = jnp.broadcast_to(valid.reshape(rows, 1), (rows, width)).astype(jnp.bfloat16)
    return pl.pallas_call(
        functools.partial(gathered_kernel, devices, slots),
        out_shape=jax.ShapeDtypeStruct((slots, width, width), jnp.float32),
        in_specs=[pl.BlockSpec(memory_space=pltpu.SMEM)] * 3 + [pl.BlockSpec(memory_space=pl.ANY)] * 2,
        out_specs=pl.BlockSpec(memory_space=pl.ANY),
        scratch_shapes=[
            pltpu.VMEM((devices + 1, rows, width), jnp.bfloat16),
            pltpu.VMEM((rows, width), jnp.bfloat16),
            pltpu.VMEM((BUFFERS, width, width), jnp.float32),
            pltpu.VMEM((width, width), jnp.float32),
            pltpu.SemaphoreType.DMA((devices,)),
            pltpu.SemaphoreType.DMA,
            pltpu.SemaphoreType.DMA((BUFFERS,)),
            pltpu.SemaphoreType.DMA((slots,)),
        ],
        compiler_params=pltpu.CompilerParams(vmem_limit_bytes=50 * 1024 * 1024),
    )(tile_owner, device.reshape(1), scale.reshape(1), x, mask)


def ring_plan(devices):
    chips = devices // 2
    order = list(range(0, chips, 2)) + list(range(1, chips, 2))[::-1]
    place = {chip: at for at, chip in enumerate(order)}
    onward = []
    for device in range(devices):
        chip, core = divmod(device, 2)
        onward.append(order[(place[chip] - 1) % chips] * 2 + core)
    backward = [onward.index(device) for device in range(devices)]
    return onward, backward


GROUPS = ((0, 1, 2), (8, 9, 10), (3, 4), (11, 12), (5, 7), (13, 15), (6,), (14,))


def first_needed(devices, chip):
    return (2 * chip - devices // 2 - devices // 8 + devices) % devices


def ring_gather(tokens, device, devices):
    onward, backward = ring_plan(devices)
    sibling = [device ^ 1 for device in range(devices)]
    over = [at ^ 12 if at // 4 in (0, 3) else at ^ 2 for at in range(devices)]

    def send(value, target):
        return lax.ppermute(value, "col", list(enumerate(target)))

    def after(value, *others):
        return lax.optimization_barrier((value, *others))[0]

    chip, chips = device // 2, devices // 2
    even = chip % 2 == 0
    next_chip = jnp.where(even, jnp.where(chip == chips - 2, chips - 1, chip + 2), jnp.where(chip == 1, 0, chip - 2))
    last_chip = jnp.where(even, jnp.where(chip == 0, 1, chip - 2), jnp.where(chip == chips - 1, chips - 2, chip + 2))
    over_chip = jnp.where((chip < 2) | (chip >= chips - 2), chip ^ 6, chip ^ 1)
    chip, chips = device // 2, devices // 2
    even = chip % 2 == 0
    next_chip = jnp.where(even, jnp.where(chip == chips - 2, chips - 1, chip + 2), jnp.where(chip == 1, 0, chip - 2))
    last_chip = jnp.where(even, jnp.where(chip == 0, 1, chip - 2), jnp.where(chip == chips - 1, chips - 2, chip + 2))
    over_chip = jnp.where((chip < 2) | (chip >= chips - 2), chip ^ 6, chip ^ 1)
    came_ahead = (chip % 4 == 1) | (chip % 4 == 2)
    slab, units = tokens.shape
    needed = devices // 2 + devices // 8 + 2

    def window(value, chip):
        blocks = value.reshape(slab, devices, units // devices)
        blocks = jnp.concatenate([blocks, blocks], axis=1)
        blocks = lax.dynamic_slice_in_dim(blocks, first_needed(devices, chip), needed, axis=1)
        return blocks.reshape(slab, -1)

    ahead, back = [tokens], [tokens]
    for _ in range(2):
        ahead.append(send(ahead[-1], onward))
        back.append(send(back[-1], backward))
    half = send(window(jnp.where(came_ahead, ahead[1], back[1]), over_chip), over)
    ahead.append(send(window(ahead[2], last_chip), onward))
    back.append(send(window(back[2], next_chip), backward))
    near = jnp.concatenate((tokens, ahead[1], back[1]), axis=0)
    middle = jnp.concatenate((ahead[2], back[2]), axis=0)
    last = jnp.concatenate((ahead[3], half), axis=0)
    near_beside = send(near, sibling)
    middle_beside = send(middle, sibling)
    last_beside = send(after(last, middle_beside), sibling)
    return [near, near_beside, middle, middle_beside, last, last_beside, back[3], send(back[3], sibling)]

def slab_origin(devices, device, number):
    chips = devices // 2
    number, flip = number % chips, number // chips
    hops = (number + 1) // 2 if number % 2 else -(number // 2)
    chip, core = device // 2, device % 2
    core = 1 - core if flip else core
    place = jnp.where(chip % 2 == 0, chip // 2, chips - 1 - chip // 2)
    place = (place + hops + chips) % chips
    chip = jnp.where(2 * place < chips, 2 * place, 2 * (chips - 1 - place) + 1)
    return 2 * chip + core


def ring_kernel(devices, slots, device_ref, table_ref, *refs):
    groups = refs[:len(GROUPS)]
    out_ref, pair, tiles, zeros, out_sems, zero_sems = refs[len(GROUPS):]
    device = device_ref[0]
    slab, width = pair.shape[1] // devices, pair.shape[2]
    first = first_needed(devices, device // 2)

    def owned(partner):
        return table_ref[devices + tile_number(devices, device, partner)] == device

    def put(buffer, slot):
        return pltpu.make_async_copy(tiles.at[buffer], out_ref.at[slot], out_sems.at[buffer])

    def clear(slot):
        return pltpu.make_async_copy(zeros, out_ref.at[slot], zero_sems.at[slot])

    def load_block(partner, masked):
        parts = []
        for numbers, ref in zip(GROUPS, groups):
            place = partner
            if ref.shape[1] < devices * width:
                place = lax.rem(partner - first + devices, devices)
            group = ref[:, pl.ds(pl.multiple_of(place * width, 128), width)].astype(jnp.float32)
            for at, number in enumerate(numbers):
                part = group[at * slab:(at + 1) * slab]
                if masked:
                    row = lax.broadcasted_iota(jnp.int32, (slab, width), 0)
                    part = jnp.where(row < table_ref[slab_origin(devices, device, number)], part, 0.0)
                parts.append(part)
        pair[0 if masked else 1] = jnp.concatenate(parts, axis=0).astype(jnp.bfloat16)

    load_block(device, True)
    valid_count = table_ref[0]
    for at in range(1, devices):
        valid_count = valid_count + table_ref[at]
    scale = 1.0 / jnp.full((8, width), valid_count.astype(jnp.float32))

    def visit(partner, slot):
        mine = owned(partner)

        @pl.when(mine)
        def _():
            buffer = lax.rem(slot, BUFFERS)
            load_block(partner, False)

            @pl.when(slot >= BUFFERS)
            def _():
                put(buffer, slot - BUFFERS).wait()

            left = (partner <= device).astype(jnp.int32)
            for row in range(0, width, STRIP):
                rows = min(STRIP, width - row)
                strip = pl.ds(row, rows)
                product = lax.dot_general(
                    pair[left, :, row:row + rows], pair[1 - left], (((0,), (0,)), ((), ())),
                    preferred_element_type=jnp.float32,
                )
                tiles[buffer, strip, :] = product * scale[:1]
                pltpu.make_async_copy(
                    tiles.at[buffer, strip], out_ref.at[slot, strip], out_sems.at[buffer]
                ).start()

        return slot + mine.astype(jnp.int32)

    count = lax.fori_loop(0, devices, visit, jnp.int32(0))

    @pl.when(count < slots)
    def _():
        zeros[...] = jnp.zeros_like(zeros)

    def start_clear(slot, carry):
        clear(slot).start()
        return carry

    lax.fori_loop(count, slots, start_clear, 0)

    def drain(slot, carry):
        put(lax.rem(slot, BUFFERS), slot).wait()
        return carry

    lax.fori_loop(jnp.maximum(count - BUFFERS, 0), count, drain, 0)

    def end_clear(slot, carry):
        clear(slot).wait()
        return carry

    lax.fori_loop(count, slots, end_clear, 0)


def ring_form(tokens, slab_lengths, tile_owner, devices, device, slots):
    slab, units = tokens.shape
    width = units // devices
    groups = ring_gather(tokens, device, devices)
    table = jnp.concatenate([slab_lengths, tile_owner])
    return pl.pallas_call(
        functools.partial(ring_kernel, devices, slots),
        out_shape=jax.ShapeDtypeStruct((slots, width, width), jnp.float32),
        in_specs=[pl.BlockSpec(memory_space=pltpu.SMEM)] * 2
        + [pl.BlockSpec(memory_space=pltpu.VMEM)] * len(groups),
        out_specs=pl.BlockSpec(memory_space=pl.ANY),
        scratch_shapes=[
            pltpu.VMEM((2, slab * devices, width), jnp.bfloat16),
            pltpu.VMEM((BUFFERS, width, width), jnp.float32),
            pltpu.VMEM((width, width), jnp.float32),
            pltpu.SemaphoreType.DMA((BUFFERS,)),
            pltpu.SemaphoreType.DMA((slots,)),
        ],
        compiler_params=pltpu.CompilerParams(vmem_limit_bytes=32 * 1024 * 1024),
        cost_estimate=pl.CostEstimate(
            flops=2 * slots * slab * devices * width * width,
            bytes_accessed=4 * slots * width * width,
            transcendentals=0,
        ),
    )(device.reshape(1), table, *groups)


def per_device(tokens, slab_lengths, tile_owner):
    devices = lax.axis_size("col")
    device = lax.axis_index("col").astype(jnp.int32)
    slots = devices // 2 + devices // 8 + 1
    width = tokens.shape[1] // devices
    form = ring_form if devices == RING_DEVICES and width % 128 == 0 else gathered_form
    return form(tokens, slab_lengths, tile_owner, devices, device, slots)


def solution(mesh):
    return jax.shard_map(
        per_device,
        mesh=mesh,
        in_specs=(P(("grp", "col"), None), P("grp"), P()),
        out_specs=P(("grp", "col"), None, None),
        check_vma=False,
    )
```

```python
import functools

import jax
import jax.numpy as jnp
from jax import lax
from jax.experimental import pallas as pl
from jax.experimental.pallas import tpu as pltpu
from jax.sharding import PartitionSpec as P

BUFFERS = 4
STRIP = 256
RING_DEVICES = 16


def tile_number(devices, device, partner):
    low = jnp.minimum(device, partner)
    high = jnp.maximum(device, partner)
    return low * devices - low * (low - 1) // 2 + (high - low)


def gathered_kernel(
    devices, slots, owner_ref, device_ref, scale_ref, x_ref, mask_ref,
    out_ref, blocks, mask, tiles, zeros, in_sems, mask_sem, out_sems, zero_sems,
):
    device = device_ref[0]
    width = blocks.shape[2]

    def owned(partner):
        return owner_ref[tile_number(devices, device, partner)] == device

    def fetch(partner):
        return pltpu.make_async_copy(x_ref.at[partner], blocks.at[partner], in_sems.at[partner])

    def put(buffer, slot):
        return pltpu.make_async_copy(tiles.at[buffer], out_ref.at[slot], out_sems.at[buffer])

    def clear(slot):
        return pltpu.make_async_copy(zeros, out_ref.at[slot], zero_sems.at[slot])

    mask_copy = pltpu.make_async_copy(mask_ref, mask, mask_sem)
    mask_copy.start()
    fetch(device).start()

    def start_fetch(partner, count):
        mine = owned(partner)

        @pl.when(mine & (partner != device))
        def _():
            fetch(partner).start()

        return count + mine.astype(jnp.int32)

    count = lax.fori_loop(0, devices, start_fetch, jnp.int32(0))

    zeros[...] = jnp.zeros_like(zeros)

    def start_clear(slot, carry):
        clear(slot).start()
        return carry

    lax.fori_loop(count, slots, start_clear, 0)

    mask_copy.wait()
    fetch(device).wait()
    blocks[devices] = blocks[device] * mask[...]
    scale = scale_ref[0]

    def visit(partner, slot):
        mine = owned(partner)

        @pl.when(mine)
        def _():
            @pl.when(partner != device)
            def _():
                fetch(partner).wait()

            buffer = lax.rem(slot, BUFFERS)

            @pl.when(slot >= BUFFERS)
            def _():
                put(buffer, slot - BUFFERS).wait()

            left = jnp.where(partner <= device, partner, devices)
            right = jnp.where(partner <= device, devices, partner)
            product = lax.dot_general(
                blocks[left], blocks[right], (((0,), (0,)), ((), ())),
                preferred_element_type=jnp.float32,
            )
            tiles[buffer] = product * scale
            put(buffer, slot).start()

        return slot + mine.astype(jnp.int32)

    lax.fori_loop(0, devices, visit, jnp.int32(0))

    def drain(slot, carry):
        put(lax.rem(slot, BUFFERS), slot).wait()
        return carry

    lax.fori_loop(jnp.maximum(count - BUFFERS, 0), count, drain, 0)

    def end_clear(slot, carry):
        clear(slot).wait()
        return carry

    lax.fori_loop(count, slots, end_clear, 0)


def gathered_form(tokens, slab_lengths, tile_owner, devices, device, slots):
    slab, units = tokens.shape
    rows = slab * devices
    width = units // devices
    x = lax.all_gather(tokens, "col", axis=0, tiled=True)
    x = x.reshape(rows, devices, width).transpose(1, 0, 2)
    scale = 1.0 / jnp.sum(slab_lengths).astype(jnp.float32)
    valid = jnp.arange(slab, dtype=jnp.int32)[None, :] < slab_lengths[:, None]
    mask = jnp.broadcast_to(valid.reshape(rows, 1), (rows, width)).astype(jnp.bfloat16)
    return pl.pallas_call(
        functools.partial(gathered_kernel, devices, slots),
        out_shape=jax.ShapeDtypeStruct((slots, width, width), jnp.float32),
        in_specs=[pl.BlockSpec(memory_space=pltpu.SMEM)] * 3 + [pl.BlockSpec(memory_space=pl.ANY)] * 2,
        out_specs=pl.BlockSpec(memory_space=pl.ANY),
        scratch_shapes=[
            pltpu.VMEM((devices + 1, rows, width), jnp.bfloat16),
            pltpu.VMEM((rows, width), jnp.bfloat16),
            pltpu.VMEM((BUFFERS, width, width), jnp.float32),
            pltpu.VMEM((width, width), jnp.float32),
            pltpu.SemaphoreType.DMA((devices,)),
            pltpu.SemaphoreType.DMA,
            pltpu.SemaphoreType.DMA((BUFFERS,)),
            pltpu.SemaphoreType.DMA((slots,)),
        ],
        compiler_params=pltpu.CompilerParams(vmem_limit_bytes=50 * 1024 * 1024),
    )(tile_owner, device.reshape(1), scale.reshape(1), x, mask)


def ring_plan(devices):
    chips = devices // 2
    order = list(range(0, chips, 2)) + list(range(1, chips, 2))[::-1]
    place = {chip: at for at, chip in enumerate(order)}
    onward = []
    for device in range(devices):
        chip, core = divmod(device, 2)
        onward.append(order[(place[chip] - 1) % chips] * 2 + core)
    backward = [onward.index(device) for device in range(devices)]
    return onward, backward


GROUPS = ((0, 1, 2), (8, 9, 10), (3, 4), (11, 12), (5, 7), (13, 15), (6,), (14,))


def first_needed(devices, chip):
    return (2 * chip - devices // 2 - devices // 8 + devices) % devices


def ring_gather(tokens, device, devices):
    onward, backward = ring_plan(devices)
    sibling = [device ^ 1 for device in range(devices)]
    over = [at ^ 12 if at // 4 in (0, 3) else at ^ 2 for at in range(devices)]

    def send(value, target):
        return lax.ppermute(value, "col", list(enumerate(target)))

    def after(value, *others):
        return lax.optimization_barrier((value, *others))[0]

    chip, chips = device // 2, devices // 2
    even = chip % 2 == 0
    next_chip = jnp.where(even, jnp.where(chip == chips - 2, chips - 1, chip + 2), jnp.where(chip == 1, 0, chip - 2))
    last_chip = jnp.where(even, jnp.where(chip == 0, 1, chip - 2), jnp.where(chip == chips - 1, chips - 2, chip + 2))
    over_chip = jnp.where((chip < 2) | (chip >= chips - 2), chip ^ 6, chip ^ 1)
    chip, chips = device // 2, devices // 2
    even = chip % 2 == 0
    next_chip = jnp.where(even, jnp.where(chip == chips - 2, chips - 1, chip + 2), jnp.where(chip == 1, 0, chip - 2))
    last_chip = jnp.where(even, jnp.where(chip == 0, 1, chip - 2), jnp.where(chip == chips - 1, chips - 2, chip + 2))
    over_chip = jnp.where((chip < 2) | (chip >= chips - 2), chip ^ 6, chip ^ 1)
    came_ahead = (chip % 4 == 1) | (chip % 4 == 2)
    slab, units = tokens.shape
    needed = devices // 2 + devices // 8 + 2

    def window(value, chip):
        blocks = value.reshape(slab, devices, units // devices)
        blocks = jnp.concatenate([blocks, blocks], axis=1)
        blocks = lax.dynamic_slice_in_dim(blocks, first_needed(devices, chip), needed, axis=1)
        return blocks.reshape(slab, -1)

    ahead, back = [tokens], [tokens]
    for _ in range(2):
        ahead.append(send(ahead[-1], onward))
        back.append(send(back[-1], backward))
    half = send(window(jnp.where(came_ahead, ahead[1], back[1]), over_chip), over)
    ahead.append(send(window(ahead[2], last_chip), onward))
    back.append(send(window(back[2], next_chip), backward))
    near = jnp.concatenate((tokens, ahead[1], back[1]), axis=0)
    middle = jnp.concatenate((ahead[2], back[2]), axis=0)
    last = jnp.concatenate((ahead[3], half), axis=0)
    near_beside = send(near, sibling)
    needed = [window(after(value, ahead[2], back[2]), chip) for value in (ahead[2], back[2])]
    middle_beside = send(jnp.concatenate(needed, axis=0), sibling)
    last_beside = send(last, sibling)
    return [near, near_beside, middle, middle_beside, last, last_beside, back[3], send(back[3], sibling)]

def slab_origin(devices, device, number):
    chips = devices // 2
    number, flip = number % chips, number // chips
    hops = (number + 1) // 2 if number % 2 else -(number // 2)
    chip, core = device // 2, device % 2
    core = 1 - core if flip else core
    place = jnp.where(chip % 2 == 0, chip // 2, chips - 1 - chip // 2)
    place = (place + hops + chips) % chips
    chip = jnp.where(2 * place < chips, 2 * place, 2 * (chips - 1 - place) + 1)
    return 2 * chip + core


def ring_kernel(devices, slots, device_ref, table_ref, *refs):
    groups = refs[:len(GROUPS)]
    out_ref, pair, tiles, zeros, out_sems, zero_sems = refs[len(GROUPS):]
    device = device_ref[0]
    slab, width = pair.shape[1] // devices, pair.shape[2]
    first = first_needed(devices, device // 2)

    def owned(partner):
        return table_ref[devices + tile_number(devices, device, partner)] == device

    def put(buffer, slot):
        return pltpu.make_async_copy(tiles.at[buffer], out_ref.at[slot], out_sems.at[buffer])

    def clear(slot):
        return pltpu.make_async_copy(zeros, out_ref.at[slot], zero_sems.at[slot])

    def load_block(partner, masked):
        parts = []
        for numbers, ref in zip(GROUPS, groups):
            place = partner
            if ref.shape[1] < devices * width:
                place = lax.rem(partner - first + devices, devices)
            group = ref[:, pl.ds(pl.multiple_of(place * width, 128), width)].astype(jnp.float32)
            for at, number in enumerate(numbers):
                part = group[at * slab:(at + 1) * slab]
                if masked:
                    row = lax.broadcasted_iota(jnp.int32, (slab, width), 0)
                    part = jnp.where(row < table_ref[slab_origin(devices, device, number)], part, 0.0)
                parts.append(part)
        pair[0 if masked else 1] = jnp.concatenate(parts, axis=0).astype(jnp.bfloat16)

    load_block(device, True)
    valid_count = table_ref[0]
    for at in range(1, devices):
        valid_count = valid_count + table_ref[at]
    scale = 1.0 / jnp.full((8, width), valid_count.astype(jnp.float32))

    def visit(partner, slot):
        mine = owned(partner)

        @pl.when(mine)
        def _():
            buffer = lax.rem(slot, BUFFERS)
            load_block(partner, False)

            @pl.when(slot >= BUFFERS)
            def _():
                put(buffer, slot - BUFFERS).wait()

            left = (partner <= device).astype(jnp.int32)
            for row in range(0, width, STRIP):
                rows = min(STRIP, width - row)
                strip = pl.ds(row, rows)
                product = lax.dot_general(
                    pair[left, :, row:row + rows], pair[1 - left], (((0,), (0,)), ((), ())),
                    preferred_element_type=jnp.float32,
                )
                tiles[buffer, strip, :] = product * scale[:1]
                pltpu.make_async_copy(
                    tiles.at[buffer, strip], out_ref.at[slot, strip], out_sems.at[buffer]
                ).start()

        return slot + mine.astype(jnp.int32)

    count = lax.fori_loop(0, devices, visit, jnp.int32(0))

    @pl.when(count < slots)
    def _():
        zeros[...] = jnp.zeros_like(zeros)

    def start_clear(slot, carry):
        clear(slot).start()
        return carry

    lax.fori_loop(count, slots, start_clear, 0)

    def drain(slot, carry):
        put(lax.rem(slot, BUFFERS), slot).wait()
        return carry

    lax.fori_loop(jnp.maximum(count - BUFFERS, 0), count, drain, 0)

    def end_clear(slot, carry):
        clear(slot).wait()
        return carry

    lax.fori_loop(count, slots, end_clear, 0)


def ring_form(tokens, slab_lengths, tile_owner, devices, device, slots):
    slab, units = tokens.shape
    width = units // devices
    groups = ring_gather(tokens, device, devices)
    table = jnp.concatenate([slab_lengths, tile_owner])
    return pl.pallas_call(
        functools.partial(ring_kernel, devices, slots),
        out_shape=jax.ShapeDtypeStruct((slots, width, width), jnp.float32),
        in_specs=[pl.BlockSpec(memory_space=pltpu.SMEM)] * 2
        + [pl.BlockSpec(memory_space=pltpu.VMEM)] * len(groups),
        out_specs=pl.BlockSpec(memory_space=pl.ANY),
        scratch_shapes=[
            pltpu.VMEM((2, slab * devices, width), jnp.bfloat16),
            pltpu.VMEM((BUFFERS, width, width), jnp.float32),
            pltpu.VMEM((width, width), jnp.float32),
            pltpu.SemaphoreType.DMA((BUFFERS,)),
            pltpu.SemaphoreType.DMA((slots,)),
        ],
        compiler_params=pltpu.CompilerParams(vmem_limit_bytes=32 * 1024 * 1024),
        cost_estimate=pl.CostEstimate(
            flops=2 * slots * slab * devices * width * width,
            bytes_accessed=4 * slots * width * width,
            transcendentals=0,
        ),
    )(device.reshape(1), table, *groups)


def per_device(tokens, slab_lengths, tile_owner):
    devices = lax.axis_size("col")
    device = lax.axis_index("col").astype(jnp.int32)
    slots = devices // 2 + devices // 8 + 1
    width = tokens.shape[1] // devices
    form = ring_form if devices == RING_DEVICES and width % 128 == 0 else gathered_form
    return form(tokens, slab_lengths, tile_owner, devices, device, slots)


def solution(mesh):
    return jax.shard_map(
        per_device,
        mesh=mesh,
        in_specs=(P(("grp", "col"), None), P("grp"), P()),
        out_specs=P(("grp", "col"), None, None),
        check_vma=False,
    )
```

```python
import functools

import jax
import jax.numpy as jnp
from jax import lax
from jax.experimental import pallas as pl
from jax.experimental.pallas import tpu as pltpu
from jax.sharding import PartitionSpec as P

BUFFERS = 4
STRIP = 128
RING_DEVICES = 16


def tile_number(devices, device, partner):
    low = jnp.minimum(device, partner)
    high = jnp.maximum(device, partner)
    return low * devices - low * (low - 1) // 2 + (high - low)


def gathered_kernel(
    devices, slots, owner_ref, device_ref, scale_ref, x_ref, mask_ref,
    out_ref, blocks, mask, tiles, zeros, in_sems, mask_sem, out_sems, zero_sems,
):
    device = device_ref[0]
    width = blocks.shape[2]

    def owned(partner):
        return owner_ref[tile_number(devices, device, partner)] == device

    def fetch(partner):
        return pltpu.make_async_copy(x_ref.at[partner], blocks.at[partner], in_sems.at[partner])

    def put(buffer, slot):
        return pltpu.make_async_copy(tiles.at[buffer], out_ref.at[slot], out_sems.at[buffer])

    def clear(slot):
        return pltpu.make_async_copy(zeros, out_ref.at[slot], zero_sems.at[slot])

    mask_copy = pltpu.make_async_copy(mask_ref, mask, mask_sem)
    mask_copy.start()
    fetch(device).start()

    def start_fetch(partner, count):
        mine = owned(partner)

        @pl.when(mine & (partner != device))
        def _():
            fetch(partner).start()

        return count + mine.astype(jnp.int32)

    count = lax.fori_loop(0, devices, start_fetch, jnp.int32(0))

    zeros[...] = jnp.zeros_like(zeros)

    def start_clear(slot, carry):
        clear(slot).start()
        return carry

    lax.fori_loop(count, slots, start_clear, 0)

    mask_copy.wait()
    fetch(device).wait()
    blocks[devices] = blocks[device] * mask[...]
    scale = scale_ref[0]

    def visit(partner, slot):
        mine = owned(partner)

        @pl.when(mine)
        def _():
            @pl.when(partner != device)
            def _():
                fetch(partner).wait()

            buffer = lax.rem(slot, BUFFERS)

            @pl.when(slot >= BUFFERS)
            def _():
                put(buffer, slot - BUFFERS).wait()

            left = jnp.where(partner <= device, partner, devices)
            right = jnp.where(partner <= device, devices, partner)
            product = lax.dot_general(
                blocks[left], blocks[right], (((0,), (0,)), ((), ())),
                preferred_element_type=jnp.float32,
            )
            tiles[buffer] = product * scale
            put(buffer, slot).start()

        return slot + mine.astype(jnp.int32)

    lax.fori_loop(0, devices, visit, jnp.int32(0))

    def drain(slot, carry):
        put(lax.rem(slot, BUFFERS), slot).wait()
        return carry

    lax.fori_loop(jnp.maximum(count - BUFFERS, 0), count, drain, 0)

    def end_clear(slot, carry):
        clear(slot).wait()
        return carry

    lax.fori_loop(count, slots, end_clear, 0)


def gathered_form(tokens, slab_lengths, tile_owner, devices, device, slots):
    slab, units = tokens.shape
    rows = slab * devices
    width = units // devices
    x = lax.all_gather(tokens, "col", axis=0, tiled=True)
    x = x.reshape(rows, devices, width).transpose(1, 0, 2)
    scale = 1.0 / jnp.sum(slab_lengths).astype(jnp.float32)
    valid = jnp.arange(slab, dtype=jnp.int32)[None, :] < slab_lengths[:, None]
    mask = jnp.broadcast_to(valid.reshape(rows, 1), (rows, width)).astype(jnp.bfloat16)
    return pl.pallas_call(
        functools.partial(gathered_kernel, devices, slots),
        out_shape=jax.ShapeDtypeStruct((slots, width, width), jnp.float32),
        in_specs=[pl.BlockSpec(memory_space=pltpu.SMEM)] * 3 + [pl.BlockSpec(memory_space=pl.ANY)] * 2,
        out_specs=pl.BlockSpec(memory_space=pl.ANY),
        scratch_shapes=[
            pltpu.VMEM((devices + 1, rows, width), jnp.bfloat16),
            pltpu.VMEM((rows, width), jnp.bfloat16),
            pltpu.VMEM((BUFFERS, width, width), jnp.float32),
            pltpu.VMEM((width, width), jnp.float32),
            pltpu.SemaphoreType.DMA((devices,)),
            pltpu.SemaphoreType.DMA,
            pltpu.SemaphoreType.DMA((BUFFERS,)),
            pltpu.SemaphoreType.DMA((slots,)),
        ],
        compiler_params=pltpu.CompilerParams(vmem_limit_bytes=50 * 1024 * 1024),
    )(tile_owner, device.reshape(1), scale.reshape(1), x, mask)


def ring_plan(devices):
    chips = devices // 2
    order = list(range(0, chips, 2)) + list(range(1, chips, 2))[::-1]
    place = {chip: at for at, chip in enumerate(order)}
    onward = []
    for device in range(devices):
        chip, core = divmod(device, 2)
        onward.append(order[(place[chip] - 1) % chips] * 2 + core)
    backward = [onward.index(device) for device in range(devices)]
    return onward, backward


GROUPS = ((0, 1, 2), (8, 9, 10), (3, 4), (11, 12), (5, 7), (13, 15), (6,), (14,))


def first_needed(devices, chip):
    return (2 * chip - devices // 2 - devices // 8 + devices) % devices


def ring_gather(tokens, device, devices):
    onward, backward = ring_plan(devices)
    sibling = [device ^ 1 for device in range(devices)]
    over = [at ^ 12 if at // 4 in (0, 3) else at ^ 2 for at in range(devices)]

    def send(value, target):
        return lax.ppermute(value, "col", list(enumerate(target)))

    def after(value, *others):
        return lax.optimization_barrier((value, *others))[0]

    chip, chips = device // 2, devices // 2
    even = chip % 2 == 0
    next_chip = jnp.where(even, jnp.where(chip == chips - 2, chips - 1, chip + 2), jnp.where(chip == 1, 0, chip - 2))
    last_chip = jnp.where(even, jnp.where(chip == 0, 1, chip - 2), jnp.where(chip == chips - 1, chips - 2, chip + 2))
    over_chip = jnp.where((chip < 2) | (chip >= chips - 2), chip ^ 6, chip ^ 1)
    chip, chips = device // 2, devices // 2
    even = chip % 2 == 0
    next_chip = jnp.where(even, jnp.where(chip == chips - 2, chips - 1, chip + 2), jnp.where(chip == 1, 0, chip - 2))
    last_chip = jnp.where(even, jnp.where(chip == 0, 1, chip - 2), jnp.where(chip == chips - 1, chips - 2, chip + 2))
    over_chip = jnp.where((chip < 2) | (chip >= chips - 2), chip ^ 6, chip ^ 1)
    came_ahead = (chip % 4 == 1) | (chip % 4 == 2)
    slab, units = tokens.shape
    needed = devices // 2 + devices // 8 + 2

    def window(value, chip):
        blocks = value.reshape(slab, devices, units // devices)
        blocks = jnp.concatenate([blocks, blocks], axis=1)
        blocks = lax.dynamic_slice_in_dim(blocks, first_needed(devices, chip), needed, axis=1)
        return blocks.reshape(slab, -1)

    ahead, back = [tokens], [tokens]
    for _ in range(2):
        ahead.append(send(ahead[-1], onward))
        back.append(send(back[-1], backward))
    half = send(window(jnp.where(came_ahead, ahead[1], back[1]), over_chip), over)
    ahead.append(send(window(ahead[2], last_chip), onward))
    back.append(send(window(back[2], next_chip), backward))
    near = jnp.concatenate((tokens, ahead[1], back[1]), axis=0)
    middle = jnp.concatenate((ahead[2], back[2]), axis=0)
    last = jnp.concatenate((ahead[3], half), axis=0)
    near_beside = send(near, sibling)
    needed = [window(after(value, ahead[2], back[2]), chip) for value in (ahead[2], back[2])]
    middle_beside = send(jnp.concatenate(needed, axis=0), sibling)
    last_beside = send(last, sibling)
    return [near, near_beside, middle, middle_beside, last, last_beside, back[3], send(back[3], sibling)]

def slab_origin(devices, device, number):
    chips = devices // 2
    number, flip = number % chips, number // chips
    hops = (number + 1) // 2 if number % 2 else -(number // 2)
    chip, core = device // 2, device % 2
    core = 1 - core if flip else core
    place = jnp.where(chip % 2 == 0, chip // 2, chips - 1 - chip // 2)
    place = (place + hops + chips) % chips
    chip = jnp.where(2 * place < chips, 2 * place, 2 * (chips - 1 - place) + 1)
    return 2 * chip + core


def ring_kernel(devices, slots, table_ref, *refs):
    groups = refs[:len(GROUPS)]
    out_ref, pair, tiles, zeros, out_sems, zero_sems = refs[len(GROUPS):]
    device = table_ref[table_ref.shape[0] - 1]
    slab, width = pair.shape[1] // devices, pair.shape[2]
    first = first_needed(devices, device // 2)

    def owned(partner):
        return table_ref[devices + tile_number(devices, device, partner)] == device

    def put(buffer, slot):
        return pltpu.make_async_copy(tiles.at[buffer], out_ref.at[slot], out_sems.at[buffer])

    def clear(slot):
        return pltpu.make_async_copy(zeros, out_ref.at[slot], zero_sems.at[slot])

    def load_block(partner, masked):
        parts = []
        for numbers, ref in zip(GROUPS, groups):
            place = partner
            if ref.shape[1] < devices * width:
                place = lax.rem(partner - first + devices, devices)
            group = ref[:, pl.ds(pl.multiple_of(place * width, 128), width)].astype(jnp.float32)
            for at, number in enumerate(numbers):
                part = group[at * slab:(at + 1) * slab]
                if masked:
                    row = lax.broadcasted_iota(jnp.int32, (slab, width), 0)
                    part = jnp.where(row < table_ref[slab_origin(devices, device, number)], part, 0.0)
                parts.append(part)
        pair[0 if masked else 1] = jnp.concatenate(parts, axis=0).astype(jnp.bfloat16)

    load_block(device, True)
    valid_count = table_ref[0]
    for at in range(1, devices):
        valid_count = valid_count + table_ref[at]
    scale = 1.0 / jnp.full((8, width), valid_count.astype(jnp.float32))

    def visit(partner, slot):
        mine = owned(partner)

        @pl.when(mine)
        def _():
            buffer = lax.rem(slot, BUFFERS)
            load_block(partner, False)

            @pl.when(slot >= BUFFERS)
            def _():
                put(buffer, slot - BUFFERS).wait()

            left = (partner <= device).astype(jnp.int32)
            for row in range(0, width, STRIP):
                rows = min(STRIP, width - row)
                strip = pl.ds(row, rows)
                product = lax.dot_general(
                    pair[left, :, row:row + rows], pair[1 - left], (((0,), (0,)), ((), ())),
                    preferred_element_type=jnp.float32,
                )
                tiles[buffer, strip, :] = product * scale[:1]
                pltpu.make_async_copy(
                    tiles.at[buffer, strip], out_ref.at[slot, strip], out_sems.at[buffer]
                ).start()

        return slot + mine.astype(jnp.int32)

    count = lax.fori_loop(0, devices, visit, jnp.int32(0))

    @pl.when(count < slots)
    def _():
        zeros[...] = jnp.zeros_like(zeros)

    def start_clear(slot, carry):
        clear(slot).start()
        return carry

    lax.fori_loop(count, slots, start_clear, 0)

    def drain(slot, carry):
        put(lax.rem(slot, BUFFERS), slot).wait()
        return carry

    lax.fori_loop(jnp.maximum(count - BUFFERS, 0), count, drain, 0)

    def end_clear(slot, carry):
        clear(slot).wait()
        return carry

    lax.fori_loop(count, slots, end_clear, 0)


def ring_form(tokens, slab_lengths, tile_owner, devices, device, slots):
    slab, units = tokens.shape
    width = units // devices
    groups = ring_gather(tokens, device, devices)
    table = jnp.concatenate([slab_lengths, tile_owner, device.reshape(1)])
    return pl.pallas_call(
        functools.partial(ring_kernel, devices, slots),
        out_shape=jax.ShapeDtypeStruct((slots, width, width), jnp.float32),
        in_specs=[pl.BlockSpec(memory_space=pltpu.SMEM)]
        + [pl.BlockSpec(memory_space=pltpu.VMEM)] * len(groups),
        out_specs=pl.BlockSpec(memory_space=pl.ANY),
        scratch_shapes=[
            pltpu.VMEM((2, slab * devices, width), jnp.bfloat16),
            pltpu.VMEM((BUFFERS, width, width), jnp.float32),
            pltpu.VMEM((width, width), jnp.float32),
            pltpu.SemaphoreType.DMA((BUFFERS,)),
            pltpu.SemaphoreType.DMA((slots,)),
        ],
        compiler_params=pltpu.CompilerParams(vmem_limit_bytes=32 * 1024 * 1024),
        cost_estimate=pl.CostEstimate(
            flops=2 * slots * slab * devices * width * width,
            bytes_accessed=4 * slots * width * width,
            transcendentals=0,
        ),
    )(table, *groups)


def per_device(tokens, slab_lengths, tile_owner):
    devices = lax.axis_size("col")
    device = lax.axis_index("col").astype(jnp.int32)
    slots = devices // 2 + devices // 8 + 1
    width = tokens.shape[1] // devices
    form = ring_form if devices == RING_DEVICES and width % 128 == 0 else gathered_form
    return form(tokens, slab_lengths, tile_owner, devices, device, slots)


def solution(mesh):
    return jax.shard_map(
        per_device,
        mesh=mesh,
        in_specs=(P(("grp", "col"), None), P("grp"), P()),
        out_specs=P(("grp", "col"), None, None),
        check_vma=False,
    )
```

```python
import functools

import jax
import jax.numpy as jnp
from jax import lax
from jax.experimental import pallas as pl
from jax.experimental.pallas import tpu as pltpu
from jax.sharding import PartitionSpec as P

BUFFERS = 4
STRIP = 128
RING_DEVICES = 16


def tile_number(devices, device, partner):
    low = jnp.minimum(device, partner)
    high = jnp.maximum(device, partner)
    return low * devices - low * (low - 1) // 2 + (high - low)


def gathered_kernel(
    devices, slots, owner_ref, device_ref, scale_ref, x_ref, mask_ref,
    out_ref, blocks, mask, tiles, zeros, in_sems, mask_sem, out_sems, zero_sems,
):
    device = device_ref[0]
    width = blocks.shape[2]

    def owned(partner):
        return owner_ref[tile_number(devices, device, partner)] == device

    def fetch(partner):
        return pltpu.make_async_copy(x_ref.at[partner], blocks.at[partner], in_sems.at[partner])

    def put(buffer, slot):
        return pltpu.make_async_copy(tiles.at[buffer], out_ref.at[slot], out_sems.at[buffer])

    def clear(slot):
        return pltpu.make_async_copy(zeros, out_ref.at[slot], zero_sems.at[slot])

    mask_copy = pltpu.make_async_copy(mask_ref, mask, mask_sem)
    mask_copy.start()
    fetch(device).start()

    def start_fetch(partner, count):
        mine = owned(partner)

        @pl.when(mine & (partner != device))
        def _():
            fetch(partner).start()

        return count + mine.astype(jnp.int32)

    count = lax.fori_loop(0, devices, start_fetch, jnp.int32(0))

    zeros[...] = jnp.zeros_like(zeros)

    def start_clear(slot, carry):
        clear(slot).start()
        return carry

    lax.fori_loop(count, slots, start_clear, 0)

    mask_copy.wait()
    fetch(device).wait()
    blocks[devices] = blocks[device] * mask[...]
    scale = scale_ref[0]

    def visit(partner, slot):
        mine = owned(partner)

        @pl.when(mine)
        def _():
            @pl.when(partner != device)
            def _():
                fetch(partner).wait()

            buffer = lax.rem(slot, BUFFERS)

            @pl.when(slot >= BUFFERS)
            def _():
                put(buffer, slot - BUFFERS).wait()

            left = jnp.where(partner <= device, partner, devices)
            right = jnp.where(partner <= device, devices, partner)
            product = lax.dot_general(
                blocks[left], blocks[right], (((0,), (0,)), ((), ())),
                preferred_element_type=jnp.float32,
            )
            tiles[buffer] = product * scale
            put(buffer, slot).start()

        return slot + mine.astype(jnp.int32)

    lax.fori_loop(0, devices, visit, jnp.int32(0))

    def drain(slot, carry):
        put(lax.rem(slot, BUFFERS), slot).wait()
        return carry

    lax.fori_loop(jnp.maximum(count - BUFFERS, 0), count, drain, 0)

    def end_clear(slot, carry):
        clear(slot).wait()
        return carry

    lax.fori_loop(count, slots, end_clear, 0)


def gathered_form(tokens, slab_lengths, tile_owner, devices, device, slots):
    slab, units = tokens.shape
    rows = slab * devices
    width = units // devices
    x = lax.all_gather(tokens, "col", axis=0, tiled=True)
    x = x.reshape(rows, devices, width).transpose(1, 0, 2)
    scale = 1.0 / jnp.sum(slab_lengths).astype(jnp.float32)
    valid = jnp.arange(slab, dtype=jnp.int32)[None, :] < slab_lengths[:, None]
    mask = jnp.broadcast_to(valid.reshape(rows, 1), (rows, width)).astype(jnp.bfloat16)
    return pl.pallas_call(
        functools.partial(gathered_kernel, devices, slots),
        out_shape=jax.ShapeDtypeStruct((slots, width, width), jnp.float32),
        in_specs=[pl.BlockSpec(memory_space=pltpu.SMEM)] * 3 + [pl.BlockSpec(memory_space=pl.ANY)] * 2,
        out_specs=pl.BlockSpec(memory_space=pl.ANY),
        scratch_shapes=[
            pltpu.VMEM((devices + 1, rows, width), jnp.bfloat16),
            pltpu.VMEM((rows, width), jnp.bfloat16),
            pltpu.VMEM((BUFFERS, width, width), jnp.float32),
            pltpu.VMEM((width, width), jnp.float32),
            pltpu.SemaphoreType.DMA((devices,)),
            pltpu.SemaphoreType.DMA,
            pltpu.SemaphoreType.DMA((BUFFERS,)),
            pltpu.SemaphoreType.DMA((slots,)),
        ],
        compiler_params=pltpu.CompilerParams(vmem_limit_bytes=50 * 1024 * 1024),
    )(tile_owner, device.reshape(1), scale.reshape(1), x, mask)


def ring_plan(devices):
    chips = devices // 2
    order = list(range(0, chips, 2)) + list(range(1, chips, 2))[::-1]
    place = {chip: at for at, chip in enumerate(order)}
    onward = []
    for device in range(devices):
        chip, core = divmod(device, 2)
        onward.append(order[(place[chip] - 1) % chips] * 2 + core)
    backward = [onward.index(device) for device in range(devices)]
    return onward, backward


GROUPS = ((0, 1, 2), (8, 9, 10), (3, 4), (11, 12), (5, 7), (13, 15), (6,), (14,))


def first_needed(devices, chip):
    return (2 * chip - devices // 2 - devices // 8 + devices) % devices


def ring_gather(tokens, device, devices):
    onward, backward = ring_plan(devices)
    sibling = [device ^ 1 for device in range(devices)]
    over = [at ^ 12 if at // 4 in (0, 3) else at ^ 2 for at in range(devices)]

    def send(value, target):
        return lax.ppermute(value, "col", list(enumerate(target)))

    def after(value, *others):
        return lax.optimization_barrier((value, *others))[0]

    chip, chips = device // 2, devices // 2
    even = chip % 2 == 0
    next_chip = jnp.where(even, jnp.where(chip == chips - 2, chips - 1, chip + 2), jnp.where(chip == 1, 0, chip - 2))
    last_chip = jnp.where(even, jnp.where(chip == 0, 1, chip - 2), jnp.where(chip == chips - 1, chips - 2, chip + 2))
    over_chip = jnp.where((chip < 2) | (chip >= chips - 2), chip ^ 6, chip ^ 1)
    chip, chips = device // 2, devices // 2
    even = chip % 2 == 0
    next_chip = jnp.where(even, jnp.where(chip == chips - 2, chips - 1, chip + 2), jnp.where(chip == 1, 0, chip - 2))
    last_chip = jnp.where(even, jnp.where(chip == 0, 1, chip - 2), jnp.where(chip == chips - 1, chips - 2, chip + 2))
    over_chip = jnp.where((chip < 2) | (chip >= chips - 2), chip ^ 6, chip ^ 1)
    came_ahead = (chip % 4 == 1) | (chip % 4 == 2)
    slab, units = tokens.shape
    needed = devices // 2 + devices // 8 + 2

    def window(value, chip):
        blocks = value.reshape(slab, devices, units // devices)
        blocks = jnp.concatenate([blocks, blocks], axis=1)
        blocks = lax.dynamic_slice_in_dim(blocks, first_needed(devices, chip), needed, axis=1)
        return blocks.reshape(slab, -1)

    ahead, back = [tokens], [tokens]
    for _ in range(2):
        ahead.append(send(ahead[-1], onward))
        back.append(send(back[-1], backward))
    half = send(window(jnp.where(came_ahead, ahead[1], back[1]), over_chip), over)
    ahead.append(send(window(ahead[2], last_chip), onward))
    back.append(send(window(back[2], next_chip), backward))
    near = jnp.concatenate((tokens, ahead[1], back[1]), axis=0)
    middle = jnp.concatenate((ahead[2], back[2]), axis=0)
    last = jnp.concatenate((ahead[3], half), axis=0)
    near_beside = send(after(near, ahead[2], back[2]), sibling)
    needed = [window(after(value, ahead[2], back[2]), chip) for value in (ahead[2], back[2])]
    middle_beside = send(jnp.concatenate(needed, axis=0), sibling)
    last_beside = send(last, sibling)
    return [near, near_beside, middle, middle_beside, last, last_beside, back[3], send(back[3], sibling)]

def slab_origin(devices, device, number):
    chips = devices // 2
    number, flip = number % chips, number // chips
    hops = (number + 1) // 2 if number % 2 else -(number // 2)
    chip, core = device // 2, device % 2
    core = 1 - core if flip else core
    place = jnp.where(chip % 2 == 0, chip // 2, chips - 1 - chip // 2)
    place = (place + hops + chips) % chips
    chip = jnp.where(2 * place < chips, 2 * place, 2 * (chips - 1 - place) + 1)
    return 2 * chip + core


def ring_kernel(devices, slots, table_ref, *refs):
    groups = refs[:len(GROUPS)]
    out_ref, pair, tiles, zeros, out_sems, zero_sems = refs[len(GROUPS):]
    device = table_ref[table_ref.shape[0] - 1]
    slab, width = pair.shape[1] // devices, pair.shape[2]
    first = first_needed(devices, device // 2)

    def owned(partner):
        return table_ref[devices + tile_number(devices, device, partner)] == device

    def put(buffer, slot):
        return pltpu.make_async_copy(tiles.at[buffer], out_ref.at[slot], out_sems.at[buffer])

    def clear(slot):
        return pltpu.make_async_copy(zeros, out_ref.at[slot], zero_sems.at[slot])

    def load_block(partner, masked):
        parts = []
        for numbers, ref in zip(GROUPS, groups):
            place = partner
            if ref.shape[1] < devices * width:
                place = lax.rem(partner - first + devices, devices)
            group = ref[:, pl.ds(pl.multiple_of(place * width, 128), width)].astype(jnp.float32)
            for at, number in enumerate(numbers):
                part = group[at * slab:(at + 1) * slab]
                if masked:
                    row = lax.broadcasted_iota(jnp.int32, (slab, width), 0)
                    part = jnp.where(row < table_ref[slab_origin(devices, device, number)], part, 0.0)
                parts.append(part)
        pair[0 if masked else 1] = jnp.concatenate(parts, axis=0).astype(jnp.bfloat16)

    load_block(device, True)
    valid_count = table_ref[0]
    for at in range(1, devices):
        valid_count = valid_count + table_ref[at]
    scale = 1.0 / jnp.full((8, width), valid_count.astype(jnp.float32))

    def visit(partner, slot):
        mine = owned(partner)

        @pl.when(mine)
        def _():
            buffer = lax.rem(slot, BUFFERS)
            load_block(partner, False)

            @pl.when(slot >= BUFFERS)
            def _():
                put(buffer, slot - BUFFERS).wait()

            left = (partner <= device).astype(jnp.int32)
            for row in range(0, width, STRIP):
                rows = min(STRIP, width - row)
                strip = pl.ds(row, rows)
                product = lax.dot_general(
                    pair[left, :, row:row + rows], pair[1 - left], (((0,), (0,)), ((), ())),
                    preferred_element_type=jnp.float32,
                )
                tiles[buffer, strip, :] = product * scale[:1]
                pltpu.make_async_copy(
                    tiles.at[buffer, strip], out_ref.at[slot, strip], out_sems.at[buffer]
                ).start()

        return slot + mine.astype(jnp.int32)

    count = lax.fori_loop(0, devices, visit, jnp.int32(0))

    @pl.when(count < slots)
    def _():
        zeros[...] = jnp.zeros_like(zeros)

    def start_clear(slot, carry):
        clear(slot).start()
        return carry

    lax.fori_loop(count, slots, start_clear, 0)

    def drain(slot, carry):
        put(lax.rem(slot, BUFFERS), slot).wait()
        return carry

    lax.fori_loop(jnp.maximum(count - BUFFERS, 0), count, drain, 0)

    def end_clear(slot, carry):
        clear(slot).wait()
        return carry

    lax.fori_loop(count, slots, end_clear, 0)


def ring_form(tokens, slab_lengths, tile_owner, devices, device, slots):
    slab, units = tokens.shape
    width = units // devices
    groups = ring_gather(tokens, device, devices)
    table = jnp.concatenate([slab_lengths, tile_owner, device.reshape(1)])
    return pl.pallas_call(
        functools.partial(ring_kernel, devices, slots),
        out_shape=jax.ShapeDtypeStruct((slots, width, width), jnp.float32),
        in_specs=[pl.BlockSpec(memory_space=pltpu.SMEM)]
        + [pl.BlockSpec(memory_space=pltpu.VMEM)] * len(groups),
        out_specs=pl.BlockSpec(memory_space=pl.ANY),
        scratch_shapes=[
            pltpu.VMEM((2, slab * devices, width), jnp.bfloat16),
            pltpu.VMEM((BUFFERS, width, width), jnp.float32),
            pltpu.VMEM((width, width), jnp.float32),
            pltpu.SemaphoreType.DMA((BUFFERS,)),
            pltpu.SemaphoreType.DMA((slots,)),
        ],
        compiler_params=pltpu.CompilerParams(vmem_limit_bytes=32 * 1024 * 1024),
        cost_estimate=pl.CostEstimate(
            flops=2 * slots * slab * devices * width * width,
            bytes_accessed=4 * slots * width * width,
            transcendentals=0,
        ),
    )(table, *groups)


def per_device(tokens, slab_lengths, tile_owner):
    devices = lax.axis_size("col")
    device = lax.axis_index("col").astype(jnp.int32)
    slots = devices // 2 + devices // 8 + 1
    width = tokens.shape[1] // devices
    form = ring_form if devices == RING_DEVICES and width % 128 == 0 else gathered_form
    return form(tokens, slab_lengths, tile_owner, devices, device, slots)


def solution(mesh):
    return jax.shard_map(
        per_device,
        mesh=mesh,
        in_specs=(P(("grp", "col"), None), P("grp"), P()),
        out_specs=P(("grp", "col"), None, None),
        check_vma=False,
    )
```

```python
import functools

import jax
import jax.numpy as jnp
from jax import lax
from jax.experimental import pallas as pl
from jax.experimental.pallas import tpu as pltpu
from jax.sharding import PartitionSpec as P

BUFFERS = 4
STRIP = 128
RING_DEVICES = 16


def tile_number(devices, device, partner):
    low = jnp.minimum(device, partner)
    high = jnp.maximum(device, partner)
    return low * devices - low * (low - 1) // 2 + (high - low)


def gathered_kernel(
    devices, slots, owner_ref, device_ref, scale_ref, x_ref, mask_ref,
    out_ref, blocks, mask, tiles, zeros, in_sems, mask_sem, out_sems, zero_sems,
):
    device = device_ref[0]
    width = blocks.shape[2]

    def owned(partner):
        return owner_ref[tile_number(devices, device, partner)] == device

    def fetch(partner):
        return pltpu.make_async_copy(x_ref.at[partner], blocks.at[partner], in_sems.at[partner])

    def put(buffer, slot):
        return pltpu.make_async_copy(tiles.at[buffer], out_ref.at[slot], out_sems.at[buffer])

    def clear(slot):
        return pltpu.make_async_copy(zeros, out_ref.at[slot], zero_sems.at[slot])

    mask_copy = pltpu.make_async_copy(mask_ref, mask, mask_sem)
    mask_copy.start()
    fetch(device).start()

    def start_fetch(partner, count):
        mine = owned(partner)

        @pl.when(mine & (partner != device))
        def _():
            fetch(partner).start()

        return count + mine.astype(jnp.int32)

    count = lax.fori_loop(0, devices, start_fetch, jnp.int32(0))

    zeros[...] = jnp.zeros_like(zeros)

    def start_clear(slot, carry):
        clear(slot).start()
        return carry

    lax.fori_loop(count, slots, start_clear, 0)

    mask_copy.wait()
    fetch(device).wait()
    blocks[devices] = blocks[device] * mask[...]
    scale = scale_ref[0]

    def visit(partner, slot):
        mine = owned(partner)

        @pl.when(mine)
        def _():
            @pl.when(partner != device)
            def _():
                fetch(partner).wait()

            buffer = lax.rem(slot, BUFFERS)

            @pl.when(slot >= BUFFERS)
            def _():
                put(buffer, slot - BUFFERS).wait()

            left = jnp.where(partner <= device, partner, devices)
            right = jnp.where(partner <= device, devices, partner)
            product = lax.dot_general(
                blocks[left], blocks[right], (((0,), (0,)), ((), ())),
                preferred_element_type=jnp.float32,
            )
            tiles[buffer] = product * scale
            put(buffer, slot).start()

        return slot + mine.astype(jnp.int32)

    lax.fori_loop(0, devices, visit, jnp.int32(0))

    def drain(slot, carry):
        put(lax.rem(slot, BUFFERS), slot).wait()
        return carry

    lax.fori_loop(jnp.maximum(count - BUFFERS, 0), count, drain, 0)

    def end_clear(slot, carry):
        clear(slot).wait()
        return carry

    lax.fori_loop(count, slots, end_clear, 0)


def gathered_form(tokens, slab_lengths, tile_owner, devices, device, slots):
    slab, units = tokens.shape
    rows = slab * devices
    width = units // devices
    x = lax.all_gather(tokens, "col", axis=0, tiled=True)
    x = x.reshape(rows, devices, width).transpose(1, 0, 2)
    scale = 1.0 / jnp.sum(slab_lengths).astype(jnp.float32)
    valid = jnp.arange(slab, dtype=jnp.int32)[None, :] < slab_lengths[:, None]
    mask = jnp.broadcast_to(valid.reshape(rows, 1), (rows, width)).astype(jnp.bfloat16)
    return pl.pallas_call(
        functools.partial(gathered_kernel, devices, slots),
        out_shape=jax.ShapeDtypeStruct((slots, width, width), jnp.float32),
        in_specs=[pl.BlockSpec(memory_space=pltpu.SMEM)] * 3 + [pl.BlockSpec(memory_space=pl.ANY)] * 2,
        out_specs=pl.BlockSpec(memory_space=pl.ANY),
        scratch_shapes=[
            pltpu.VMEM((devices + 1, rows, width), jnp.bfloat16),
            pltpu.VMEM((rows, width), jnp.bfloat16),
            pltpu.VMEM((BUFFERS, width, width), jnp.float32),
            pltpu.VMEM((width, width), jnp.float32),
            pltpu.SemaphoreType.DMA((devices,)),
            pltpu.SemaphoreType.DMA,
            pltpu.SemaphoreType.DMA((BUFFERS,)),
            pltpu.SemaphoreType.DMA((slots,)),
        ],
        compiler_params=pltpu.CompilerParams(vmem_limit_bytes=50 * 1024 * 1024),
    )(tile_owner, device.reshape(1), scale.reshape(1), x, mask)


def ring_plan(devices):
    chips = devices // 2
    order = list(range(0, chips, 2)) + list(range(1, chips, 2))[::-1]
    place = {chip: at for at, chip in enumerate(order)}
    onward = []
    for device in range(devices):
        chip, core = divmod(device, 2)
        onward.append(order[(place[chip] - 1) % chips] * 2 + core)
    backward = [onward.index(device) for device in range(devices)]
    return onward, backward


GROUPS = ((0, 1, 2), (8, 9, 10), (3, 4), (11, 12), (5, 7), (13, 15), (6,), (14,))


def first_needed(devices, chip):
    return (2 * chip - devices // 2 - devices // 8 + devices) % devices


def ring_gather(tokens, device, devices):
    onward, backward = ring_plan(devices)
    sibling = [device ^ 1 for device in range(devices)]
    over = [at ^ 12 if at // 4 in (0, 3) else at ^ 2 for at in range(devices)]

    def send(value, target):
        return lax.ppermute(value, "col", list(enumerate(target)))

    def after(value, *others):
        return lax.optimization_barrier((value, *others))[0]

    chip, chips = device // 2, devices // 2
    even = chip % 2 == 0
    next_chip = jnp.where(even, jnp.where(chip == chips - 2, chips - 1, chip + 2), jnp.where(chip == 1, 0, chip - 2))
    last_chip = jnp.where(even, jnp.where(chip == 0, 1, chip - 2), jnp.where(chip == chips - 1, chips - 2, chip + 2))
    over_chip = jnp.where((chip < 2) | (chip >= chips - 2), chip ^ 6, chip ^ 1)
    chip, chips = device // 2, devices // 2
    even = chip % 2 == 0
    next_chip = jnp.where(even, jnp.where(chip == chips - 2, chips - 1, chip + 2), jnp.where(chip == 1, 0, chip - 2))
    last_chip = jnp.where(even, jnp.where(chip == 0, 1, chip - 2), jnp.where(chip == chips - 1, chips - 2, chip + 2))
    over_chip = jnp.where((chip < 2) | (chip >= chips - 2), chip ^ 6, chip ^ 1)
    came_ahead = (chip % 4 == 1) | (chip % 4 == 2)
    slab, units = tokens.shape
    needed = devices // 2 + devices // 8 + 2

    def window(value, chip):
        blocks = value.reshape(slab, devices, units // devices)
        blocks = jnp.concatenate([blocks, blocks], axis=1)
        blocks = lax.dynamic_slice_in_dim(blocks, first_needed(devices, chip), needed, axis=1)
        return blocks.reshape(slab, -1)

    ahead, back = [tokens], [tokens]
    for _ in range(2):
        ahead.append(send(ahead[-1], onward))
        back.append(send(back[-1], backward))
    half = send(window(jnp.where(came_ahead, ahead[1], back[1]), over_chip), over)
    ahead.append(send(window(ahead[2], last_chip), onward))
    back.append(send(window(back[2], next_chip), backward))
    near = jnp.concatenate((tokens, ahead[1], back[1]), axis=0)
    middle = jnp.concatenate((ahead[2], back[2]), axis=0)
    last = jnp.concatenate((ahead[3], half), axis=0)
    near_rows = after(near, ahead[2], back[2])
    near_cut = [window(near_rows[at:at + slab], chip) for at in range(0, 3 * slab, slab)]
    near_beside = send(jnp.concatenate(near_cut, axis=0), sibling)
    middle_cut = [window(after(value, ahead[2], back[2]), chip) for value in (ahead[2], back[2])]
    middle_beside = send(jnp.concatenate(middle_cut, axis=0), sibling)
    last_beside = send(last, sibling)
    return [near, near_beside, middle, middle_beside, last, last_beside, back[3], send(back[3], sibling)]

def slab_origin(devices, device, number):
    chips = devices // 2
    number, flip = number % chips, number // chips
    hops = (number + 1) // 2 if number % 2 else -(number // 2)
    chip, core = device // 2, device % 2
    core = 1 - core if flip else core
    place = jnp.where(chip % 2 == 0, chip // 2, chips - 1 - chip // 2)
    place = (place + hops + chips) % chips
    chip = jnp.where(2 * place < chips, 2 * place, 2 * (chips - 1 - place) + 1)
    return 2 * chip + core


def ring_kernel(devices, slots, table_ref, *refs):
    groups = refs[:len(GROUPS)]
    out_ref, pair, tiles, zeros, out_sems, zero_sems = refs[len(GROUPS):]
    device = table_ref[table_ref.shape[0] - 1]
    slab, width = pair.shape[1] // devices, pair.shape[2]
    first = first_needed(devices, device // 2)

    def owned(partner):
        return table_ref[devices + tile_number(devices, device, partner)] == device

    def put(buffer, slot):
        return pltpu.make_async_copy(tiles.at[buffer], out_ref.at[slot], out_sems.at[buffer])

    def clear(slot):
        return pltpu.make_async_copy(zeros, out_ref.at[slot], zero_sems.at[slot])

    def load_block(partner, masked):
        parts = []
        for numbers, ref in zip(GROUPS, groups):
            place = partner
            if ref.shape[1] < devices * width:
                place = lax.rem(partner - first + devices, devices)
            group = ref[:, pl.ds(pl.multiple_of(place * width, 128), width)].astype(jnp.float32)
            for at, number in enumerate(numbers):
                part = group[at * slab:(at + 1) * slab]
                if masked:
                    row = lax.broadcasted_iota(jnp.int32, (slab, width), 0)
                    part = jnp.where(row < table_ref[slab_origin(devices, device, number)], part, 0.0)
                parts.append(part)
        pair[0 if masked else 1] = jnp.concatenate(parts, axis=0).astype(jnp.bfloat16)

    load_block(device, True)
    valid_count = table_ref[0]
    for at in range(1, devices):
        valid_count = valid_count + table_ref[at]
    scale = 1.0 / jnp.full((8, width), valid_count.astype(jnp.float32))

    def visit(partner, slot):
        mine = owned(partner)

        @pl.when(mine)
        def _():
            buffer = lax.rem(slot, BUFFERS)
            load_block(partner, False)

            @pl.when(slot >= BUFFERS)
            def _():
                put(buffer, slot - BUFFERS).wait()

            left = (partner <= device).astype(jnp.int32)
            for row in range(0, width, STRIP):
                rows = min(STRIP, width - row)
                strip = pl.ds(row, rows)
                product = lax.dot_general(
                    pair[left, :, row:row + rows], pair[1 - left], (((0,), (0,)), ((), ())),
                    preferred_element_type=jnp.float32,
                )
                tiles[buffer, strip, :] = product * scale[:1]
                pltpu.make_async_copy(
                    tiles.at[buffer, strip], out_ref.at[slot, strip], out_sems.at[buffer]
                ).start()

        return slot + mine.astype(jnp.int32)

    count = lax.fori_loop(0, devices, visit, jnp.int32(0))

    @pl.when(count < slots)
    def _():
        zeros[...] = jnp.zeros_like(zeros)

    def start_clear(slot, carry):
        clear(slot).start()
        return carry

    lax.fori_loop(count, slots, start_clear, 0)

    def drain(slot, carry):
        put(lax.rem(slot, BUFFERS), slot).wait()
        return carry

    lax.fori_loop(jnp.maximum(count - BUFFERS, 0), count, drain, 0)

    def end_clear(slot, carry):
        clear(slot).wait()
        return carry

    lax.fori_loop(count, slots, end_clear, 0)


def ring_form(tokens, slab_lengths, tile_owner, devices, device, slots):
    slab, units = tokens.shape
    width = units // devices
    groups = ring_gather(tokens, device, devices)
    table = jnp.concatenate([slab_lengths, tile_owner, device.reshape(1)])
    return pl.pallas_call(
        functools.partial(ring_kernel, devices, slots),
        out_shape=jax.ShapeDtypeStruct((slots, width, width), jnp.float32),
        in_specs=[pl.BlockSpec(memory_space=pltpu.SMEM)]
        + [pl.BlockSpec(memory_space=pltpu.VMEM)] * len(groups),
        out_specs=pl.BlockSpec(memory_space=pl.ANY),
        scratch_shapes=[
            pltpu.VMEM((2, slab * devices, width), jnp.bfloat16),
            pltpu.VMEM((BUFFERS, width, width), jnp.float32),
            pltpu.VMEM((width, width), jnp.float32),
            pltpu.SemaphoreType.DMA((BUFFERS,)),
            pltpu.SemaphoreType.DMA((slots,)),
        ],
        compiler_params=pltpu.CompilerParams(vmem_limit_bytes=32 * 1024 * 1024),
        cost_estimate=pl.CostEstimate(
            flops=2 * slots * slab * devices * width * width,
            bytes_accessed=4 * slots * width * width,
            transcendentals=0,
        ),
    )(table, *groups)


def per_device(tokens, slab_lengths, tile_owner):
    devices = lax.axis_size("col")
    device = lax.axis_index("col").astype(jnp.int32)
    slots = devices // 2 + devices // 8 + 1
    width = tokens.shape[1] // devices
    form = ring_form if devices == RING_DEVICES and width % 128 == 0 else gathered_form
    return form(tokens, slab_lengths, tile_owner, devices, device, slots)


def solution(mesh):
    return jax.shard_map(
        per_device,
        mesh=mesh,
        in_specs=(P(("grp", "col"), None), P("grp"), P()),
        out_specs=P(("grp", "col"), None, None),
        check_vma=False,
    )
```

```python
import functools

import jax
import jax.numpy as jnp
from jax import lax
from jax.experimental import pallas as pl
from jax.experimental.pallas import tpu as pltpu
from jax.sharding import PartitionSpec as P

BUFFERS = 4
STRIP = 128
RING_DEVICES = 16


def tile_number(devices, device, partner):
    low = jnp.minimum(device, partner)
    high = jnp.maximum(device, partner)
    return low * devices - low * (low - 1) // 2 + (high - low)


def gathered_kernel(
    devices, slots, owner_ref, device_ref, scale_ref, x_ref, mask_ref,
    out_ref, blocks, mask, tiles, zeros, in_sems, mask_sem, out_sems, zero_sems,
):
    device = device_ref[0]
    width = blocks.shape[2]

    def owned(partner):
        return owner_ref[tile_number(devices, device, partner)] == device

    def fetch(partner):
        return pltpu.make_async_copy(x_ref.at[partner], blocks.at[partner], in_sems.at[partner])

    def put(buffer, slot):
        return pltpu.make_async_copy(tiles.at[buffer], out_ref.at[slot], out_sems.at[buffer])

    def clear(slot):
        return pltpu.make_async_copy(zeros, out_ref.at[slot], zero_sems.at[slot])

    mask_copy = pltpu.make_async_copy(mask_ref, mask, mask_sem)
    mask_copy.start()
    fetch(device).start()

    def start_fetch(partner, count):
        mine = owned(partner)

        @pl.when(mine & (partner != device))
        def _():
            fetch(partner).start()

        return count + mine.astype(jnp.int32)

    count = lax.fori_loop(0, devices, start_fetch, jnp.int32(0))

    zeros[...] = jnp.zeros_like(zeros)

    def start_clear(slot, carry):
        clear(slot).start()
        return carry

    lax.fori_loop(count, slots, start_clear, 0)

    mask_copy.wait()
    fetch(device).wait()
    blocks[devices] = blocks[device] * mask[...]
    scale = scale_ref[0]

    def visit(partner, slot):
        mine = owned(partner)

        @pl.when(mine)
        def _():
            @pl.when(partner != device)
            def _():
                fetch(partner).wait()

            buffer = lax.rem(slot, BUFFERS)

            @pl.when(slot >= BUFFERS)
            def _():
                put(buffer, slot - BUFFERS).wait()

            left = jnp.where(partner <= device, partner, devices)
            right = jnp.where(partner <= device, devices, partner)
            product = lax.dot_general(
                blocks[left], blocks[right], (((0,), (0,)), ((), ())),
                preferred_element_type=jnp.float32,
            )
            tiles[buffer] = product * scale
            put(buffer, slot).start()

        return slot + mine.astype(jnp.int32)

    lax.fori_loop(0, devices, visit, jnp.int32(0))

    def drain(slot, carry):
        put(lax.rem(slot, BUFFERS), slot).wait()
        return carry

    lax.fori_loop(jnp.maximum(count - BUFFERS, 0), count, drain, 0)

    def end_clear(slot, carry):
        clear(slot).wait()
        return carry

    lax.fori_loop(count, slots, end_clear, 0)


def gathered_form(tokens, slab_lengths, tile_owner, devices, device, slots):
    slab, units = tokens.shape
    rows = slab * devices
    width = units // devices
    x = lax.all_gather(tokens, "col", axis=0, tiled=True)
    x = x.reshape(rows, devices, width).transpose(1, 0, 2)
    scale = 1.0 / jnp.sum(slab_lengths).astype(jnp.float32)
    valid = jnp.arange(slab, dtype=jnp.int32)[None, :] < slab_lengths[:, None]
    mask = jnp.broadcast_to(valid.reshape(rows, 1), (rows, width)).astype(jnp.bfloat16)
    return pl.pallas_call(
        functools.partial(gathered_kernel, devices, slots),
        out_shape=jax.ShapeDtypeStruct((slots, width, width), jnp.float32),
        in_specs=[pl.BlockSpec(memory_space=pltpu.SMEM)] * 3 + [pl.BlockSpec(memory_space=pl.ANY)] * 2,
        out_specs=pl.BlockSpec(memory_space=pl.ANY),
        scratch_shapes=[
            pltpu.VMEM((devices + 1, rows, width), jnp.bfloat16),
            pltpu.VMEM((rows, width), jnp.bfloat16),
            pltpu.VMEM((BUFFERS, width, width), jnp.float32),
            pltpu.VMEM((width, width), jnp.float32),
            pltpu.SemaphoreType.DMA((devices,)),
            pltpu.SemaphoreType.DMA,
            pltpu.SemaphoreType.DMA((BUFFERS,)),
            pltpu.SemaphoreType.DMA((slots,)),
        ],
        compiler_params=pltpu.CompilerParams(vmem_limit_bytes=50 * 1024 * 1024),
    )(tile_owner, device.reshape(1), scale.reshape(1), x, mask)


def ring_plan(devices):
    chips = devices // 2
    order = list(range(0, chips, 2)) + list(range(1, chips, 2))[::-1]
    place = {chip: at for at, chip in enumerate(order)}
    onward = []
    for device in range(devices):
        chip, core = divmod(device, 2)
        onward.append(order[(place[chip] - 1) % chips] * 2 + core)
    backward = [onward.index(device) for device in range(devices)]
    return onward, backward


GROUPS = ((0, 1, 2), (3, 4), (8, 9, 10, 11, 12), (5, 7), (13, 15), (6,), (14,))


def first_needed(devices, chip):
    return (2 * chip - devices // 2 - devices // 8 + devices) % devices


def ring_gather(tokens, device, devices):
    onward, backward = ring_plan(devices)
    sibling = [device ^ 1 for device in range(devices)]
    over = [at ^ 12 if at // 4 in (0, 3) else at ^ 2 for at in range(devices)]

    def send(value, target):
        return lax.ppermute(value, "col", list(enumerate(target)))

    def after(value, *others):
        return lax.optimization_barrier((value, *others))[0]

    chip, chips = device // 2, devices // 2
    even = chip % 2 == 0
    next_chip = jnp.where(even, jnp.where(chip == chips - 2, chips - 1, chip + 2), jnp.where(chip == 1, 0, chip - 2))
    last_chip = jnp.where(even, jnp.where(chip == 0, 1, chip - 2), jnp.where(chip == chips - 1, chips - 2, chip + 2))
    over_chip = jnp.where((chip < 2) | (chip >= chips - 2), chip ^ 6, chip ^ 1)
    chip, chips = device // 2, devices // 2
    even = chip % 2 == 0
    next_chip = jnp.where(even, jnp.where(chip == chips - 2, chips - 1, chip + 2), jnp.where(chip == 1, 0, chip - 2))
    last_chip = jnp.where(even, jnp.where(chip == 0, 1, chip - 2), jnp.where(chip == chips - 1, chips - 2, chip + 2))
    over_chip = jnp.where((chip < 2) | (chip >= chips - 2), chip ^ 6, chip ^ 1)
    came_ahead = (chip % 4 == 1) | (chip % 4 == 2)
    slab, units = tokens.shape
    needed = devices // 2 + devices // 8 + 2

    def window(value, chip):
        blocks = value.reshape(slab, devices, units // devices)
        blocks = jnp.concatenate([blocks, blocks], axis=1)
        blocks = lax.dynamic_slice_in_dim(blocks, first_needed(devices, chip), needed, axis=1)
        return blocks.reshape(slab, -1)

    ahead, back = [tokens], [tokens]
    for _ in range(2):
        ahead.append(send(ahead[-1], onward))
        back.append(send(back[-1], backward))
    half = send(window(jnp.where(came_ahead, ahead[1], back[1]), over_chip), over)
    ahead.append(send(window(ahead[2], last_chip), onward))
    back.append(send(window(back[2], next_chip), backward))
    near = jnp.concatenate((tokens, ahead[1], back[1]), axis=0)
    middle = jnp.concatenate((ahead[2], back[2]), axis=0)
    last = jnp.concatenate((ahead[3], half), axis=0)
    rows = [after(near, ahead[2], back[2])[at:at + slab] for at in range(0, 3 * slab, slab)]
    rows += [after(value, ahead[2], back[2]) for value in (ahead[2], back[2])]
    early_beside = send(jnp.concatenate([window(value, chip) for value in rows], axis=0), sibling)
    last_beside = send(last, sibling)
    return [near, middle, early_beside, last, last_beside, back[3], send(back[3], sibling)]

def slab_origin(devices, device, number):
    chips = devices // 2
    number, flip = number % chips, number // chips
    hops = (number + 1) // 2 if number % 2 else -(number // 2)
    chip, core = device // 2, device % 2
    core = 1 - core if flip else core
    place = jnp.where(chip % 2 == 0, chip // 2, chips - 1 - chip // 2)
    place = (place + hops + chips) % chips
    chip = jnp.where(2 * place < chips, 2 * place, 2 * (chips - 1 - place) + 1)
    return 2 * chip + core


def ring_kernel(devices, slots, table_ref, *refs):
    groups = refs[:len(GROUPS)]
    out_ref, pair, tiles, zeros, out_sems, zero_sems = refs[len(GROUPS):]
    device = table_ref[table_ref.shape[0] - 1]
    slab, width = pair.shape[1] // devices, pair.shape[2]
    first = first_needed(devices, device // 2)

    def owned(partner):
        return table_ref[devices + tile_number(devices, device, partner)] == device

    def put(buffer, slot):
        return pltpu.make_async_copy(tiles.at[buffer], out_ref.at[slot], out_sems.at[buffer])

    def clear(slot):
        return pltpu.make_async_copy(zeros, out_ref.at[slot], zero_sems.at[slot])

    def load_block(partner, masked):
        parts = []
        for numbers, ref in zip(GROUPS, groups):
            place = partner
            if ref.shape[1] < devices * width:
                place = lax.rem(partner - first + devices, devices)
            group = ref[:, pl.ds(pl.multiple_of(place * width, 128), width)].astype(jnp.float32)
            for at, number in enumerate(numbers):
                part = group[at * slab:(at + 1) * slab]
                if masked:
                    row = lax.broadcasted_iota(jnp.int32, (slab, width), 0)
                    part = jnp.where(row < table_ref[slab_origin(devices, device, number)], part, 0.0)
                parts.append(part)
        pair[0 if masked else 1] = jnp.concatenate(parts, axis=0).astype(jnp.bfloat16)

    load_block(device, True)
    valid_count = table_ref[0]
    for at in range(1, devices):
        valid_count = valid_count + table_ref[at]
    scale = 1.0 / jnp.full((8, width), valid_count.astype(jnp.float32))

    def visit(partner, slot):
        mine = owned(partner)

        @pl.when(mine)
        def _():
            buffer = lax.rem(slot, BUFFERS)
            load_block(partner, False)

            @pl.when(slot >= BUFFERS)
            def _():
                put(buffer, slot - BUFFERS).wait()

            left = (partner <= device).astype(jnp.int32)
            for row in range(0, width, STRIP):
                rows = min(STRIP, width - row)
                strip = pl.ds(row, rows)
                product = lax.dot_general(
                    pair[left, :, row:row + rows], pair[1 - left], (((0,), (0,)), ((), ())),
                    preferred_element_type=jnp.float32,
                )
                tiles[buffer, strip, :] = product * scale[:1]
                pltpu.make_async_copy(
                    tiles.at[buffer, strip], out_ref.at[slot, strip], out_sems.at[buffer]
                ).start()

        return slot + mine.astype(jnp.int32)

    count = lax.fori_loop(0, devices, visit, jnp.int32(0))

    @pl.when(count < slots)
    def _():
        zeros[...] = jnp.zeros_like(zeros)

    def start_clear(slot, carry):
        clear(slot).start()
        return carry

    lax.fori_loop(count, slots, start_clear, 0)

    def drain(slot, carry):
        put(lax.rem(slot, BUFFERS), slot).wait()
        return carry

    lax.fori_loop(jnp.maximum(count - BUFFERS, 0), count, drain, 0)

    def end_clear(slot, carry):
        clear(slot).wait()
        return carry

    lax.fori_loop(count, slots, end_clear, 0)


def ring_form(tokens, slab_lengths, tile_owner, devices, device, slots):
    slab, units = tokens.shape
    width = units // devices
    groups = ring_gather(tokens, device, devices)
    table = jnp.concatenate([slab_lengths, tile_owner, device.reshape(1)])
    return pl.pallas_call(
        functools.partial(ring_kernel, devices, slots),
        out_shape=jax.ShapeDtypeStruct((slots, width, width), jnp.float32),
        in_specs=[pl.BlockSpec(memory_space=pltpu.SMEM)]
        + [pl.BlockSpec(memory_space=pltpu.VMEM)] * len(groups),
        out_specs=pl.BlockSpec(memory_space=pl.ANY),
        scratch_shapes=[
            pltpu.VMEM((2, slab * devices, width), jnp.bfloat16),
            pltpu.VMEM((BUFFERS, width, width), jnp.float32),
            pltpu.VMEM((width, width), jnp.float32),
            pltpu.SemaphoreType.DMA((BUFFERS,)),
            pltpu.SemaphoreType.DMA((slots,)),
        ],
        compiler_params=pltpu.CompilerParams(vmem_limit_bytes=32 * 1024 * 1024),
        cost_estimate=pl.CostEstimate(
            flops=2 * slots * slab * devices * width * width,
            bytes_accessed=4 * slots * width * width,
            transcendentals=0,
        ),
    )(table, *groups)


def per_device(tokens, slab_lengths, tile_owner):
    devices = lax.axis_size("col")
    device = lax.axis_index("col").astype(jnp.int32)
    slots = devices // 2 + devices // 8 + 1
    width = tokens.shape[1] // devices
    form = ring_form if devices == RING_DEVICES and width % 128 == 0 else gathered_form
    return form(tokens, slab_lengths, tile_owner, devices, device, slots)


def solution(mesh):
    return jax.shard_map(
        per_device,
        mesh=mesh,
        in_specs=(P(("grp", "col"), None), P("grp"), P()),
        out_specs=P(("grp", "col"), None, None),
        check_vma=False,
    )
```

```python
import functools

import jax
import jax.numpy as jnp
from jax import lax
from jax.experimental import pallas as pl
from jax.experimental.pallas import tpu as pltpu
from jax.sharding import PartitionSpec as P

BUFFERS = 6
STRIP = 128
RING_DEVICES = 16


def tile_number(devices, device, partner):
    low = jnp.minimum(device, partner)
    high = jnp.maximum(device, partner)
    return low * devices - low * (low - 1) // 2 + (high - low)


def gathered_kernel(
    devices, slots, owner_ref, device_ref, scale_ref, x_ref, mask_ref,
    out_ref, blocks, mask, tiles, zeros, in_sems, mask_sem, out_sems, zero_sems,
):
    device = device_ref[0]
    width = blocks.shape[2]

    def owned(partner):
        return owner_ref[tile_number(devices, device, partner)] == device

    def fetch(partner):
        return pltpu.make_async_copy(x_ref.at[partner], blocks.at[partner], in_sems.at[partner])

    def put(buffer, slot):
        return pltpu.make_async_copy(tiles.at[buffer], out_ref.at[slot], out_sems.at[buffer])

    def clear(slot):
        return pltpu.make_async_copy(zeros, out_ref.at[slot], zero_sems.at[slot])

    mask_copy = pltpu.make_async_copy(mask_ref, mask, mask_sem)
    mask_copy.start()
    fetch(device).start()

    def start_fetch(partner, count):
        mine = owned(partner)

        @pl.when(mine & (partner != device))
        def _():
            fetch(partner).start()

        return count + mine.astype(jnp.int32)

    count = lax.fori_loop(0, devices, start_fetch, jnp.int32(0))

    zeros[...] = jnp.zeros_like(zeros)

    def start_clear(slot, carry):
        clear(slot).start()
        return carry

    lax.fori_loop(count, slots, start_clear, 0)

    mask_copy.wait()
    fetch(device).wait()
    blocks[devices] = blocks[device] * mask[...]
    scale = scale_ref[0]

    def visit(partner, slot):
        mine = owned(partner)

        @pl.when(mine)
        def _():
            @pl.when(partner != device)
            def _():
                fetch(partner).wait()

            buffer = lax.rem(slot, BUFFERS)

            @pl.when(slot >= BUFFERS)
            def _():
                put(buffer, slot - BUFFERS).wait()

            left = jnp.where(partner <= device, partner, devices)
            right = jnp.where(partner <= device, devices, partner)
            product = lax.dot_general(
                blocks[left], blocks[right], (((0,), (0,)), ((), ())),
                preferred_element_type=jnp.float32,
            )
            tiles[buffer] = product * scale
            put(buffer, slot).start()

        return slot + mine.astype(jnp.int32)

    lax.fori_loop(0, devices, visit, jnp.int32(0))

    def drain(slot, carry):
        put(lax.rem(slot, BUFFERS), slot).wait()
        return carry

    lax.fori_loop(jnp.maximum(count - BUFFERS, 0), count, drain, 0)

    def end_clear(slot, carry):
        clear(slot).wait()
        return carry

    lax.fori_loop(count, slots, end_clear, 0)


def gathered_form(tokens, slab_lengths, tile_owner, devices, device, slots):
    slab, units = tokens.shape
    rows = slab * devices
    width = units // devices
    x = lax.all_gather(tokens, "col", axis=0, tiled=True)
    x = x.reshape(rows, devices, width).transpose(1, 0, 2)
    scale = 1.0 / jnp.sum(slab_lengths).astype(jnp.float32)
    valid = jnp.arange(slab, dtype=jnp.int32)[None, :] < slab_lengths[:, None]
    mask = jnp.broadcast_to(valid.reshape(rows, 1), (rows, width)).astype(jnp.bfloat16)
    return pl.pallas_call(
        functools.partial(gathered_kernel, devices, slots),
        out_shape=jax.ShapeDtypeStruct((slots, width, width), jnp.float32),
        in_specs=[pl.BlockSpec(memory_space=pltpu.SMEM)] * 3 + [pl.BlockSpec(memory_space=pl.ANY)] * 2,
        out_specs=pl.BlockSpec(memory_space=pl.ANY),
        scratch_shapes=[
            pltpu.VMEM((devices + 1, rows, width), jnp.bfloat16),
            pltpu.VMEM((rows, width), jnp.bfloat16),
            pltpu.VMEM((BUFFERS, width, width), jnp.float32),
            pltpu.VMEM((width, width), jnp.float32),
            pltpu.SemaphoreType.DMA((devices,)),
            pltpu.SemaphoreType.DMA,
            pltpu.SemaphoreType.DMA((BUFFERS,)),
            pltpu.SemaphoreType.DMA((slots,)),
        ],
        compiler_params=pltpu.CompilerParams(vmem_limit_bytes=50 * 1024 * 1024),
    )(tile_owner, device.reshape(1), scale.reshape(1), x, mask)


def ring_plan(devices):
    chips = devices // 2
    order = list(range(0, chips, 2)) + list(range(1, chips, 2))[::-1]
    place = {chip: at for at, chip in enumerate(order)}
    onward = []
    for device in range(devices):
        chip, core = divmod(device, 2)
        onward.append(order[(place[chip] - 1) % chips] * 2 + core)
    backward = [onward.index(device) for device in range(devices)]
    return onward, backward


GROUPS = ((0, 1, 2), (8, 9, 10), (3, 4), (11, 12), (5, 7), (13, 15), (6,), (14,))


def first_needed(devices, chip):
    return (2 * chip - devices // 2 - devices // 8 + devices) % devices


def ring_gather(tokens, device, devices):
    onward, backward = ring_plan(devices)
    sibling = [device ^ 1 for device in range(devices)]
    over = [at ^ 12 if at // 4 in (0, 3) else at ^ 2 for at in range(devices)]

    def send(value, target):
        return lax.ppermute(value, "col", list(enumerate(target)))

    def after(value, *others):
        return lax.optimization_barrier((value, *others))[0]

    chip, chips = device // 2, devices // 2
    even = chip % 2 == 0
    next_chip = jnp.where(even, jnp.where(chip == chips - 2, chips - 1, chip + 2), jnp.where(chip == 1, 0, chip - 2))
    last_chip = jnp.where(even, jnp.where(chip == 0, 1, chip - 2), jnp.where(chip == chips - 1, chips - 2, chip + 2))
    over_chip = jnp.where((chip < 2) | (chip >= chips - 2), chip ^ 6, chip ^ 1)
    chip, chips = device // 2, devices // 2
    even = chip % 2 == 0
    next_chip = jnp.where(even, jnp.where(chip == chips - 2, chips - 1, chip + 2), jnp.where(chip == 1, 0, chip - 2))
    last_chip = jnp.where(even, jnp.where(chip == 0, 1, chip - 2), jnp.where(chip == chips - 1, chips - 2, chip + 2))
    over_chip = jnp.where((chip < 2) | (chip >= chips - 2), chip ^ 6, chip ^ 1)
    came_ahead = (chip % 4 == 1) | (chip % 4 == 2)
    slab, units = tokens.shape
    needed = devices // 2 + devices // 8 + 2

    def window(value, chip):
        blocks = value.reshape(slab, devices, units // devices)
        blocks = jnp.concatenate([blocks, blocks], axis=1)
        blocks = lax.dynamic_slice_in_dim(blocks, first_needed(devices, chip), needed, axis=1)
        return blocks.reshape(slab, -1)

    ahead, back = [tokens], [tokens]
    for _ in range(2):
        ahead.append(send(ahead[-1], onward))
        back.append(send(back[-1], backward))
    half = send(window(jnp.where(came_ahead, ahead[1], back[1]), over_chip), over)
    ahead.append(send(window(ahead[2], last_chip), onward))
    back.append(send(window(back[2], next_chip), backward))
    near = jnp.concatenate((tokens, ahead[1], back[1]), axis=0)
    middle = jnp.concatenate((ahead[2], back[2]), axis=0)
    last = jnp.concatenate((ahead[3], half), axis=0)
    near_beside = send(after(near, ahead[2], back[2]), sibling)
    needed = [window(after(value, ahead[2], back[2]), chip) for value in (ahead[2], back[2])]
    middle_beside = send(jnp.concatenate(needed, axis=0), sibling)
    last_beside = send(last, sibling)
    return [near, near_beside, middle, middle_beside, last, last_beside, back[3], send(back[3], sibling)]

def slab_origin(devices, device, number):
    chips = devices // 2
    number, flip = number % chips, number // chips
    hops = (number + 1) // 2 if number % 2 else -(number // 2)
    chip, core = device // 2, device % 2
    core = 1 - core if flip else core
    place = jnp.where(chip % 2 == 0, chip // 2, chips - 1 - chip // 2)
    place = (place + hops + chips) % chips
    chip = jnp.where(2 * place < chips, 2 * place, 2 * (chips - 1 - place) + 1)
    return 2 * chip + core


def ring_kernel(devices, slots, table_ref, *refs):
    groups = refs[:len(GROUPS)]
    out_ref, pair, tiles, zeros, out_sems, zero_sems = refs[len(GROUPS):]
    device = table_ref[table_ref.shape[0] - 1]
    slab, width = pair.shape[1] // devices, pair.shape[2]
    first = first_needed(devices, device // 2)

    def owned(partner):
        return table_ref[devices + tile_number(devices, device, partner)] == device

    def put(buffer, slot):
        return pltpu.make_async_copy(tiles.at[buffer], out_ref.at[slot], out_sems.at[buffer])

    def clear(slot):
        return pltpu.make_async_copy(zeros, out_ref.at[slot], zero_sems.at[slot])

    def load_block(partner, masked):
        parts = []
        for numbers, ref in zip(GROUPS, groups):
            place = partner
            if ref.shape[1] < devices * width:
                place = lax.rem(partner - first + devices, devices)
            group = ref[:, pl.ds(pl.multiple_of(place * width, 128), width)].astype(jnp.float32)
            for at, number in enumerate(numbers):
                part = group[at * slab:(at + 1) * slab]
                if masked:
                    row = lax.broadcasted_iota(jnp.int32, (slab, width), 0)
                    part = jnp.where(row < table_ref[slab_origin(devices, device, number)], part, 0.0)
                parts.append(part)
        pair[0 if masked else 1] = jnp.concatenate(parts, axis=0).astype(jnp.bfloat16)

    load_block(device, True)
    valid_count = table_ref[0]
    for at in range(1, devices):
        valid_count = valid_count + table_ref[at]
    scale = 1.0 / jnp.full((8, width), valid_count.astype(jnp.float32))

    def visit(partner, slot):
        mine = owned(partner)

        @pl.when(mine)
        def _():
            buffer = lax.rem(slot, BUFFERS)
            load_block(partner, False)

            @pl.when(slot >= BUFFERS)
            def _():
                put(buffer, slot - BUFFERS).wait()

            left = (partner <= device).astype(jnp.int32)
            for row in range(0, width, STRIP):
                rows = min(STRIP, width - row)
                strip = pl.ds(row, rows)
                product = lax.dot_general(
                    pair[left, :, row:row + rows], pair[1 - left], (((0,), (0,)), ((), ())),
                    preferred_element_type=jnp.float32,
                )
                tiles[buffer, strip, :] = product * scale[:1]
                pltpu.make_async_copy(
                    tiles.at[buffer, strip], out_ref.at[slot, strip], out_sems.at[buffer]
                ).start()

        return slot + mine.astype(jnp.int32)

    count = lax.fori_loop(0, devices, visit, jnp.int32(0))

    @pl.when(count < slots)
    def _():
        zeros[...] = jnp.zeros_like(zeros)

    def start_clear(slot, carry):
        clear(slot).start()
        return carry

    lax.fori_loop(count, slots, start_clear, 0)

    def drain(slot, carry):
        put(lax.rem(slot, BUFFERS), slot).wait()
        return carry

    lax.fori_loop(jnp.maximum(count - BUFFERS, 0), count, drain, 0)

    def end_clear(slot, carry):
        clear(slot).wait()
        return carry

    lax.fori_loop(count, slots, end_clear, 0)


def ring_form(tokens, slab_lengths, tile_owner, devices, device, slots):
    slab, units = tokens.shape
    width = units // devices
    groups = ring_gather(tokens, device, devices)
    table = jnp.concatenate([slab_lengths, tile_owner, device.reshape(1)])
    return pl.pallas_call(
        functools.partial(ring_kernel, devices, slots),
        out_shape=jax.ShapeDtypeStruct((slots, width, width), jnp.float32),
        in_specs=[pl.BlockSpec(memory_space=pltpu.SMEM)]
        + [pl.BlockSpec(memory_space=pltpu.VMEM)] * len(groups),
        out_specs=pl.BlockSpec(memory_space=pl.ANY),
        scratch_shapes=[
            pltpu.VMEM((2, slab * devices, width), jnp.bfloat16),
            pltpu.VMEM((BUFFERS, width, width), jnp.float32),
            pltpu.VMEM((width, width), jnp.float32),
            pltpu.SemaphoreType.DMA((BUFFERS,)),
            pltpu.SemaphoreType.DMA((slots,)),
        ],
        compiler_params=pltpu.CompilerParams(vmem_limit_bytes=32 * 1024 * 1024),
        cost_estimate=pl.CostEstimate(
            flops=2 * slots * slab * devices * width * width,
            bytes_accessed=4 * slots * width * width,
            transcendentals=0,
        ),
    )(table, *groups)


def per_device(tokens, slab_lengths, tile_owner):
    devices = lax.axis_size("col")
    device = lax.axis_index("col").astype(jnp.int32)
    slots = devices // 2 + devices // 8 + 1
    width = tokens.shape[1] // devices
    form = ring_form if devices == RING_DEVICES and width % 128 == 0 else gathered_form
    return form(tokens, slab_lengths, tile_owner, devices, device, slots)


def solution(mesh):
    return jax.shard_map(
        per_device,
        mesh=mesh,
        in_specs=(P(("grp", "col"), None), P("grp"), P()),
        out_specs=P(("grp", "col"), None, None),
        check_vma=False,
    )
```
